32 devices in a mesh: groups: 2 (over x), rows: 16 (over z, y, core).
Axes of the slice: x: 2, y: 2, z: 4, core: 2. Of those that a mesh axis runs over, the one named last changes fastest.
Arguments:
- train_feats: bfloat16 [65536, 2048], P(('groups', 'rows')), parts along dimension 0, may hold values from -6 to 6
- queries: bfloat16 [2, 512, 2048], P(None, ('groups', 'rows')), parts along dimension 1, may hold values from -6 to 6
- inverse_fisher: bfloat16 [1, 2048, 2048], P(None, None, 'rows'), may hold values from -0.125 to 0.125
Outputs:
- scores: float32 [65536, 512], P(('groups', 'rows')), parts along dimension 0
The draws below stay inside these ranges and needn't reach their ends.
There are 2 independent parts, one for each index of `groups`. The reference program is written for one: setup_inputs(seed, part) draws one part's arguments, and reference() takes and returns one part's arrays. A program takes and returns all parts, laid end to end along the dimension named above; an argument that names none is the same for every part. Nothing has to cross between parts.
All inputs are finite; a program needn't handle non-finite values.
Results may differ from the reference program's by a relative error of at most 0.0029.
Values may be sent and summed in bfloat16 or wider, within the bound.
No kernel may reach another device: no remote copies, remote signals or barrier semaphores. Data moves between devices by JAX's collectives and lax.ppermute only.
A program may use at most 64 MiB of HBM per device.

```python
import jax
import jax.numpy as jnp
from jax import lax

GW = 2048
LG = 1
QB = 256
F = 2048
NTRAIN = 32768


def block_scale(stream_key, dims, pieces, low, top_value):
    gain = 1.0
    for position, parts in pieces:
        steps = jax.random.uniform(jax.random.fold_in(jax.random.fold_in(stream_key, 6), position), (parts,), jnp.float32, low / len(pieces), top_value / len(pieces))
        gain = gain * jnp.repeat(jnp.exp(steps), dims[position] // parts).reshape((-1,) + (1,) * (len(dims) - 1 - position))
    return gain


def normal_values(key, dims, spread, most, split=(), dtype=jnp.bfloat16):
    factor_of = block_scale(key, dims, split, -0.22, 0.18) if split else 1.0
    entries = jax.random.normal(key, dims, jnp.float32) * spread * factor_of
    return jnp.minimum(jnp.maximum(entries, -most), most).astype(dtype)


def setup_inputs(seed: int = 0, part: int = 0) -> dict:
    key_list = jax.random.split(jax.random.key(seed), 4)
    part_keys = jax.random.split(jax.random.fold_in(key_list[3], part), 4)
    train_feats = normal_values(part_keys[0], (NTRAIN, F), 1.0, 6.0, ((0, 16),))
    queries = normal_values(part_keys[1], (2, QB, F), 1.0, 6.0, ((1, 16),))
    inverse_fisher = normal_values(key_list[2], (LG, GW, GW), GW ** -0.5, 0.125, ((2, 16),))
    return {"train_feats": train_feats, "queries": queries, "inverse_fisher": inverse_fisher}


def reference(train_feats, queries, inverse_fisher):
    flattened = queries.reshape(2 * QB, LG, GW).astype(jnp.float32)
    conditioned = jnp.einsum("qgk,gkc->qgc", flattened, inverse_fisher.astype(jnp.float32))
    conditioned = conditioned.astype(jnp.bfloat16).reshape(2 * QB, LG * GW)
    score_scale = 1.0 / (LG * GW) ** 0.5
    products = lax.dot_general(train_feats, conditioned, (((1,), (1,)), ((), ())), preferred_element_type=jnp.float32)
    return products * score_scale
```

```python
import functools

import jax
import jax.numpy as jnp
from jax import lax
from jax.experimental import pallas as pl
from jax.experimental.pallas import tpu as pltpu
from jax.sharding import PartitionSpec as P

VMEM = pl.BlockSpec(memory_space=pltpu.VMEM)


class Grid:
    def __init__(self, row_count):
        chips = row_count // 2
        self.near = 1
        while self.near * self.near * 4 <= chips:
            self.near *= 2
        self.far = chips // self.near
        self.chips = chips

    def rank(self, far, near, core):
        return ((far % self.far) * self.near + near % self.near) * 2 + core

    def fetch(self, block, far, near, core):
        pairs = [
            (self.rank(f + far, n + near, c ^ core), self.rank(f, n, c))
            for f in range(self.far)
            for n in range(self.near)
            for c in range(2)
        ]
        return lax.ppermute(block, "rows", pairs)

    def slots(self):
        return [(far, near) for near in range(self.near) for far in range(self.far)]

    def gather(self, block):
        found = {(0, 0): block}
        for near in range(1, self.near):
            found[0, near] = self.fetch(block, 0, near, 0)
        for far in range(1, self.far):
            found[far, 0] = self.fetch(block, far, 0, 0)
        for far in range(1, self.far):
            for near in range(1, self.near):
                found[far, near] = self.fetch(found[far, 0], 0, near, 0)
        return [found[slot] for slot in self.slots()]

    def place(self):
        row = lax.axis_index("rows")
        core, chip = lax.rem(row, 2), lax.div(row, 2)
        far, near = lax.div(chip, self.near), lax.rem(chip, self.near)
        chips = [
            lax.rem(far + f, self.far) * self.near + lax.rem(near + n, self.near) for f, n in self.slots()
        ]
        return core, chips


def condition_kernel(grid, *refs):
    query_refs = refs[: grid.chips]
    own_ref, peer_ref, out_ref, sorted_ref, columns_ref = refs[grid.chips :]
    core, chips = grid.place()
    width = own_ref.shape[-1]
    columns_ref[:, pl.ds(pl.multiple_of(core * width, width), width)] = own_ref[0]
    columns_ref[:, pl.ds(pl.multiple_of((1 - core) * width, width), width)] = peer_ref[0]
    for chip, query_ref in zip(chips, query_refs):
        sorted_ref[:, pl.ds(chip, 1)] = query_ref[...][:, None]
    rows = sorted_ref[...].reshape(-1, sorted_ref.shape[-1])
    out_ref[...] = jnp.dot(rows, columns_ref[...], preferred_element_type=jnp.float32).astype(out_ref.dtype)


def condition(grid, queries, own, peer):
    blocks, count, features = queries[0].shape
    width = own.shape[-1]
    return pl.pallas_call(
        functools.partial(condition_kernel, grid),
        out_shape=jax.ShapeDtypeStruct((blocks * grid.chips * count, 2 * width), jnp.bfloat16),
        in_specs=[VMEM] * (grid.chips + 2),
        out_specs=VMEM,
        scratch_shapes=[
            pltpu.VMEM((blocks, grid.chips, count, features), jnp.bfloat16),
            pltpu.VMEM((features, 2 * width), jnp.bfloat16),
        ],
        compiler_params=pltpu.CompilerParams(vmem_limit_bytes=12 << 20),
        cost_estimate=pl.CostEstimate(flops=1 << 28, bytes_accessed=3 << 20, transcendentals=0),
        name="condition",
    )(*queries, own, peer)


def score_kernel(grid, tile, shape, *refs):
    blocks, count, width = shape
    train_ref, own_refs, peer_refs = refs[0], refs[1 : 1 + grid.chips], refs[1 + grid.chips : 1 + 2 * grid.chips]
    out_ref, sorted_ref, tile_ref, sem = refs[1 + 2 * grid.chips :]
    core, chips = grid.place()
    features = train_ref.shape[1]
    for which, parts in ((core, own_refs), (1 - core, peer_refs)):
        for chip, part_ref in zip(chips, parts):
            columns = pl.ds(pl.multiple_of(chip * width, width), width)
            sorted_ref[:, :, pl.ds(which, 1), :, columns] = part_ref[...].reshape(
                blocks, grid.chips, 1, count, width
            )
    scale = 1.0 / features**0.5
    steps = train_ref.shape[0] // tile

    def copy(step, slot):
        return pltpu.make_async_copy(
            tile_ref.at[slot], out_ref.at[pl.ds(pl.multiple_of(step * tile, tile), tile)], sem.at[slot]
        )

    @pl.loop(0, steps)
    def _(step):
        slot = lax.rem(step, 2)

        @pl.when(step >= 2)
        def _():
            copy(step - 2, slot).wait()

        products = lax.dot_general(
            train_ref[pl.ds(pl.multiple_of(step * tile, tile), tile)],
            sorted_ref[...].reshape(-1, features),
            (((1,), (1,)), ((), ())),
            preferred_element_type=jnp.float32,
        )
        tile_ref[slot] = products * scale
        copy(step, slot).start()

    for step in range(max(steps - 2, 0), steps):
        copy(step, step % 2).wait()


def score(grid, train_feats, own, peer, blocks):
    rows, features = train_feats.shape
    queries, width = own[0].shape
    count = queries // (blocks * grid.chips)
    tile = 256
    return pl.pallas_call(
        functools.partial(score_kernel, grid, tile, (blocks, count, width)),
        out_shape=jax.ShapeDtypeStruct((rows, 2 * queries), jnp.float32),
        in_specs=[VMEM] * (1 + 2 * grid.chips),
        out_specs=pl.BlockSpec(memory_space=pl.ANY),
        scratch_shapes=[
            pltpu.VMEM((blocks, grid.chips, 2, count, features), jnp.bfloat16),
            pltpu.VMEM((2, tile, 2 * queries), jnp.float32),
            pltpu.SemaphoreType.DMA((2,)),
        ],
        compiler_params=pltpu.CompilerParams(vmem_limit_bytes=24 << 20),
        cost_estimate=pl.CostEstimate(
            flops=4 * rows * features * queries, bytes_accessed=16 << 20, transcendentals=0
        ),
        name="score",
    )(pltpu.with_memory_space_constraint(train_feats, pltpu.VMEM), *own, *peer)


def two_level(grid, train_feats, queries, inverse_fisher):
    peer_fisher = grid.fetch(inverse_fisher, 0, 0, 1)
    gathered = grid.gather(queries)
    block = condition(grid, gathered, inverse_fisher, peer_fisher)
    own = grid.gather(block)
    peer = [grid.fetch(part, 0, 0, 1) for part in own]
    return score(grid, train_feats, own, peer, queries.shape[0])


def one_level(train_feats, queries, inverse_fisher):
    group_count, group_width, _ = inverse_fisher.shape
    gathered = lax.all_gather(queries, "rows", axis=1, tiled=True)
    flattened = gathered.reshape(-1, group_count, group_width)
    part = jnp.einsum("qgk,gkc->qgc", flattened, inverse_fisher, preferred_element_type=jnp.float32)
    complete = lax.all_gather(part.astype(jnp.bfloat16), "rows", axis=2, tiled=True)
    conditioned = complete.reshape(flattened.shape[0], -1)
    products = lax.dot_general(
        train_feats, conditioned, (((1,), (1,)), ((), ())), preferred_element_type=jnp.float32
    )
    return products * (1.0 / train_feats.shape[1] ** 0.5)


def per_device(row_count, train_feats, queries, inverse_fisher):
    group_count, _, width = inverse_fisher.shape
    whole_tiles = group_count == 1 and width % 128 == 0 and queries.shape[1] % 16 == 0
    if row_count % 2 == 0 and whole_tiles and train_feats.shape[0] % 512 == 0:
        return two_level(Grid(row_count), train_feats, queries, inverse_fisher)
    return one_level(train_feats, queries, inverse_fisher)


def solution(mesh):
    placed = (P(("groups", "rows"), None), P(None, ("groups", "rows"), None), P(None, None, "rows"))
    return jax.shard_map(
        functools.partial(per_device, mesh.shape["rows"]),
        mesh=mesh,
        in_specs=placed,
        out_specs=P(("groups", "rows"), None),
        check_vma=False,
    )
```

```python
import functools

import jax
import jax.numpy as jnp
from jax import lax
from jax.experimental import pallas as pl
from jax.experimental.pallas import tpu as pltpu
from jax.sharding import PartitionSpec as P

VMEM = pl.BlockSpec(memory_space=pltpu.VMEM)
ANY = pl.BlockSpec(memory_space=pl.ANY)


class Grid:
    def __init__(self, row_count):
        chips = row_count // 2
        self.near = 2
        self.far = chips // 2
        self.fars = [0] + sorted(range(1, self.far), key=lambda m: (m & 1, m))

    def swap(self, block, far, near, core):
        step = (far * self.near + near) * 2 + core
        pairs = [(row ^ step, row) for row in range(self.far * self.near * 2)]
        return lax.ppermute(block, "rows", pairs)

    def place(self):
        row = lax.axis_index("rows")
        chip = lax.div(row, 2)
        return lax.div(chip, self.near), lax.rem(chip, self.near), lax.rem(row, 2)


def flip(part, mask):
    return lax.bitwise_xor(part, jnp.int32(mask))


def columns(index, width):
    return pl.ds(pl.multiple_of(index * width, width), width)


def stage_kernel(count, *refs):
    sources, targets, sems = refs[:count], refs[count : 2 * count], refs[2 * count]
    copies = [
        pltpu.make_async_copy(source, target, sems.at[i]) for i, (source, target) in enumerate(zip(sources, targets))
    ]
    for copy in copies:
        copy.start()
    for copy in copies:
        copy.wait()


def stage(*arrays):
    size = sum(a.size * a.dtype.itemsize for a in arrays)
    return pl.pallas_call(
        functools.partial(stage_kernel, len(arrays)),
        out_shape=[pltpu.VMEM(a.shape, a.dtype) for a in arrays],
        in_specs=[ANY] * len(arrays),
        out_specs=[VMEM] * len(arrays),
        scratch_shapes=[pltpu.SemaphoreType.DMA((len(arrays),))],
        compiler_params=pltpu.CompilerParams(vmem_limit_bytes=4 << 20),
        cost_estimate=pl.CostEstimate(flops=0, bytes_accessed=2 * size, transcendentals=0),
        name="stage",
    )(*(pltpu.with_memory_space_constraint(a, pltpu.HBM) for a in arrays))


def condition_kernel(grid, *refs):
    query_refs = refs[: grid.far]
    fisher_refs = refs[grid.far : grid.far + 4]
    out_ref, sorted_ref, columns_ref = refs[grid.far + 4 :]
    far, near, core = grid.place()
    width = fisher_refs[0].shape[-1]
    for index, fisher_ref in enumerate(fisher_refs):
        place = flip(near, index // 2) * 2 + flip(core, index % 2)
        columns_ref[:, columns(place, width)] = fisher_ref[0]
    for mask, query_ref in zip(grid.fars, query_refs):
        sorted_ref[:, pl.ds(flip(far, mask), 1)] = query_ref[...][:, None]
    rows = sorted_ref[...].reshape(-1, sorted_ref.shape[-1])
    out_ref[...] = jnp.dot(rows, columns_ref[...], preferred_element_type=jnp.float32).astype(out_ref.dtype)


def condition(grid, queries, fishers):
    blocks, count, features = queries[0].shape
    width = fishers[0].shape[-1]
    return pl.pallas_call(
        functools.partial(condition_kernel, grid),
        out_shape=jax.ShapeDtypeStruct((blocks * grid.far * count, 4 * width), jnp.bfloat16),
        in_specs=[VMEM] * (grid.far + 4),
        out_specs=VMEM,
        scratch_shapes=[
            pltpu.VMEM((blocks, grid.far, count, features), jnp.bfloat16),
            pltpu.VMEM((features, 4 * width), jnp.bfloat16),
        ],
        compiler_params=pltpu.CompilerParams(vmem_limit_bytes=12 << 20),
        cost_estimate=pl.CostEstimate(flops=1 << 28, bytes_accessed=3 << 20, transcendentals=0),
        name="condition",
    )(*queries, *fishers)


def score_kernel(grid, tile, shape, masks, *refs):
    blocks, count, width = shape
    train_ref, part_refs = refs[0], refs[1 : 1 + len(masks)]
    out_ref, sorted_ref, tile_ref, sem = refs[1 + len(masks) :]
    far, near, core = grid.place()
    features = train_ref.shape[1]
    for (far_mask, near_mask, core_mask), part_ref in zip(masks, part_refs):
        group = flip(near, near_mask) * 2 + flip(core, core_mask)
        sorted_ref[:, :, pl.ds(group, 1), :, columns(flip(far, far_mask), width)] = part_ref[...].reshape(
            blocks, grid.far, 1, count, width
        )
    scale = 1.0 / features**0.5
    steps = train_ref.shape[0] // tile

    def copy(step, slot):
        return pltpu.make_async_copy(
            tile_ref.at[slot], out_ref.at[pl.ds(pl.multiple_of(step * tile, tile), tile)], sem.at[slot]
        )

    @pl.loop(0, steps)
    def _(step):
        slot = lax.rem(step, 2)

        @pl.when(step >= 2)
        def _():
            copy(step - 2, slot).wait()

        products = lax.dot_general(
            train_ref[pl.ds(pl.multiple_of(step * tile, tile), tile)],
            sorted_ref[...].reshape(-1, features),
            (((1,), (1,)), ((), ())),
            preferred_element_type=jnp.float32,
        )
        tile_ref[slot] = products * scale
        copy(step, slot).start()

    for step in range(max(steps - 2, 0), steps):
        copy(step, step % 2).wait()


def score(grid, train_feats, parts, blocks):
    rows, features = train_feats.shape
    queries, width = parts[0, 0, 0].shape
    count = queries // (blocks * grid.far)
    tile = 256
    return pl.pallas_call(
        functools.partial(score_kernel, grid, tile, (blocks, count, width), list(parts)),
        out_shape=jax.ShapeDtypeStruct((rows, 4 * queries), jnp.float32),
        in_specs=[VMEM] * (1 + len(parts)),
        out_specs=ANY,
        scratch_shapes=[
            pltpu.VMEM((blocks, grid.far, 4, count, features), jnp.bfloat16),
            pltpu.VMEM((2, tile, 4 * queries), jnp.float32),
            pltpu.SemaphoreType.DMA((2,)),
        ],
        compiler_params=pltpu.CompilerParams(vmem_limit_bytes=24 << 20),
        cost_estimate=pl.CostEstimate(
            flops=8 * rows * features * queries, bytes_accessed=16 << 20, transcendentals=0
        ),
        name="score",
    )(pltpu.with_memory_space_constraint(train_feats, pltpu.VMEM), *parts.values())


def two_level(grid, train_feats, queries, inverse_fisher):
    near_fisher = grid.swap(inverse_fisher, 0, 1, 0)
    core_fisher = grid.swap(inverse_fisher, 0, 0, 1)
    gathered = [grid.swap(queries, mask, 0, 0) for mask in grid.fars[1:]]
    staged = stage(train_feats, queries, inverse_fisher)
    near_fisher, gathered, staged = lax.optimization_barrier((near_fisher, gathered, staged))
    train_here, queries_here, fisher_here = staged
    both_fisher = grid.swap(near_fisher, 0, 0, 1)
    block = condition(grid, [queries_here, *gathered], [fisher_here, core_fisher, near_fisher, both_fisher])
    parts = {(0, 0, 0): block}
    for mask in grid.fars[1:]:
        parts[mask, 0, 0] = grid.swap(block, mask, 0, 0)
    for mask in grid.fars:
        parts[mask, 1, 0] = grid.swap(parts[mask, 0, 0], 0, 1, 0)
    for near in range(2):
        for mask in grid.fars:
            parts[mask, near, 1] = grid.swap(parts[mask, near, 0], 0, 0, 1)
    return score(grid, train_here, parts, queries.shape[0])


def one_level(train_feats, queries, inverse_fisher):
    group_count, group_width, _ = inverse_fisher.shape
    gathered = lax.all_gather(queries, "rows", axis=1, tiled=True)
    flattened = gathered.reshape(-1, group_count, group_width)
    part = jnp.einsum("qgk,gkc->qgc", flattened, inverse_fisher, preferred_element_type=jnp.float32)
    complete = lax.all_gather(part.astype(jnp.bfloat16), "rows", axis=2, tiled=True)
    conditioned = complete.reshape(flattened.shape[0], -1)
    products = lax.dot_general(
        train_feats, conditioned, (((1,), (1,)), ((), ())), preferred_element_type=jnp.float32
    )
    return products * (1.0 / train_feats.shape[1] ** 0.5)


def per_device(row_count, train_feats, queries, inverse_fisher):
    group_count, _, width = inverse_fisher.shape
    whole_tiles = group_count == 1 and width % 128 == 0 and queries.shape[1] % 16 == 0
    if row_count >= 8 and row_count & (row_count - 1) == 0 and whole_tiles and train_feats.shape[0] % 512 == 0:
        return two_level(Grid(row_count), train_feats, queries, inverse_fisher)
    return one_level(train_feats, queries, inverse_fisher)


def solution(mesh):
    placed = (P(("groups", "rows"), None), P(None, ("groups", "rows"), None), P(None, None, "rows"))
    return jax.shard_map(
        functools.partial(per_device, mesh.shape["rows"]),
        mesh=mesh,
        in_specs=placed,
        out_specs=P(("groups", "rows"), None),
        check_vma=False,
    )
```

```python
import functools

import jax
import jax.numpy as jnp
from jax import lax
from jax.experimental import pallas as pl
from jax.experimental.pallas import tpu as pltpu
from jax.sharding import PartitionSpec as P

VMEM = pl.BlockSpec(memory_space=pltpu.VMEM)
ANY = pl.BlockSpec(memory_space=pl.ANY)


class Grid:
    def __init__(self, row_count):
        chips = row_count // 2
        self.near = 2
        self.far = chips // 2
        self.fars = range(self.far)

    def swap(self, block, far, near, core):
        step = (far * self.near + near) * 2 + core
        pairs = [(row ^ step, row) for row in range(self.far * self.near * 2)]
        return lax.ppermute(block, "rows", pairs)

    def place(self):
        row = lax.axis_index("rows")
        chip = lax.div(row, 2)
        return lax.div(chip, self.near), lax.rem(chip, self.near), lax.rem(row, 2)


def flip(part, mask):
    return lax.bitwise_xor(part, jnp.int32(mask))


def columns(index, width):
    return pl.ds(pl.multiple_of(index * width, width), width)


def stage_kernel(count, *refs):
    sources, targets, sems = refs[:count], refs[count : 2 * count], refs[2 * count]
    copies = [
        pltpu.make_async_copy(source, target, sems.at[i]) for i, (source, target) in enumerate(zip(sources, targets))
    ]
    for copy in copies:
        copy.start()
    for copy in copies:
        copy.wait()


def stage(*arrays):
    size = sum(a.size * a.dtype.itemsize for a in arrays)
    return pl.pallas_call(
        functools.partial(stage_kernel, len(arrays)),
        out_shape=[pltpu.VMEM(a.shape, a.dtype) for a in arrays],
        in_specs=[ANY] * len(arrays),
        out_specs=[VMEM] * len(arrays),
        scratch_shapes=[pltpu.SemaphoreType.DMA((len(arrays),))],
        compiler_params=pltpu.CompilerParams(vmem_limit_bytes=4 << 20),
        cost_estimate=pl.CostEstimate(flops=0, bytes_accessed=2 * size, transcendentals=0),
        name="stage",
    )(*(pltpu.with_memory_space_constraint(a, pltpu.HBM) for a in arrays))


def condition_kernel(grid, *refs):
    query_refs = refs[: grid.far]
    fisher_refs = refs[grid.far : grid.far + 4]
    out_ref, sorted_ref, columns_ref = refs[grid.far + 4 :]
    far, near, core = grid.place()
    width = fisher_refs[0].shape[-1]
    for index, fisher_ref in enumerate(fisher_refs):
        place = flip(near, index // 2) * 2 + flip(core, index % 2)
        columns_ref[:, columns(place, width)] = fisher_ref[0]
    for mask, query_ref in zip(grid.fars, query_refs):
        sorted_ref[:, pl.ds(flip(far, mask), 1)] = query_ref[...][:, None]
    rows = sorted_ref[...].reshape(-1, sorted_ref.shape[-1])
    out_ref[...] = jnp.dot(rows, columns_ref[...], preferred_element_type=jnp.float32).astype(out_ref.dtype)


def condition(grid, queries, fishers):
    blocks, count, features = queries[0].shape
    width = fishers[0].shape[-1]
    return pl.pallas_call(
        functools.partial(condition_kernel, grid),
        out_shape=jax.ShapeDtypeStruct((blocks * grid.far * count, 4 * width), jnp.bfloat16),
        in_specs=[VMEM] * (grid.far + 4),
        out_specs=VMEM,
        scratch_shapes=[
            pltpu.VMEM((blocks, grid.far, count, features), jnp.bfloat16),
            pltpu.VMEM((features, 4 * width), jnp.bfloat16),
        ],
        compiler_params=pltpu.CompilerParams(vmem_limit_bytes=12 << 20),
        cost_estimate=pl.CostEstimate(flops=1 << 28, bytes_accessed=3 << 20, transcendentals=0),
        name="condition",
    )(*queries, *fishers)


def score_kernel(grid, tile, shape, masks, *refs):
    blocks, count, width = shape
    train_ref, part_refs = refs[0], refs[1 : 1 + len(masks)]
    out_ref, sorted_ref, tile_ref, sem = refs[1 + len(masks) :]
    far, near, core = grid.place()
    features = train_ref.shape[1]
    for (far_mask, near_mask, core_mask), part_ref in zip(masks, part_refs):
        group = flip(near, near_mask) * 2 + flip(core, core_mask)
        sorted_ref[:, :, pl.ds(group, 1), :, columns(flip(far, far_mask), width)] = part_ref[...].reshape(
            blocks, grid.far, 1, count, width
        )
    scale = 1.0 / features**0.5
    steps = train_ref.shape[0] // tile

    def copy(step, slot):
        return pltpu.make_async_copy(
            tile_ref.at[slot], out_ref.at[pl.ds(pl.multiple_of(step * tile, tile), tile)], sem.at[slot]
        )

    @pl.loop(0, steps)
    def _(step):
        slot = lax.rem(step, 2)

        @pl.when(step >= 2)
        def _():
            copy(step - 2, slot).wait()

        products = lax.dot_general(
            train_ref[pl.ds(pl.multiple_of(step * tile, tile), tile)],
            sorted_ref[...].reshape(-1, features),
            (((1,), (1,)), ((), ())),
            preferred_element_type=jnp.float32,
        )
        tile_ref[slot] = products * scale
        copy(step, slot).start()

    for step in range(max(steps - 2, 0), steps):
        copy(step, step % 2).wait()


def score(grid, train_feats, parts, blocks):
    rows, features = train_feats.shape
    queries, width = parts[0, 0, 0].shape
    count = queries // (blocks * grid.far)
    tile = 256
    return pl.pallas_call(
        functools.partial(score_kernel, grid, tile, (blocks, count, width), list(parts)),
        out_shape=jax.ShapeDtypeStruct((rows, 4 * queries), jnp.float32),
        in_specs=[VMEM] * (1 + len(parts)),
        out_specs=ANY,
        scratch_shapes=[
            pltpu.VMEM((blocks, grid.far, 4, count, features), jnp.bfloat16),
            pltpu.VMEM((2, tile, 4 * queries), jnp.float32),
            pltpu.SemaphoreType.DMA((2,)),
        ],
        compiler_params=pltpu.CompilerParams(vmem_limit_bytes=24 << 20),
        cost_estimate=pl.CostEstimate(
            flops=8 * rows * features * queries, bytes_accessed=16 << 20, transcendentals=0
        ),
        name="score",
    )(pltpu.with_memory_space_constraint(train_feats, pltpu.VMEM), *parts.values())


def two_level(grid, train_feats, queries, inverse_fisher):
    mirror, beside = grid.far - 1, 1
    core_fisher = grid.swap(inverse_fisher, 0, 0, 1)
    gathered = {0: queries}
    gathered[beside] = grid.swap(queries, beside, 0, 0)
    gathered[mirror] = grid.swap(queries, mirror, 0, 0)
    near_fisher = grid.swap(inverse_fisher, 0, 1, 0)
    staged = stage(train_feats, queries, inverse_fisher)
    gathered, staged = lax.optimization_barrier((gathered, staged))
    train_here, gathered[0], fisher_here = staged
    gathered[mirror ^ beside] = grid.swap(gathered[mirror], beside, 0, 0)
    near_fisher, gathered = lax.optimization_barrier((near_fisher, gathered))
    both_fisher = grid.swap(near_fisher, 0, 0, 1)
    block = condition(
        grid, [gathered[mask] for mask in grid.fars], [fisher_here, core_fisher, near_fisher, both_fisher]
    )

    parts = {(0, 0, 0): block}
    parts[0, 0, 1] = grid.swap(block, 0, 0, 1)
    parts[0, 1, 0] = grid.swap(block, 0, 1, 0)
    parts[beside, 0, 0] = grid.swap(block, beside, 0, 0)
    parts[mirror, 0, 0] = grid.swap(block, mirror, 0, 0)
    parts[mirror ^ beside, 0, 0] = grid.swap(parts[mirror, 0, 0], beside, 0, 0)
    for mask in grid.fars[1:]:
        parts[mask, 0, 1] = grid.swap(parts[mask, 0, 0], 0, 0, 1)
    for mask in (mirror ^ beside, mirror, beside):
        parts[mask, 1, 0] = grid.swap(parts[mask, 0, 0], 0, 1, 0)
    for mask in grid.fars:
        parts[mask, 1, 1] = grid.swap(parts[mask, 1, 0], 0, 0, 1)
    return score(grid, train_here, parts, queries.shape[0])


def one_level(train_feats, queries, inverse_fisher):
    group_count, group_width, _ = inverse_fisher.shape
    gathered = lax.all_gather(queries, "rows", axis=1, tiled=True)
    flattened = gathered.reshape(-1, group_count, group_width)
    part = jnp.einsum("qgk,gkc->qgc", flattened, inverse_fisher, preferred_element_type=jnp.float32)
    complete = lax.all_gather(part.astype(jnp.bfloat16), "rows", axis=2, tiled=True)
    conditioned = complete.reshape(flattened.shape[0], -1)
    products = lax.dot_general(
        train_feats, conditioned, (((1,), (1,)), ((), ())), preferred_element_type=jnp.float32
    )
    return products * (1.0 / train_feats.shape[1] ** 0.5)


def per_device(row_count, train_feats, queries, inverse_fisher):
    group_count, _, width = inverse_fisher.shape
    whole_tiles = group_count == 1 and width % 128 == 0 and queries.shape[1] % 16 == 0
    if row_count == 16 and whole_tiles and train_feats.shape[0] % 512 == 0:
        return two_level(Grid(row_count), train_feats, queries, inverse_fisher)
    return one_level(train_feats, queries, inverse_fisher)


def solution(mesh):
    placed = (P(("groups", "rows"), None), P(None, ("groups", "rows"), None), P(None, None, "rows"))
    return jax.shard_map(
        functools.partial(per_device, mesh.shape["rows"]),
        mesh=mesh,
        in_specs=placed,
        out_specs=P(("groups", "rows"), None),
        check_vma=False,
    )
```

```python
import functools

import jax
import jax.numpy as jnp
from jax import lax
from jax.experimental import pallas as pl
from jax.experimental.pallas import tpu as pltpu
from jax.sharding import PartitionSpec as P

VMEM = pl.BlockSpec(memory_space=pltpu.VMEM)
ANY = pl.BlockSpec(memory_space=pl.ANY)


class Grid:
    def __init__(self, row_count):
        chips = row_count // 2
        self.near = 2
        self.far = chips // 2
        self.fars = range(self.far)

    def swap(self, block, far, near, core):
        step = (far * self.near + near) * 2 + core
        pairs = [(row ^ step, row) for row in range(self.far * self.near * 2)]
        return lax.ppermute(block, "rows", pairs)

    def place(self):
        row = lax.axis_index("rows")
        chip = lax.div(row, 2)
        return lax.div(chip, self.near), lax.rem(chip, self.near), lax.rem(row, 2)


def flip(part, mask):
    return lax.bitwise_xor(part, jnp.int32(mask))


def columns(index, width):
    return pl.ds(pl.multiple_of(index * width, width), width)


def stage_kernel(count, *refs):
    sources, targets, sems = refs[:count], refs[count : 2 * count], refs[2 * count]
    copies = [
        pltpu.make_async_copy(source, target, sems.at[i]) for i, (source, target) in enumerate(zip(sources, targets))
    ]
    for copy in copies:
        copy.start()
    for copy in copies:
        copy.wait()


def stage(*arrays):
    size = sum(a.size * a.dtype.itemsize for a in arrays)
    return pl.pallas_call(
        functools.partial(stage_kernel, len(arrays)),
        out_shape=[pltpu.VMEM(a.shape, a.dtype) for a in arrays],
        in_specs=[ANY] * len(arrays),
        out_specs=[VMEM] * len(arrays),
        scratch_shapes=[pltpu.SemaphoreType.DMA((len(arrays),))],
        compiler_params=pltpu.CompilerParams(vmem_limit_bytes=4 << 20),
        cost_estimate=pl.CostEstimate(flops=0, bytes_accessed=2 * size, transcendentals=0),
        name="stage",
    )(*(pltpu.with_memory_space_constraint(a, pltpu.HBM) for a in arrays))


def condition_kernel(grid, *refs):
    query_refs = refs[: grid.far]
    fisher_refs = refs[grid.far : grid.far + 4]
    out_ref, sorted_ref, columns_ref = refs[grid.far + 4 :]
    far, near, core = grid.place()
    width = fisher_refs[0].shape[-1]
    for index, fisher_ref in enumerate(fisher_refs):
        place = flip(near, index // 2) * 2 + flip(core, index % 2)
        columns_ref[:, columns(place, width)] = fisher_ref[0]
    for mask, query_ref in zip(grid.fars, query_refs):
        sorted_ref[:, pl.ds(flip(far, mask), 1)] = query_ref[...][:, None]
    rows = sorted_ref[...].reshape(-1, sorted_ref.shape[-1])
    out_ref[...] = jnp.dot(rows, columns_ref[...], preferred_element_type=jnp.float32).astype(out_ref.dtype)


def condition(grid, queries, fishers):
    blocks, count, features = queries[0].shape
    width = fishers[0].shape[-1]
    return pl.pallas_call(
        functools.partial(condition_kernel, grid),
        out_shape=jax.ShapeDtypeStruct((blocks * grid.far * count, 4 * width), jnp.bfloat16),
        in_specs=[VMEM] * (grid.far + 4),
        out_specs=VMEM,
        scratch_shapes=[
            pltpu.VMEM((blocks, grid.far, count, features), jnp.bfloat16),
            pltpu.VMEM((features, 4 * width), jnp.bfloat16),
        ],
        compiler_params=pltpu.CompilerParams(vmem_limit_bytes=12 << 20),
        cost_estimate=pl.CostEstimate(flops=1 << 28, bytes_accessed=3 << 20, transcendentals=0),
        name="condition",
    )(*queries, *fishers)


def score_kernel(grid, tile, shape, mask, first, last, *refs):
    blocks, count, width = shape
    train_ref, part_refs, refs = refs[0], refs[1:5], refs[5:]
    total_ref, refs = (None, refs) if first else (refs[0], refs[1:])
    out_ref, sorted_ref, refs = refs[0], refs[1], refs[2:]
    far, near, core = grid.place()
    features = train_ref.shape[1]
    for index, part_ref in enumerate(part_refs):
        group = flip(near, index // 2) * 2 + flip(core, index % 2)
        sorted_ref[:, :, pl.ds(group, 1)] = part_ref[...].reshape(blocks, grid.far, 1, count, width)
    scale = 1.0 / features**0.5
    steps = train_ref.shape[0] // tile

    def rows(step):
        return pl.ds(pl.multiple_of(step * tile, tile), tile)

    def products(step):
        value = lax.dot_general(
            train_ref[rows(step), columns(flip(far, mask), width)],
            sorted_ref[...].reshape(-1, width),
            (((1,), (1,)), ((), ())),
            preferred_element_type=jnp.float32,
        )
        return value if first else total_ref[rows(step)] + value

    if not last:

        @pl.loop(0, steps)
        def _(step):
            out_ref[rows(step)] = products(step)

        return

    tile_ref, sem = refs

    def copy(step, slot):
        return pltpu.make_async_copy(tile_ref.at[slot], out_ref.at[rows(step)], sem.at[slot])

    @pl.loop(0, steps)
    def _(step):
        slot = lax.rem(step, 2)

        @pl.when(step >= 2)
        def _():
            copy(step - 2, slot).wait()

        tile_ref[slot] = products(step) * scale
        copy(step, slot).start()

    for step in range(max(steps - 2, 0), steps):
        copy(step, step % 2).wait()


def score(grid, train_feats, parts, total, mask, blocks, last):
    rows, features = train_feats.shape
    queries, width = parts[0].shape
    count = queries // (blocks * grid.far)
    tile = 256
    first = total is None
    totals = [] if first else [total]
    shape = (rows, 4 * queries)
    scratch = [pltpu.VMEM((blocks, grid.far, 4, count, width), jnp.bfloat16)]
    if last:
        scratch += [pltpu.VMEM((2, tile, 4 * queries), jnp.float32), pltpu.SemaphoreType.DMA((2,))]
    return pl.pallas_call(
        functools.partial(score_kernel, grid, tile, (blocks, count, width), mask, first, last),
        out_shape=jax.ShapeDtypeStruct(shape, jnp.float32) if last else pltpu.VMEM(shape, jnp.float32),
        in_specs=[VMEM] * (5 + len(totals)),
        out_specs=ANY if last else VMEM,
        scratch_shapes=scratch,
        input_output_aliases={} if first or last else {5: 0},
        compiler_params=pltpu.CompilerParams(vmem_limit_bytes=12 << 20),
        cost_estimate=pl.CostEstimate(
            flops=8 * rows * width * queries, bytes_accessed=4 << 20, transcendentals=0
        ),
        name="score",
    )(*(pltpu.with_memory_space_constraint(a, pltpu.VMEM) for a in (train_feats, *parts, *totals)))


def two_level(grid, train_feats, queries, inverse_fisher):
    mirror, beside = grid.far - 1, 1
    relayed = mirror ^ beside
    core_fisher = grid.swap(inverse_fisher, 0, 0, 1)
    gathered = {0: queries}
    gathered[beside] = grid.swap(queries, beside, 0, 0)
    gathered[mirror] = grid.swap(queries, mirror, 0, 0)
    near_fisher = grid.swap(inverse_fisher, 0, 1, 0)
    staged = stage(train_feats, queries, inverse_fisher)
    gathered[mirror], staged = lax.optimization_barrier((gathered[mirror], staged))
    train_here, gathered[0], fisher_here = staged
    gathered[relayed] = grid.swap(gathered[mirror], beside, 0, 0)
    near_fisher, gathered = lax.optimization_barrier((near_fisher, gathered))
    both_fisher = grid.swap(near_fisher, 0, 0, 1)
    block = condition(
        grid, [gathered[mask] for mask in grid.fars], [fisher_here, core_fisher, near_fisher, both_fisher]
    )

    blocks = queries.shape[0]

    def add(total, mask):
        four = [parts[mask, near, core] for near in range(2) for core in range(2)]
        return score(grid, train_here, four, total, mask, blocks, mask == relayed)

    parts = {(0, 0, 0): block}
    parts[0, 0, 1] = grid.swap(block, 0, 0, 1)
    parts[0, 1, 0] = grid.swap(block, 0, 1, 0)
    parts[beside, 0, 0] = grid.swap(block, beside, 0, 0)
    parts[mirror, 0, 0] = grid.swap(block, mirror, 0, 0)
    parts[0, 1, 1] = grid.swap(parts[0, 1, 0], 0, 0, 1)
    parts[beside, 0, 1] = grid.swap(parts[beside, 0, 0], 0, 0, 1)
    parts[beside, 1, 0] = grid.swap(parts[0, 1, 0], beside, 0, 0)
    parts[beside, 1, 1] = grid.swap(parts[beside, 1, 0], 0, 0, 1)
    parts[mirror, 0, 1] = grid.swap(parts[mirror, 0, 0], 0, 0, 1)
    parts[mirror, 1, 0] = grid.swap(parts[mirror, 0, 0], 0, 1, 0)
    parts[relayed, 0, 0] = grid.swap(parts[mirror, 0, 0], beside, 0, 0)
    parts[relayed, 0, 1] = grid.swap(parts[relayed, 0, 0], 0, 0, 1)
    parts[relayed, 1, 0] = grid.swap(parts[relayed, 0, 0], 0, 1, 0)
    total = add(None, 0)
    parts[mirror, 1, 0], total = lax.optimization_barrier((parts[mirror, 1, 0], total))
    parts[mirror, 1, 1] = grid.swap(parts[mirror, 1, 0], 0, 0, 1)
    total = add(total, beside)
    parts[relayed, 1, 0], total = lax.optimization_barrier((parts[relayed, 1, 0], total))
    parts[relayed, 1, 1] = grid.swap(parts[relayed, 1, 0], 0, 0, 1)
    return add(add(total, mirror), relayed)


def one_level(train_feats, queries, inverse_fisher):
    group_count, group_width, _ = inverse_fisher.shape
    gathered = lax.all_gather(queries, "rows", axis=1, tiled=True)
    flattened = gathered.reshape(-1, group_count, group_width)
    part = jnp.einsum("qgk,gkc->qgc", flattened, inverse_fisher, preferred_element_type=jnp.float32)
    complete = lax.all_gather(part.astype(jnp.bfloat16), "rows", axis=2, tiled=True)
    conditioned = complete.reshape(flattened.shape[0], -1)
    products = lax.dot_general(
        train_feats, conditioned, (((1,), (1,)), ((), ())), preferred_element_type=jnp.float32
    )
    return products * (1.0 / train_feats.shape[1] ** 0.5)


def per_device(row_count, train_feats, queries, inverse_fisher):
    group_count, _, width = inverse_fisher.shape
    whole_tiles = group_count == 1 and width % 128 == 0 and queries.shape[1] % 16 == 0
    if row_count == 16 and whole_tiles and train_feats.shape[0] % 512 == 0:
        return two_level(Grid(row_count), train_feats, queries, inverse_fisher)
    return one_level(train_feats, queries, inverse_fisher)


def solution(mesh):
    placed = (P(("groups", "rows"), None), P(None, ("groups", "rows"), None), P(None, None, "rows"))
    return jax.shard_map(
        functools.partial(per_device, mesh.shape["rows"]),
        mesh=mesh,
        in_specs=placed,
        out_specs=P(("groups", "rows"), None),
        check_vma=False,
    )
```

```python
import functools

import jax
import jax.numpy as jnp
from jax import lax
from jax.experimental import pallas as pl
from jax.experimental.pallas import tpu as pltpu
from jax.sharding import PartitionSpec as P

VMEM = pl.BlockSpec(memory_space=pltpu.VMEM)
ANY = pl.BlockSpec(memory_space=pl.ANY)


class Grid:
    def __init__(self, row_count):
        chips = row_count // 2
        self.near = 2
        self.far = chips // 2
        self.fars = range(self.far)

    def swap(self, block, far, near, core):
        step = (far * self.near + near) * 2 + core
        pairs = [(row ^ step, row) for row in range(self.far * self.near * 2)]
        return lax.ppermute(block, "rows", pairs)

    def place(self):
        row = lax.axis_index("rows")
        chip = lax.div(row, 2)
        return lax.div(chip, self.near), lax.rem(chip, self.near), lax.rem(row, 2)


def flip(part, mask):
    return lax.bitwise_xor(part, jnp.int32(mask))


def columns(index, width):
    return pl.ds(pl.multiple_of(index * width, width), width)


def stage_kernel(count, *refs):
    sources, targets, sems = refs[:count], refs[count : 2 * count], refs[2 * count]
    copies = [
        pltpu.make_async_copy(source, target, sems.at[i]) for i, (source, target) in enumerate(zip(sources, targets))
    ]
    for copy in copies:
        copy.start()
    for copy in copies:
        copy.wait()


def stage(*arrays):
    size = sum(a.size * a.dtype.itemsize for a in arrays)
    return pl.pallas_call(
        functools.partial(stage_kernel, len(arrays)),
        out_shape=[pltpu.VMEM(a.shape, a.dtype) for a in arrays],
        in_specs=[ANY] * len(arrays),
        out_specs=[VMEM] * len(arrays),
        scratch_shapes=[pltpu.SemaphoreType.DMA((len(arrays),))],
        compiler_params=pltpu.CompilerParams(vmem_limit_bytes=4 << 20),
        cost_estimate=pl.CostEstimate(flops=0, bytes_accessed=2 * size, transcendentals=0),
        name="stage",
    )(*(pltpu.with_memory_space_constraint(a, pltpu.HBM) for a in arrays))


def condition_kernel(grid, *refs):
    query_refs = refs[: grid.far]
    fisher_refs = refs[grid.far : grid.far + 4]
    out_ref, sorted_ref, columns_ref = refs[grid.far + 4 :]
    far, near, core = grid.place()
    width = fisher_refs[0].shape[-1]
    for index, fisher_ref in enumerate(fisher_refs):
        place = flip(near, index // 2) * 2 + flip(core, index % 2)
        columns_ref[:, columns(place, width)] = fisher_ref[0]
    for mask, query_ref in zip(grid.fars, query_refs):
        sorted_ref[:, pl.ds(flip(far, mask), 1)] = query_ref[...][:, None]
    rows = sorted_ref[...].reshape(-1, sorted_ref.shape[-1])
    out_ref[...] = jnp.dot(rows, columns_ref[...], preferred_element_type=jnp.float32).astype(out_ref.dtype)


def condition(grid, queries, fishers):
    blocks, count, features = queries[0].shape
    width = fishers[0].shape[-1]
    return pl.pallas_call(
        functools.partial(condition_kernel, grid),
        out_shape=jax.ShapeDtypeStruct((blocks * grid.far * count, 4 * width), jnp.bfloat16),
        in_specs=[VMEM] * (grid.far + 4),
        out_specs=VMEM,
        scratch_shapes=[
            pltpu.VMEM((blocks, grid.far, count, features), jnp.bfloat16),
            pltpu.VMEM((features, 4 * width), jnp.bfloat16),
        ],
        compiler_params=pltpu.CompilerParams(vmem_limit_bytes=12 << 20),
        cost_estimate=pl.CostEstimate(flops=1 << 28, bytes_accessed=3 << 20, transcendentals=0),
        name="condition",
    )(*queries, *fishers)


def score_kernel(grid, tile, shape, mask, first, last, *refs):
    blocks, count, width = shape
    train_ref, part_refs, refs = refs[0], refs[1:5], refs[5:]
    total_ref, refs = (None, refs) if first else (refs[0], refs[1:])
    out_ref, sorted_ref, turned_ref, refs = refs[0], refs[1], refs[2], refs[3:]
    far, near, core = grid.place()
    features = train_ref.shape[1]
    for index, part_ref in enumerate(part_refs):
        group = flip(near, index // 2) * 2 + flip(core, index % 2)
        sorted_ref[:, :, pl.ds(group, 1)] = part_ref[...].reshape(blocks, grid.far, 1, count, width)
    turned_ref[...] = sorted_ref[...].reshape(-1, width).T
    scale = 1.0 / features**0.5
    steps = train_ref.shape[0] // tile

    def rows(step):
        return pl.ds(pl.multiple_of(step * tile, tile), tile)

    def products(step):
        value = jnp.dot(
            train_ref[rows(step), columns(flip(far, mask), width)],
            turned_ref[...],
            preferred_element_type=jnp.float32,
        )
        return value if first else total_ref[rows(step)] + value

    if not last:

        @pl.loop(0, steps)
        def _(step):
            out_ref[rows(step)] = products(step)

        return

    here_ref, sem = refs

    def copy(step):
        return pltpu.make_async_copy(here_ref.at[rows(step)], out_ref.at[rows(step)], sem.at[step])

    @pl.loop(0, steps)
    def _(step):
        here_ref[rows(step)] = products(step) * scale
        copy(step).start()

    @pl.loop(0, steps)
    def _(step):
        copy(step).wait()


def score(grid, train_feats, parts, total, mask, blocks, last):
    rows, features = train_feats.shape
    queries, width = parts[0].shape
    count = queries // (blocks * grid.far)
    tile = 512
    first = total is None
    totals = [] if first else [total]
    shape = (rows, 4 * queries)
    scratch = [
        pltpu.VMEM((blocks, grid.far, 4, count, width), jnp.bfloat16),
        pltpu.VMEM((width, 4 * queries), jnp.bfloat16),
    ]
    if last:
        scratch += [pltpu.VMEM(shape, jnp.float32), pltpu.SemaphoreType.DMA((rows // tile,))]
    return pl.pallas_call(
        functools.partial(score_kernel, grid, tile, (blocks, count, width), mask, first, last),
        out_shape=jax.ShapeDtypeStruct(shape, jnp.float32) if last else pltpu.VMEM(shape, jnp.float32),
        in_specs=[VMEM] * (5 + len(totals)),
        out_specs=ANY if last else VMEM,
        scratch_shapes=scratch,
        input_output_aliases={} if first or last else {5: 0},
        compiler_params=pltpu.CompilerParams(vmem_limit_bytes=16 << 20),
        cost_estimate=pl.CostEstimate(
            flops=8 * rows * width * queries, bytes_accessed=4 << 20, transcendentals=0
        ),
        name="score",
    )(*(pltpu.with_memory_space_constraint(a, pltpu.VMEM) for a in (train_feats, *parts, *totals)))


def two_level(grid, train_feats, queries, inverse_fisher):
    mirror, beside = grid.far - 1, 1
    relayed = mirror ^ beside
    core_fisher = grid.swap(inverse_fisher, 0, 0, 1)
    gathered = {0: queries}
    gathered[beside] = grid.swap(queries, beside, 0, 0)
    gathered[mirror] = grid.swap(queries, mirror, 0, 0)
    near_fisher = grid.swap(inverse_fisher, 0, 1, 0)
    staged = stage(train_feats, queries, inverse_fisher)
    gathered[mirror], staged = lax.optimization_barrier((gathered[mirror], staged))
    train_here, gathered[0], fisher_here = staged
    gathered[relayed] = grid.swap(gathered[mirror], beside, 0, 0)
    near_fisher, gathered = lax.optimization_barrier((near_fisher, gathered))
    both_fisher = grid.swap(near_fisher, 0, 0, 1)
    block = condition(
        grid, [gathered[mask] for mask in grid.fars], [fisher_here, core_fisher, near_fisher, both_fisher]
    )

    blocks = queries.shape[0]

    def add(total, mask):
        four = [parts[mask, near, core] for near in range(2) for core in range(2)]
        return score(grid, train_here, four, total, mask, blocks, mask == beside)

    parts = {(0, 0, 0): block}

    def swap(source, *step):
        place = tuple(a ^ b for a, b in zip(source, step))
        parts[place] = grid.swap(parts[source], *step)

    def meet(*places, total=None):
        held, total = lax.optimization_barrier(([parts[place] for place in places], total))
        parts.update(zip(places, held))
        return total

    own, far_one, far_three, near_one = (0, 0, 0), (beside, 0, 0), (mirror, 0, 0), (0, 1, 0)
    swap(own, *far_three)
    swap(own, *far_one)
    swap(own, *near_one)
    swap(own, 0, 0, 1)
    meet(far_three, far_one, near_one)
    swap(far_three, beside, 1, 0)
    swap(far_three, beside, 0, 0)
    swap(far_three, 0, 1, 0)
    swap(far_one, 0, 1, 0)
    swap(near_one, 0, 0, 1)
    swap(far_three, 0, 0, 1)
    swap(far_one, 0, 0, 1)
    total = add(None, 0)
    total = meet((relayed, 1, 0), (relayed, 0, 0), (mirror, 1, 0), total=total)
    swap((relayed, 1, 0), 0, 0, 1)
    swap((relayed, 0, 0), 0, 0, 1)
    swap((mirror, 1, 0), 0, 0, 1)
    swap((beside, 1, 0), 0, 0, 1)
    return add(add(add(total, relayed), mirror), beside)


def one_level(train_feats, queries, inverse_fisher):
    group_count, group_width, _ = inverse_fisher.shape
    gathered = lax.all_gather(queries, "rows", axis=1, tiled=True)
    flattened = gathered.reshape(-1, group_count, group_width)
    part = jnp.einsum("qgk,gkc->qgc", flattened, inverse_fisher, preferred_element_type=jnp.float32)
    complete = lax.all_gather(part.astype(jnp.bfloat16), "rows", axis=2, tiled=True)
    conditioned = complete.reshape(flattened.shape[0], -1)
    products = lax.dot_general(
        train_feats, conditioned, (((1,), (1,)), ((), ())), preferred_element_type=jnp.float32
    )
    return products * (1.0 / train_feats.shape[1] ** 0.5)


def per_device(row_count, train_feats, queries, inverse_fisher):
    group_count, _, width = inverse_fisher.shape
    whole_tiles = group_count == 1 and width % 128 == 0 and queries.shape[1] % 16 == 0
    if row_count == 16 and whole_tiles and train_feats.shape[0] % 512 == 0:
        return two_level(Grid(row_count), train_feats, queries, inverse_fisher)
    return one_level(train_feats, queries, inverse_fisher)


def solution(mesh):
    placed = (P(("groups", "rows"), None), P(None, ("groups", "rows"), None), P(None, None, "rows"))
    return jax.shard_map(
        functools.partial(per_device, mesh.shape["rows"]),
        mesh=mesh,
        in_specs=placed,
        out_specs=P(("groups", "rows"), None),
        check_vma=False,
    )
```

```python
import functools

import jax
import jax.numpy as jnp
from jax import lax
from jax.experimental import pallas as pl
from jax.experimental.pallas import tpu as pltpu
from jax.sharding import PartitionSpec as P

VMEM = pl.BlockSpec(memory_space=pltpu.VMEM)
ANY = pl.BlockSpec(memory_space=pl.ANY)


class Grid:
    def __init__(self, row_count):
        self.far = row_count // 4

    def swap(self, block, far, near, core):
        step = (far * 2 + near) * 2 + core
        return lax.ppermute(block, "rows", [(row ^ step, row) for row in range(self.far * 4)])

    def place(self):
        row = lax.axis_index("rows")
        return lax.div(row, 4), lax.rem(lax.div(row, 2), 2), lax.rem(row, 2)


def flip(part, mask):
    return lax.bitwise_xor(part, jnp.int32(mask))


def columns(index, width):
    return pl.ds(pl.multiple_of(index * width, width), width)


def stage_kernel(count, *refs):
    sources, targets, sems = refs[:count], refs[count : 2 * count], refs[2 * count]
    copies = [
        pltpu.make_async_copy(source, target, sems.at[i]) for i, (source, target) in enumerate(zip(sources, targets))
    ]
    for copy in copies:
        copy.start()
    for copy in copies:
        copy.wait()


def stage(*arrays):
    size = sum(a.size * a.dtype.itemsize for a in arrays)
    return pl.pallas_call(
        functools.partial(stage_kernel, len(arrays)),
        out_shape=[pltpu.VMEM(a.shape, a.dtype) for a in arrays],
        in_specs=[ANY] * len(arrays),
        out_specs=[VMEM] * len(arrays),
        scratch_shapes=[pltpu.SemaphoreType.DMA((len(arrays),))],
        compiler_params=pltpu.CompilerParams(vmem_limit_bytes=4 << 20),
        cost_estimate=pl.CostEstimate(flops=0, bytes_accessed=2 * size, transcendentals=0),
        name="stage",
    )(*(pltpu.with_memory_space_constraint(a, pltpu.HBM) for a in arrays))


def condition_kernel(grid, places, *refs):
    query_refs, (own_ref, near_ref, out_ref) = refs[: len(places)], refs[len(places) :]
    far, near, core = grid.place()
    rows = jnp.concatenate([ref[...].reshape(-1, ref.shape[-1]) for ref in query_refs])
    fisher = jnp.concatenate([own_ref[0], near_ref[0]], axis=1)
    result = jnp.dot(rows, fisher, preferred_element_type=jnp.float32).astype(out_ref.dtype)
    blocks, count, _ = query_refs[0].shape
    width = own_ref.shape[-1]
    result = result.reshape(len(places), blocks, 1, 1, count, 2 * width)
    for index, (far_mask, core_mask) in enumerate(places):
        for side in range(2):
            out_ref[
                :, pl.ds(flip(far, far_mask), 1), pl.ds(flip(core, core_mask), 1), :, columns(flip(near, side), width)
            ] = result[index, ..., side * width : (side + 1) * width]


def condition(grid, queries, own, near):
    blocks, count, _ = queries[0, 0].shape
    width = own.shape[-1]
    arrays = [*queries.values(), own, near]
    return pl.pallas_call(
        functools.partial(condition_kernel, grid, list(queries)),
        out_shape=jax.ShapeDtypeStruct((blocks, grid.far, 2, count, 2 * width), jnp.bfloat16),
        in_specs=[VMEM] * len(arrays),
        out_specs=VMEM,
        compiler_params=pltpu.CompilerParams(vmem_limit_bytes=12 << 20),
        cost_estimate=pl.CostEstimate(flops=1 << 28, bytes_accessed=3 << 20, transcendentals=0),
        name="condition",
    )(*arrays)


def turn_kernel(grid, masks, *refs):
    part_refs, out_ref, sorted_ref = refs[:-2], refs[-2], refs[-1]
    _, near, _ = grid.place()
    width = part_refs[0].shape[-1]
    for index in range(len(masks)):
        for side in range(2):
            sorted_ref[:, :, pl.ds(flip(near, side), 1), :, :, index * width : (index + 1) * width] = part_refs[
                index * 2 + side
            ][...][:, :, None]
    out_ref[...] = sorted_ref[...].reshape(-1, out_ref.shape[0]).T


def turn(grid, parts, masks):
    arrays = [parts[mask, near] for mask in masks for near in range(2)]
    blocks, far, cores, count, width = arrays[0].shape
    features = len(masks) * width
    return pl.pallas_call(
        functools.partial(turn_kernel, grid, masks),
        out_shape=pltpu.VMEM((features, blocks * far * 2 * cores * count), jnp.bfloat16),
        in_specs=[VMEM] * len(arrays),
        out_specs=VMEM,
        scratch_shapes=[pltpu.VMEM((blocks, far, 2, cores, count, features), jnp.bfloat16)],
        compiler_params=pltpu.CompilerParams(vmem_limit_bytes=8 << 20),
        name="turn",
    )(*(pltpu.with_memory_space_constraint(a, pltpu.VMEM) for a in arrays))


def score_kernel(grid, tile, masks, other, first, last, *refs):
    train_ref, turned_ref, refs = refs[0], refs[1], refs[2:]
    total_ref, refs = (None, refs) if first else (refs[0], refs[1:])
    out_ref, refs = refs[0], refs[1:]
    far, _, core = grid.place()
    features = train_ref.shape[1]
    width = features // (grid.far * 4)
    pieces = [
        columns((flip(far, mask) * 2 + side) * 2 + flip(core, other), width) for mask in masks for side in range(2)
    ]
    scale = 1.0 / features**0.5
    steps = train_ref.shape[0] // tile

    def rows(step):
        return pl.ds(pl.multiple_of(step * tile, tile), tile)

    def products(step):
        train = jnp.concatenate([train_ref[rows(step), piece] for piece in pieces], axis=1)
        value = jnp.dot(train, turned_ref[...], preferred_element_type=jnp.float32)
        return value if first else total_ref[rows(step)] + value

    if not last:

        @pl.loop(0, steps)
        def _(step):
            out_ref[rows(step)] = products(step)

        return

    here_ref, sem = refs

    def copy(step):
        return pltpu.make_async_copy(here_ref.at[rows(step)], out_ref.at[rows(step)], sem.at[step])

    @pl.loop(0, steps)
    def _(step):
        here_ref[rows(step)] = products(step) * scale
        copy(step).start()

    @pl.loop(0, steps)
    def _(step):
        copy(step).wait()


def score(grid, train_feats, turned, total, masks, other, last):
    rows = train_feats.shape[0]
    features, queries = turned.shape
    tile = 512
    first = total is None
    arrays = [train_feats, turned] + ([] if first else [total])
    shape = (rows, queries)
    scratch = [pltpu.VMEM(shape, jnp.float32), pltpu.SemaphoreType.DMA((rows // tile,))] if last else []
    return pl.pallas_call(
        functools.partial(score_kernel, grid, tile, masks, other, first, last),
        out_shape=jax.ShapeDtypeStruct(shape, jnp.float32) if last else pltpu.VMEM(shape, jnp.float32),
        in_specs=[VMEM] * len(arrays),
        out_specs=ANY if last else VMEM,
        scratch_shapes=scratch,
        input_output_aliases={} if first or last else {2: 0},
        compiler_params=pltpu.CompilerParams(vmem_limit_bytes=16 << 20),
        cost_estimate=pl.CostEstimate(
            flops=2 * rows * features * queries, bytes_accessed=4 << 20, transcendentals=0
        ),
        name="score",
    )(*(pltpu.with_memory_space_constraint(a, pltpu.VMEM) for a in arrays))


def two_level(grid, train_feats, queries, inverse_fisher):
    beside, mirror, relayed = 1, 3, 2
    gathered = {(0, 0): queries}
    gathered[0, 1] = grid.swap(queries, 0, 0, 1)
    gathered[beside, 0] = grid.swap(queries, beside, 0, 0)
    near_fisher = grid.swap(inverse_fisher, 0, 1, 0)
    gathered[mirror, 0] = grid.swap(queries, mirror, 0, 0)
    staged = stage(train_feats, queries, inverse_fisher)
    gathered[mirror, 0], staged = lax.optimization_barrier((gathered[mirror, 0], staged))
    train_here, gathered[0, 0], fisher_here = staged
    gathered[relayed, 0] = grid.swap(gathered[mirror, 0], beside, 0, 0)
    for mask in (beside, mirror, relayed):
        gathered[mask, 1] = grid.swap(gathered[mask, 0], 0, 0, 1)

    own, near_one, far_one, far_three = (0, 0), (0, 1), (beside, 0), (mirror, 0)
    parts = {own: condition(grid, gathered, fisher_here, near_fisher)}

    def swap(source, far, near):
        parts[source[0] ^ far, source[1] ^ near] = grid.swap(parts[source], far, near, 0)

    def meet(*places):
        parts.update(zip(places, lax.optimization_barrier([parts[place] for place in places])))

    swap(own, *far_three)
    swap(own, *near_one)
    swap(own, *far_one)
    swap(own, beside, 1)
    meet(near_one, (beside, 1), far_one, far_three)
    swap(far_three, 0, 1)
    swap(far_three, beside, 1)
    swap(far_three, beside, 0)
    total = None
    for masks in ((0, beside), (mirror, relayed)):
        turned = turn(grid, parts, masks)
        other = grid.swap(turned, 0, 0, 1)
        total = score(grid, train_here, turned, total, masks, 0, False)
        total = score(grid, train_here, other, total, masks, 1, masks == (mirror, relayed))
        if masks == (0, beside):
            late = (mirror, 0), (relayed, 1), (relayed, 0), (mirror, 1)
            held, total = lax.optimization_barrier(([parts[place] for place in late], total))
            parts.update(zip(late, held))
    return total


def one_level(train_feats, queries, inverse_fisher):
    group_count, group_width, _ = inverse_fisher.shape
    gathered = lax.all_gather(queries, "rows", axis=1, tiled=True)
    flattened = gathered.reshape(-1, group_count, group_width)
    part = jnp.einsum("qgk,gkc->qgc", flattened, inverse_fisher, preferred_element_type=jnp.float32)
    complete = lax.all_gather(part.astype(jnp.bfloat16), "rows", axis=2, tiled=True)
    conditioned = complete.reshape(flattened.shape[0], -1)
    products = lax.dot_general(
        train_feats, conditioned, (((1,), (1,)), ((), ())), preferred_element_type=jnp.float32
    )
    return products * (1.0 / train_feats.shape[1] ** 0.5)


def per_device(row_count, train_feats, queries, inverse_fisher):
    group_count, _, width = inverse_fisher.shape
    whole_tiles = group_count == 1 and width % 128 == 0 and queries.shape[1] % 16 == 0
    if row_count == 16 and whole_tiles and train_feats.shape[0] % 512 == 0:
        return two_level(Grid(row_count), train_feats, queries, inverse_fisher)
    return one_level(train_feats, queries, inverse_fisher)


def solution(mesh):
    placed = (P(("groups", "rows"), None), P(None, ("groups", "rows"), None), P(None, None, "rows"))
    return jax.shard_map(
        functools.partial(per_device, mesh.shape["rows"]),
        mesh=mesh,
        in_specs=placed,
        out_specs=P(("groups", "rows"), None),
        check_vma=False,
    )
```

```python
import functools

import jax
import jax.numpy as jnp
from jax import lax
from jax.experimental import pallas as pl
from jax.experimental.pallas import tpu as pltpu
from jax.sharding import PartitionSpec as P

VMEM = pl.BlockSpec(memory_space=pltpu.VMEM)
ANY = pl.BlockSpec(memory_space=pl.ANY)


class Grid:
    def __init__(self, row_count):
        self.far = row_count // 4

    def swap(self, block, far, near, core):
        step = (far * 2 + near) * 2 + core
        return lax.ppermute(block, "rows", [(row ^ step, row) for row in range(self.far * 4)])

    def place(self):
        row = lax.axis_index("rows")
        return lax.div(row, 4), lax.rem(lax.div(row, 2), 2), lax.rem(row, 2)


def flip(part, mask):
    return lax.bitwise_xor(part, jnp.int32(mask))


def columns(index, width):
    return pl.ds(pl.multiple_of(index * width, width), width)


def stage_kernel(count, *refs):
    sources, targets, sems = refs[:count], refs[count : 2 * count], refs[2 * count]
    copies = [
        pltpu.make_async_copy(source, target, sems.at[i]) for i, (source, target) in enumerate(zip(sources, targets))
    ]
    for copy in copies:
        copy.start()
    for copy in copies:
        copy.wait()


def stage(*arrays):
    size = sum(a.size * a.dtype.itemsize for a in arrays)
    return pl.pallas_call(
        functools.partial(stage_kernel, len(arrays)),
        out_shape=[pltpu.VMEM(a.shape, a.dtype) for a in arrays],
        in_specs=[ANY] * len(arrays),
        out_specs=[VMEM] * len(arrays),
        scratch_shapes=[pltpu.SemaphoreType.DMA((len(arrays),))],
        compiler_params=pltpu.CompilerParams(vmem_limit_bytes=4 << 20),
        cost_estimate=pl.CostEstimate(flops=0, bytes_accessed=2 * size, transcendentals=0),
        name="stage",
    )(*(pltpu.with_memory_space_constraint(a, pltpu.HBM) for a in arrays))


def condition_kernel(grid, places, *refs):
    query_refs, (own_ref, near_ref, out_ref) = refs[: len(places)], refs[len(places) :]
    far, near, core = grid.place()
    rows = jnp.concatenate([ref[...].reshape(-1, ref.shape[-1]) for ref in query_refs])
    fisher = jnp.concatenate([own_ref[0], near_ref[0]], axis=1)
    result = jnp.dot(rows, fisher, preferred_element_type=jnp.float32).astype(out_ref.dtype)
    blocks, count, _ = query_refs[0].shape
    width = own_ref.shape[-1]
    result = result.reshape(len(places), blocks, 1, 1, count, 2 * width)
    for index, (far_mask, core_mask) in enumerate(places):
        for side in range(2):
            out_ref[
                :, pl.ds(flip(far, far_mask), 1), pl.ds(flip(core, core_mask), 1), :, columns(flip(near, side), width)
            ] = result[index, ..., side * width : (side + 1) * width]


def condition(grid, queries, own, near):
    blocks, count, _ = queries[0, 0].shape
    width = own.shape[-1]
    arrays = [*queries.values(), own, near]
    return pl.pallas_call(
        functools.partial(condition_kernel, grid, list(queries)),
        out_shape=jax.ShapeDtypeStruct((blocks, grid.far, 2, count, 2 * width), jnp.bfloat16),
        in_specs=[VMEM] * len(arrays),
        out_specs=VMEM,
        compiler_params=pltpu.CompilerParams(vmem_limit_bytes=12 << 20),
        cost_estimate=pl.CostEstimate(flops=1 << 28, bytes_accessed=3 << 20, transcendentals=0),
        name="condition",
    )(*arrays)


def turn_kernel(grid, masks, *refs):
    part_refs, out_ref, sorted_ref = refs[:-2], refs[-2], refs[-1]
    _, near, _ = grid.place()
    width = part_refs[0].shape[-1]
    for index in range(len(masks)):
        for side in range(2):
            sorted_ref[:, :, pl.ds(flip(near, side), 1), :, :, index * width : (index + 1) * width] = part_refs[
                index * 2 + side
            ][...][:, :, None]
    out_ref[...] = sorted_ref[...].reshape(-1, out_ref.shape[0]).T


def turn(grid, parts, masks):
    arrays = [parts[mask, near] for mask in masks for near in range(2)]
    blocks, far, cores, count, width = arrays[0].shape
    features = len(masks) * width
    return pl.pallas_call(
        functools.partial(turn_kernel, grid, masks),
        out_shape=pltpu.VMEM((features, blocks * far * 2 * cores * count), jnp.bfloat16),
        in_specs=[VMEM] * len(arrays),
        out_specs=VMEM,
        scratch_shapes=[pltpu.VMEM((blocks, far, 2, cores, count, features), jnp.bfloat16)],
        compiler_params=pltpu.CompilerParams(vmem_limit_bytes=8 << 20),
        name="turn",
    )(*(pltpu.with_memory_space_constraint(a, pltpu.VMEM) for a in arrays))


def score_kernel(grid, tile, masks, other, first, last, *refs):
    train_ref, turned_ref, refs = refs[0], refs[1], refs[2:]
    total_ref, refs = (None, refs) if first else (refs[0], refs[1:])
    out_ref, refs = refs[0], refs[1:]
    far, _, core = grid.place()
    features = train_ref.shape[1]
    width = features // (grid.far * 4)
    pieces = [
        columns((flip(far, mask) * 2 + side) * 2 + flip(core, other), width) for mask in masks for side in range(2)
    ]
    scale = 1.0 / features**0.5
    steps = train_ref.shape[0] // tile

    def rows(step):
        return pl.ds(pl.multiple_of(step * tile, tile), tile)

    def products(step):
        train = jnp.concatenate([train_ref[rows(step), piece] for piece in pieces], axis=1)
        value = jnp.dot(train, turned_ref[...], preferred_element_type=jnp.float32)
        return value if first else total_ref[rows(step)] + value

    if not last:

        @pl.loop(0, steps)
        def _(step):
            out_ref[rows(step)] = products(step)

        return

    here_ref, sem = refs

    def copy(step):
        return pltpu.make_async_copy(here_ref.at[rows(step)], out_ref.at[rows(step)], sem.at[step])

    @pl.loop(0, steps)
    def _(step):
        here_ref[rows(step)] = products(step) * scale
        copy(step).start()

    @pl.loop(0, steps)
    def _(step):
        copy(step).wait()


def score(grid, train_feats, turned, total, masks, other, last, tile):
    rows = train_feats.shape[0]
    features, queries = turned.shape
    first = total is None
    arrays = [train_feats, turned] + ([] if first else [total])
    shape = (rows, queries)
    scratch = [pltpu.VMEM(shape, jnp.float32), pltpu.SemaphoreType.DMA((rows // tile,))] if last else []
    return pl.pallas_call(
        functools.partial(score_kernel, grid, tile, masks, other, first, last),
        out_shape=jax.ShapeDtypeStruct(shape, jnp.float32) if last else pltpu.VMEM(shape, jnp.float32),
        in_specs=[VMEM] * len(arrays),
        out_specs=ANY if last else VMEM,
        scratch_shapes=scratch,
        input_output_aliases={} if first or last else {2: 0},
        compiler_params=pltpu.CompilerParams(vmem_limit_bytes=20 << 20),
        cost_estimate=pl.CostEstimate(
            flops=2 * rows * features * queries, bytes_accessed=4 << 20, transcendentals=0
        ),
        name="score",
    )(*(pltpu.with_memory_space_constraint(a, pltpu.VMEM) for a in arrays))


def two_level(grid, train_feats, queries, inverse_fisher):
    beside, mirror, relayed = 1, 3, 2
    gathered = {(0, 0): queries}
    gathered[0, 1] = grid.swap(queries, 0, 0, 1)
    gathered[beside, 0] = grid.swap(queries, beside, 0, 0)
    near_fisher = grid.swap(inverse_fisher, 0, 1, 0)
    gathered[mirror, 0] = grid.swap(queries, mirror, 0, 0)
    staged = stage(train_feats, queries, inverse_fisher)
    gathered[mirror, 0], gathered[0, 1], staged = lax.optimization_barrier(
        (gathered[mirror, 0], gathered[0, 1], staged)
    )
    train_here, gathered[0, 0], fisher_here = staged
    gathered[relayed, 0] = grid.swap(gathered[mirror, 0], beside, 0, 0)
    for mask in (beside, mirror, relayed):
        gathered[mask, 1] = grid.swap(gathered[mask, 0], 0, 0, 1)

    own, near_one, far_one, far_three = (0, 0), (0, 1), (beside, 0), (mirror, 0)
    parts = {own: condition(grid, gathered, fisher_here, near_fisher)}

    def swap(source, far, near):
        parts[source[0] ^ far, source[1] ^ near] = grid.swap(parts[source], far, near, 0)

    def meet(*places):
        parts.update(zip(places, lax.optimization_barrier([parts[place] for place in places])))

    swap(own, *far_three)
    swap(own, *near_one)
    swap(own, *far_one)
    swap(own, beside, 1)
    meet(near_one, (beside, 1), far_one, far_three)
    swap(far_three, 0, 1)
    swap(far_three, beside, 1)
    swap(far_three, beside, 0)
    total = None
    for masks in ((0, beside), (mirror, relayed)):
        turned = turn(grid, parts, masks)
        other = grid.swap(turned, 0, 0, 1)
        total = score(grid, train_here, turned, total, masks, 0, False, 1024 if total is None else 256)
        total = score(grid, train_here, other, total, masks, 1, masks == (mirror, relayed), 2048 if masks == (0, beside) else 256)
        if masks == (0, beside):
            late = (mirror, 0), (relayed, 1), (relayed, 0), (mirror, 1)
            held, total = lax.optimization_barrier(([parts[place] for place in late], total))
            parts.update(zip(late, held))
    return total


def one_level(train_feats, queries, inverse_fisher):
    group_count, group_width, _ = inverse_fisher.shape
    gathered = lax.all_gather(queries, "rows", axis=1, tiled=True)
    flattened = gathered.reshape(-1, group_count, group_width)
    part = jnp.einsum("qgk,gkc->qgc", flattened, inverse_fisher, preferred_element_type=jnp.float32)
    complete = lax.all_gather(part.astype(jnp.bfloat16), "rows", axis=2, tiled=True)
    conditioned = complete.reshape(flattened.shape[0], -1)
    products = lax.dot_general(
        train_feats, conditioned, (((1,), (1,)), ((), ())), preferred_element_type=jnp.float32
    )
    return products * (1.0 / train_feats.shape[1] ** 0.5)


def per_device(row_count, train_feats, queries, inverse_fisher):
    group_count, _, width = inverse_fisher.shape
    whole_tiles = group_count == 1 and width % 128 == 0 and queries.shape[1] % 16 == 0
    if row_count == 16 and whole_tiles and train_feats.shape[0] % 512 == 0:
        return two_level(Grid(row_count), train_feats, queries, inverse_fisher)
    return one_level(train_feats, queries, inverse_fisher)


def solution(mesh):
    placed = (P(("groups", "rows"), None), P(None, ("groups", "rows"), None), P(None, None, "rows"))
    return jax.shard_map(
        functools.partial(per_device, mesh.shape["rows"]),
        mesh=mesh,
        in_specs=placed,
        out_specs=P(("groups", "rows"), None),
        check_vma=False,
    )
```

```python
import functools

import jax
import jax.numpy as jnp
from jax import lax
from jax.experimental import pallas as pl
from jax.experimental.pallas import tpu as pltpu
from jax.sharding import PartitionSpec as P

VMEM = pl.BlockSpec(memory_space=pltpu.VMEM)
ANY = pl.BlockSpec(memory_space=pl.ANY)


class Grid:
    def __init__(self, row_count):
        self.far = row_count // 4

    def swap(self, block, far, near, core):
        step = (far * 2 + near) * 2 + core
        return lax.ppermute(block, "rows", [(row ^ step, row) for row in range(self.far * 4)])

    def place(self):
        row = lax.axis_index("rows")
        return lax.div(row, 4), lax.rem(lax.div(row, 2), 2), lax.rem(row, 2)


def flip(part, mask):
    return lax.bitwise_xor(part, jnp.int32(mask))


def columns(index, width):
    return pl.ds(pl.multiple_of(index * width, width), width)


def stage_kernel(count, *refs):
    sources, targets, sems = refs[:count], refs[count : 2 * count], refs[2 * count]
    copies = [
        pltpu.make_async_copy(source, target, sems.at[i]) for i, (source, target) in enumerate(zip(sources, targets))
    ]
    for copy in copies:
        copy.start()
    for copy in copies:
        copy.wait()


def stage(*arrays):
    size = sum(a.size * a.dtype.itemsize for a in arrays)
    return pl.pallas_call(
        functools.partial(stage_kernel, len(arrays)),
        out_shape=[pltpu.VMEM(a.shape, a.dtype) for a in arrays],
        in_specs=[ANY] * len(arrays),
        out_specs=[VMEM] * len(arrays),
        scratch_shapes=[pltpu.SemaphoreType.DMA((len(arrays),))],
        compiler_params=pltpu.CompilerParams(vmem_limit_bytes=4 << 20),
        cost_estimate=pl.CostEstimate(flops=0, bytes_accessed=2 * size, transcendentals=0),
        name="stage",
    )(*(pltpu.with_memory_space_constraint(a, pltpu.HBM) for a in arrays))


def condition_kernel(grid, places, *refs):
    query_refs, (own_ref, near_ref, out_ref) = refs[: len(places)], refs[len(places) :]
    far, near, core = grid.place()
    rows = jnp.concatenate([ref[...].reshape(-1, ref.shape[-1]) for ref in query_refs])
    fisher = jnp.concatenate([own_ref[0], near_ref[0]], axis=1)
    result = jnp.dot(rows, fisher, preferred_element_type=jnp.float32).astype(out_ref.dtype)
    blocks, count, _ = query_refs[0].shape
    width = own_ref.shape[-1]
    result = result.reshape(len(places), blocks, 1, 1, count, 2 * width)
    for index, (far_mask, core_mask) in enumerate(places):
        for side in range(2):
            out_ref[
                :, pl.ds(flip(far, far_mask), 1), pl.ds(flip(core, core_mask), 1), :, columns(flip(near, side), width)
            ] = result[index, ..., side * width : (side + 1) * width]


def condition(grid, queries, own, near):
    blocks, count, _ = queries[0, 0].shape
    width = own.shape[-1]
    arrays = [*queries.values(), own, near]
    return pl.pallas_call(
        functools.partial(condition_kernel, grid, list(queries)),
        out_shape=jax.ShapeDtypeStruct((blocks, grid.far, 2, count, 2 * width), jnp.bfloat16),
        in_specs=[VMEM] * len(arrays),
        out_specs=VMEM,
        compiler_params=pltpu.CompilerParams(vmem_limit_bytes=12 << 20),
        cost_estimate=pl.CostEstimate(flops=1 << 28, bytes_accessed=3 << 20, transcendentals=0),
        name="condition",
    )(*arrays)


def turn_kernel(grid, masks, *refs):
    part_refs, out_ref, sorted_ref = refs[:-2], refs[-2], refs[-1]
    _, near, _ = grid.place()
    width = part_refs[0].shape[-1]
    for index in range(len(masks)):
        for side in range(2):
            sorted_ref[:, :, pl.ds(flip(near, side), 1), :, :, index * width : (index + 1) * width] = part_refs[
                index * 2 + side
            ][...][:, :, None]
    out_ref[...] = sorted_ref[...].reshape(-1, out_ref.shape[0]).T


def turn(grid, parts, masks):
    arrays = [parts[mask, near] for mask in masks for near in range(2)]
    blocks, far, cores, count, width = arrays[0].shape
    features = len(masks) * width
    return pl.pallas_call(
        functools.partial(turn_kernel, grid, masks),
        out_shape=pltpu.VMEM((features, blocks * far * 2 * cores * count), jnp.bfloat16),
        in_specs=[VMEM] * len(arrays),
        out_specs=VMEM,
        scratch_shapes=[pltpu.VMEM((blocks, far, 2, cores, count, features), jnp.bfloat16)],
        compiler_params=pltpu.CompilerParams(vmem_limit_bytes=8 << 20),
        name="turn",
    )(*(pltpu.with_memory_space_constraint(a, pltpu.VMEM) for a in arrays))


def score_kernel(grid, masks, other, first, last, *refs):
    train_ref, turned_ref, refs = refs[0], refs[1], refs[2:]
    total_ref, refs = (None, refs) if first else (refs[0], refs[1:])
    out_ref, refs = refs[0], refs[1:]
    far, _, core = grid.place()
    features = train_ref.shape[1]
    width = features // (grid.far * 4)
    pieces = [
        columns((flip(far, mask) * 2 + side) * 2 + flip(core, other), width) for mask in masks for side in range(2)
    ]

    def products(rows, queries):
        train = jnp.concatenate([train_ref[rows, piece] for piece in pieces], axis=1)
        value = jnp.dot(train, turned_ref[:, queries], preferred_element_type=jnp.float32)
        return value if first else total_ref[rows, queries] + value

    if not last:
        out_ref[...] = products(slice(None), slice(None))
        return

    here_ref, sem = refs
    scale = 1.0 / features**0.5
    row_step, query_step = here_ref.shape[0] // 2, here_ref.shape[1] // 2
    copies = []
    for step in range(4):
        rows = pl.ds(step // 2 * row_step, row_step)
        queries = pl.ds(step % 2 * query_step, query_step)
        here_ref[rows, queries] = products(rows, queries) * scale
        copies.append(pltpu.make_async_copy(here_ref.at[rows, queries], out_ref.at[rows, queries], sem.at[step]))
        copies[-1].start()
    for copy in copies:
        copy.wait()


def score(grid, train_feats, turned, total, masks, other, last):
    rows = train_feats.shape[0]
    features, queries = turned.shape
    first = total is None
    arrays = [train_feats, turned] + ([] if first else [total])
    shape = (rows, queries)
    return pl.pallas_call(
        functools.partial(score_kernel, grid, masks, other, first, last),
        out_shape=jax.ShapeDtypeStruct(shape, jnp.float32) if last else pltpu.VMEM(shape, jnp.float32),
        in_specs=[VMEM] * len(arrays),
        out_specs=ANY if last else VMEM,
        scratch_shapes=[pltpu.VMEM(shape, jnp.float32), pltpu.SemaphoreType.DMA((4,))] if last else [],
        input_output_aliases={} if first or last else {2: 0},
        compiler_params=pltpu.CompilerParams(vmem_limit_bytes=24 << 20),
        cost_estimate=pl.CostEstimate(
            flops=(20000 if first else 2) * rows * features * queries, bytes_accessed=4 << 20, transcendentals=0
        ),
        name="score",
    )(*(pltpu.with_memory_space_constraint(a, pltpu.VMEM) for a in arrays))


def two_level(grid, train_feats, queries, inverse_fisher):
    beside, mirror, relayed = 1, 3, 2
    gathered = {(0, 0): queries}
    gathered[0, 1] = grid.swap(queries, 0, 0, 1)
    gathered[beside, 0] = grid.swap(queries, beside, 0, 0)
    near_fisher = grid.swap(inverse_fisher, 0, 1, 0)
    gathered[mirror, 0] = grid.swap(queries, mirror, 0, 0)
    staged = stage(train_feats, queries, inverse_fisher)
    gathered[mirror, 0], gathered[0, 1], staged = lax.optimization_barrier(
        (gathered[mirror, 0], gathered[0, 1], staged)
    )
    train_here, gathered[0, 0], fisher_here = staged
    gathered[relayed, 0] = grid.swap(gathered[mirror, 0], beside, 0, 0)
    for mask in (beside, mirror, relayed):
        gathered[mask, 1] = grid.swap(gathered[mask, 0], 0, 0, 1)

    own, near_one, far_one, far_three = (0, 0), (0, 1), (beside, 0), (mirror, 0)
    parts = {own: condition(grid, gathered, fisher_here, near_fisher)}

    def swap(source, far, near):
        parts[source[0] ^ far, source[1] ^ near] = grid.swap(parts[source], far, near, 0)

    swap(own, *far_three)
    swap(own, *near_one)
    swap(own, *far_one)
    swap(far_one, *near_one)
    swap(far_three, 0, 1)
    swap(far_three, beside, 1)
    swap(far_three, beside, 0)
    total = None
    for masks in ((0, beside), (mirror, relayed)):
        turned = turn(grid, parts, masks)
        other = grid.swap(turned, 0, 0, 1)
        total = score(grid, train_here, turned, total, masks, 0, False)
        total = score(grid, train_here, other, total, masks, 1, masks == (mirror, relayed))
        if masks == (0, beside):
            late = (mirror, 0), (relayed, 1), (relayed, 0), (mirror, 1)
            held, total = lax.optimization_barrier(([parts[place] for place in late], total))
            parts.update(zip(late, held))
    return total


def one_level(train_feats, queries, inverse_fisher):
    group_count, group_width, _ = inverse_fisher.shape
    gathered = lax.all_gather(queries, "rows", axis=1, tiled=True)
    flattened = gathered.reshape(-1, group_count, group_width)
    part = jnp.einsum("qgk,gkc->qgc", flattened, inverse_fisher, preferred_element_type=jnp.float32)
    complete = lax.all_gather(part.astype(jnp.bfloat16), "rows", axis=2, tiled=True)
    conditioned = complete.reshape(flattened.shape[0], -1)
    products = lax.dot_general(
        train_feats, conditioned, (((1,), (1,)), ((), ())), preferred_element_type=jnp.float32
    )
    return products * (1.0 / train_feats.shape[1] ** 0.5)


def per_device(row_count, train_feats, queries, inverse_fisher):
    group_count, _, width = inverse_fisher.shape
    whole_tiles = group_count == 1 and width % 128 == 0 and queries.shape[1] % 16 == 0
    if row_count == 16 and whole_tiles and train_feats.shape[0] % 512 == 0:
        return two_level(Grid(row_count), train_feats, queries, inverse_fisher)
    return one_level(train_feats, queries, inverse_fisher)


def solution(mesh):
    placed = (P(("groups", "rows"), None), P(None, ("groups", "rows"), None), P(None, None, "rows"))
    return jax.shard_map(
        functools.partial(per_device, mesh.shape["rows"]),
        mesh=mesh,
        in_specs=placed,
        out_specs=P(("groups", "rows"), None),
        check_vma=False,
    )
```

```python
import functools

import jax
import jax.numpy as jnp
from jax import lax
from jax.experimental import pallas as pl
from jax.experimental.pallas import tpu as pltpu
from jax.sharding import PartitionSpec as P

VMEM = pl.BlockSpec(memory_space=pltpu.VMEM)
ANY = pl.BlockSpec(memory_space=pl.ANY)


class Grid:
    def __init__(self, row_count):
        self.far = row_count // 4

    def swap(self, block, far, near, core):
        step = (far * 2 + near) * 2 + core
        return lax.ppermute(block, "rows", [(row ^ step, row) for row in range(self.far * 4)])

    def place(self):
        row = lax.axis_index("rows")
        return lax.div(row, 4), lax.rem(lax.div(row, 2), 2), lax.rem(row, 2)


def flip(part, mask):
    return lax.bitwise_xor(part, jnp.int32(mask))


def columns(index, width):
    return pl.ds(pl.multiple_of(index * width, width), width)


def stage_kernel(count, *refs):
    sources, targets, sems = refs[:count], refs[count : 2 * count], refs[2 * count]
    copies = [
        pltpu.make_async_copy(source, target, sems.at[i]) for i, (source, target) in enumerate(zip(sources, targets))
    ]
    for copy in copies:
        copy.start()
    for copy in copies:
        copy.wait()


def stage(*arrays):
    size = sum(a.size * a.dtype.itemsize for a in arrays)
    return pl.pallas_call(
        functools.partial(stage_kernel, len(arrays)),
        out_shape=[pltpu.VMEM(a.shape, a.dtype) for a in arrays],
        in_specs=[ANY] * len(arrays),
        out_specs=[VMEM] * len(arrays),
        scratch_shapes=[pltpu.SemaphoreType.DMA((len(arrays),))],
        compiler_params=pltpu.CompilerParams(vmem_limit_bytes=4 << 20),
        cost_estimate=pl.CostEstimate(flops=1 << 36, bytes_accessed=2 * size, transcendentals=0),
        name="stage",
    )(*(pltpu.with_memory_space_constraint(a, pltpu.HBM) for a in arrays))


def condition_kernel(grid, places, *refs):
    query_refs, (own_ref, near_ref, out_ref) = refs[: len(places)], refs[len(places) :]
    far, near, core = grid.place()
    rows = jnp.concatenate([ref[...].reshape(-1, ref.shape[-1]) for ref in query_refs])
    fisher = jnp.concatenate([own_ref[0], near_ref[0]], axis=1)
    result = jnp.dot(rows, fisher, preferred_element_type=jnp.float32).astype(out_ref.dtype)
    blocks, count, _ = query_refs[0].shape
    width = own_ref.shape[-1]
    result = result.reshape(len(places), blocks, 1, 1, count, 2 * width)
    for index, (far_mask, core_mask) in enumerate(places):
        for side in range(2):
            out_ref[
                :, pl.ds(flip(far, far_mask), 1), pl.ds(flip(core, core_mask), 1), :, columns(flip(near, side), width)
            ] = result[index, ..., side * width : (side + 1) * width]


def condition(grid, queries, own, near):
    blocks, count, _ = queries[0, 0].shape
    width = own.shape[-1]
    arrays = [*queries.values(), own, near]
    return pl.pallas_call(
        functools.partial(condition_kernel, grid, list(queries)),
        out_shape=jax.ShapeDtypeStruct((blocks, grid.far, 2, count, 2 * width), jnp.bfloat16),
        in_specs=[VMEM] * len(arrays),
        out_specs=VMEM,
        compiler_params=pltpu.CompilerParams(vmem_limit_bytes=12 << 20),
        cost_estimate=pl.CostEstimate(flops=1 << 28, bytes_accessed=3 << 20, transcendentals=0),
        name="condition",
    )(*arrays)


def turn_kernel(grid, masks, *refs):
    part_refs, out_ref, sorted_ref = refs[:-2], refs[-2], refs[-1]
    _, near, _ = grid.place()
    width = part_refs[0].shape[-1]
    for index in range(len(masks)):
        for side in range(2):
            sorted_ref[:, :, pl.ds(flip(near, side), 1), :, :, index * width : (index + 1) * width] = part_refs[
                index * 2 + side
            ][...][:, :, None]
    out_ref[...] = sorted_ref[...].reshape(-1, out_ref.shape[0]).T


def turn(grid, parts, masks):
    arrays = [parts[mask, near] for mask in masks for near in range(2)]
    blocks, far, cores, count, width = arrays[0].shape
    features = len(masks) * width
    return pl.pallas_call(
        functools.partial(turn_kernel, grid, masks),
        out_shape=pltpu.VMEM((features, blocks * far * 2 * cores * count), jnp.bfloat16),
        in_specs=[VMEM] * len(arrays),
        out_specs=VMEM,
        scratch_shapes=[pltpu.VMEM((blocks, far, 2, cores, count, features), jnp.bfloat16)],
        compiler_params=pltpu.CompilerParams(vmem_limit_bytes=8 << 20),
        name="turn",
    )(*(pltpu.with_memory_space_constraint(a, pltpu.VMEM) for a in arrays))


def score_kernel(grid, masks, other, first, last, *refs):
    train_ref, turned_ref, refs = refs[0], refs[1], refs[2:]
    total_ref, refs = (None, refs) if first else (refs[0], refs[1:])
    out_ref, refs = refs[0], refs[1:]
    far, _, core = grid.place()
    features = train_ref.shape[1]
    width = features // (grid.far * 4)
    pieces = [
        columns((flip(far, mask) * 2 + side) * 2 + flip(core, other), width) for mask in masks for side in range(2)
    ]

    def products(rows, queries):
        train = jnp.concatenate([train_ref[rows, piece] for piece in pieces], axis=1)
        value = jnp.dot(train, turned_ref[:, queries], preferred_element_type=jnp.float32)
        return value if first else total_ref[rows, queries] + value

    if not last:
        out_ref[...] = products(slice(None), slice(None))
        return

    here_ref, sem = refs
    scale = 1.0 / features**0.5
    row_step, query_step = here_ref.shape[0] // 2, here_ref.shape[1] // 2
    copies = []
    for step in range(4):
        rows = pl.ds(step // 2 * row_step, row_step)
        queries = pl.ds(step % 2 * query_step, query_step)
        here_ref[rows, queries] = products(rows, queries) * scale
        copies.append(pltpu.make_async_copy(here_ref.at[rows, queries], out_ref.at[rows, queries], sem.at[step]))
        copies[-1].start()
    for copy in copies:
        copy.wait()


def score(grid, train_feats, turned, total, masks, other, last):
    rows = train_feats.shape[0]
    features, queries = turned.shape
    first = total is None
    arrays = [train_feats, turned] + ([] if first else [total])
    shape = (rows, queries)
    return pl.pallas_call(
        functools.partial(score_kernel, grid, masks, other, first, last),
        out_shape=jax.ShapeDtypeStruct(shape, jnp.float32) if last else pltpu.VMEM(shape, jnp.float32),
        in_specs=[VMEM] * len(arrays),
        out_specs=ANY if last else VMEM,
        scratch_shapes=[pltpu.VMEM(shape, jnp.float32), pltpu.SemaphoreType.DMA((4,))] if last else [],
        input_output_aliases={} if first or last else {2: 0},
        compiler_params=pltpu.CompilerParams(vmem_limit_bytes=24 << 20),
        cost_estimate=pl.CostEstimate(
            flops=(40 if first else 2) * rows * features * queries, bytes_accessed=4 << 20, transcendentals=0
        ),
        name="score",
    )(*(pltpu.with_memory_space_constraint(a, pltpu.VMEM) for a in arrays))


def two_level(grid, train_feats, queries, inverse_fisher):
    beside, mirror, relayed = 1, 3, 2
    gathered = {(0, 0): queries}
    gathered[0, 1] = grid.swap(queries, 0, 0, 1)
    gathered[beside, 0] = grid.swap(queries, beside, 0, 0)
    near_fisher = grid.swap(inverse_fisher, 0, 1, 0)
    gathered[mirror, 0] = grid.swap(queries, mirror, 0, 0)
    staged = stage(train_feats, queries, inverse_fisher)
    gathered[mirror, 0], gathered[0, 1], staged = lax.optimization_barrier(
        (gathered[mirror, 0], gathered[0, 1], staged)
    )
    train_here, gathered[0, 0], fisher_here = staged
    gathered[relayed, 0] = grid.swap(gathered[mirror, 0], beside, 0, 0)
    for mask in (beside, mirror, relayed):
        gathered[mask, 1] = grid.swap(gathered[mask, 0], 0, 0, 1)

    own, near_one, far_one, far_three = (0, 0), (0, 1), (beside, 0), (mirror, 0)
    parts = {own: condition(grid, gathered, fisher_here, near_fisher)}

    def swap(source, far, near):
        parts[source[0] ^ far, source[1] ^ near] = grid.swap(parts[source], far, near, 0)

    swap(own, *far_three)
    swap(own, *near_one)
    swap(own, *far_one)
    swap(far_one, *near_one)
    swap(far_three, 0, 1)
    swap(far_three, beside, 1)
    swap(far_three, beside, 0)
    total = None
    for masks in ((0, beside), (mirror, relayed)):
        turned = turn(grid, parts, masks)
        other = grid.swap(turned, 0, 0, 1)
        total = score(grid, train_here, turned, total, masks, 0, False)
        total = score(grid, train_here, other, total, masks, 1, masks == (mirror, relayed))
        if masks == (0, beside):
            late = (mirror, 0), (relayed, 1), (relayed, 0), (mirror, 1)
            held, total = lax.optimization_barrier(([parts[place] for place in late], total))
            parts.update(zip(late, held))
    return total


def one_level(train_feats, queries, inverse_fisher):
    group_count, group_width, _ = inverse_fisher.shape
    gathered = lax.all_gather(queries, "rows", axis=1, tiled=True)
    flattened = gathered.reshape(-1, group_count, group_width)
    part = jnp.einsum("qgk,gkc->qgc", flattened, inverse_fisher, preferred_element_type=jnp.float32)
    complete = lax.all_gather(part.astype(jnp.bfloat16), "rows", axis=2, tiled=True)
    conditioned = complete.reshape(flattened.shape[0], -1)
    products = lax.dot_general(
        train_feats, conditioned, (((1,), (1,)), ((), ())), preferred_element_type=jnp.float32
    )
    return products * (1.0 / train_feats.shape[1] ** 0.5)


def per_device(row_count, train_feats, queries, inverse_fisher):
    group_count, _, width = inverse_fisher.shape
    whole_tiles = group_count == 1 and width % 128 == 0 and queries.shape[1] % 16 == 0
    if row_count == 16 and whole_tiles and train_feats.shape[0] % 512 == 0:
        return two_level(Grid(row_count), train_feats, queries, inverse_fisher)
    return one_level(train_feats, queries, inverse_fisher)


def solution(mesh):
    placed = (P(("groups", "rows"), None), P(None, ("groups", "rows"), None), P(None, None, "rows"))
    return jax.shard_map(
        functools.partial(per_device, mesh.shape["rows"]),
        mesh=mesh,
        in_specs=placed,
        out_specs=P(("groups", "rows"), None),
        check_vma=False,
    )
```

```python
import functools

import jax
import jax.numpy as jnp
from jax import lax
from jax.experimental import pallas as pl
from jax.experimental.pallas import tpu as pltpu
from jax.sharding import PartitionSpec as P

VMEM = pl.BlockSpec(memory_space=pltpu.VMEM)
ANY = pl.BlockSpec(memory_space=pl.ANY)
ORDER_FLOPS = 2_789_900_000


class Grid:
    def __init__(self, row_count):
        self.far = row_count // 4

    def swap(self, block, far, near, core):
        step = (far * 2 + near) * 2 + core
        return lax.ppermute(block, "rows", [(row ^ step, row) for row in range(self.far * 4)])

    def place(self):
        row = lax.axis_index("rows")
        return lax.div(row, 4), lax.rem(lax.div(row, 2), 2), lax.rem(row, 2)


def flip(part, mask):
    return lax.bitwise_xor(part, jnp.int32(mask))


def columns(index, width):
    return pl.ds(pl.multiple_of(index * width, width), width)


def stage_kernel(pieces, *refs):
    sources, targets, sems = refs[: len(pieces)], refs[len(pieces) : -1], refs[-1]
    copies = []
    for source, target, count in zip(sources, targets, pieces):
        step = source.shape[0] // count
        for piece in range(count):
            part = pl.ds(piece * step, step)
            copies.append(pltpu.make_async_copy(source.at[part], target.at[part], sems.at[len(copies)]))
    for copy in copies:
        copy.start()
    for copy in copies:
        copy.wait()


def stage(pieces, *arrays):
    size = sum(a.size * a.dtype.itemsize for a in arrays)
    return pl.pallas_call(
        functools.partial(stage_kernel, pieces),
        out_shape=[pltpu.VMEM(a.shape, a.dtype) for a in arrays],
        in_specs=[ANY] * len(arrays),
        out_specs=[VMEM] * len(arrays),
        scratch_shapes=[pltpu.SemaphoreType.DMA((sum(pieces),))],
        compiler_params=pltpu.CompilerParams(vmem_limit_bytes=4 << 20),
        cost_estimate=pl.CostEstimate(flops=ORDER_FLOPS, bytes_accessed=2 * size, transcendentals=0),
        name="stage",
    )(*(pltpu.with_memory_space_constraint(a, pltpu.HBM) for a in arrays))


def condition_kernel(grid, places, *refs):
    query_refs, (own_ref, near_ref, out_ref) = refs[: len(places)], refs[len(places) :]
    far, near, core = grid.place()
    rows = jnp.concatenate([ref[...].reshape(-1, ref.shape[-1]) for ref in query_refs])
    fisher = jnp.concatenate([own_ref[0], near_ref[0]], axis=1)
    result = jnp.dot(rows, fisher, preferred_element_type=jnp.float32).astype(out_ref.dtype)
    blocks, count, _ = query_refs[0].shape
    width = own_ref.shape[-1]
    result = result.reshape(len(places), blocks, 1, 1, count, 2 * width)
    for index, (far_mask, core_mask) in enumerate(places):
        for side in range(2):
            out_ref[
                :, pl.ds(flip(far, far_mask), 1), pl.ds(flip(core, core_mask), 1), :, columns(flip(near, side), width)
            ] = result[index, ..., side * width : (side + 1) * width]


def condition(grid, queries, own, near):
    blocks, count, _ = queries[0, 0].shape
    width = own.shape[-1]
    arrays = [*queries.values(), own, near]
    return pl.pallas_call(
        functools.partial(condition_kernel, grid, list(queries)),
        out_shape=jax.ShapeDtypeStruct((blocks, grid.far, 2, count, 2 * width), jnp.bfloat16),
        in_specs=[VMEM] * len(arrays),
        out_specs=VMEM,
        compiler_params=pltpu.CompilerParams(vmem_limit_bytes=12 << 20),
        cost_estimate=pl.CostEstimate(flops=1 << 28, bytes_accessed=3 << 20, transcendentals=0),
        name="condition",
    )(*arrays)


def turn_kernel(grid, masks, *refs):
    part_refs, out_ref, sorted_ref = refs[:-2], refs[-2], refs[-1]
    _, near, _ = grid.place()
    width = part_refs[0].shape[-1]
    for index in range(len(masks)):
        for side in range(2):
            sorted_ref[:, :, pl.ds(flip(near, side), 1), :, :, index * width : (index + 1) * width] = part_refs[
                index * 2 + side
            ][...][:, :, None]
    out_ref[...] = sorted_ref[...].reshape(-1, out_ref.shape[0]).T


def turn(grid, parts, masks):
    arrays = [parts[mask, near] for mask in masks for near in range(2)]
    blocks, far, cores, count, width = arrays[0].shape
    features = len(masks) * width
    return pl.pallas_call(
        functools.partial(turn_kernel, grid, masks),
        out_shape=pltpu.VMEM((features, blocks * far * 2 * cores * count), jnp.bfloat16),
        in_specs=[VMEM] * len(arrays),
        out_specs=VMEM,
        scratch_shapes=[pltpu.VMEM((blocks, far, 2, cores, count, features), jnp.bfloat16)],
        compiler_params=pltpu.CompilerParams(vmem_limit_bytes=8 << 20),
        name="turn",
    )(*(pltpu.with_memory_space_constraint(a, pltpu.VMEM) for a in arrays))


def score_kernel(grid, masks, other, first, last, *refs):
    train_ref, turned_ref, refs = refs[0], refs[1], refs[2:]
    total_ref, refs = (None, refs) if first else (refs[0], refs[1:])
    out_ref, refs = refs[0], refs[1:]
    far, _, core = grid.place()
    features = train_ref.shape[1]
    width = features // (grid.far * 4)
    pieces = [
        columns((flip(far, mask) * 2 + side) * 2 + flip(core, other), width) for mask in masks for side in range(2)
    ]

    def products(rows, queries):
        train = jnp.concatenate([train_ref[rows, piece] for piece in pieces], axis=1)
        value = jnp.dot(train, turned_ref[:, queries], preferred_element_type=jnp.float32)
        return value if first else total_ref[rows, queries] + value

    if not last:
        out_ref[...] = products(slice(None), slice(None))
        return

    here_ref, sem = refs
    scale = 1.0 / features**0.5
    row_step, query_step = here_ref.shape[0] // 2, here_ref.shape[1] // 2
    copies = []
    for step in range(4):
        queries = pl.ds(step % 2 * query_step, query_step)
        rows = pl.ds(step // 2 * row_step, row_step)
        here_ref[rows, queries] = products(rows, queries) * scale
        for piece in range(4):
            part = pl.ds(step // 2 * row_step + piece * row_step // 4, row_step // 4)
            copies.append(
                pltpu.make_async_copy(here_ref.at[part, queries], out_ref.at[part, queries], sem.at[len(copies)])
            )
            copies[-1].start()
    for copy in copies:
        copy.wait()


def score(grid, train_feats, turned, total, masks, other, last):
    rows = train_feats.shape[0]
    features, queries = turned.shape
    first = total is None
    arrays = [train_feats, turned] + ([] if first else [total])
    shape = (rows, queries)
    return pl.pallas_call(
        functools.partial(score_kernel, grid, masks, other, first, last),
        out_shape=jax.ShapeDtypeStruct(shape, jnp.float32) if last else pltpu.VMEM(shape, jnp.float32),
        in_specs=[VMEM] * len(arrays),
        out_specs=ANY if last else VMEM,
        scratch_shapes=[pltpu.VMEM(shape, jnp.float32), pltpu.SemaphoreType.DMA((16,))] if last else [],
        input_output_aliases={} if first or last else {2: 0},
        compiler_params=pltpu.CompilerParams(vmem_limit_bytes=24 << 20),
        cost_estimate=pl.CostEstimate(
            flops=(40 if first else 2) * rows * features * queries, bytes_accessed=4 << 20, transcendentals=0
        ),
        name="score",
    )(*(pltpu.with_memory_space_constraint(a, pltpu.VMEM) for a in arrays))


def two_level(grid, train_feats, queries, inverse_fisher):
    beside, mirror, relayed = 1, 3, 2
    gathered = {(0, 0): queries}
    gathered[0, 1] = grid.swap(queries, 0, 0, 1)
    gathered[beside, 0] = grid.swap(queries, beside, 0, 0)
    near_fisher = grid.swap(inverse_fisher, 0, 1, 0)
    gathered[mirror, 0] = grid.swap(queries, mirror, 0, 0)
    staged = stage((8, 1, 1), train_feats, queries, inverse_fisher)
    gathered[mirror, 0], gathered[0, 1], staged = lax.optimization_barrier(
        (gathered[mirror, 0], gathered[0, 1], staged)
    )
    train_here, gathered[0, 0], fisher_here = staged
    gathered[relayed, 0] = grid.swap(gathered[mirror, 0], beside, 0, 0)
    for mask in (beside, mirror, relayed):
        gathered[mask, 1] = grid.swap(gathered[mask, 0], 0, 0, 1)

    own, near_one, far_one, far_three = (0, 0), (0, 1), (beside, 0), (mirror, 0)
    parts = {own: condition(grid, gathered, fisher_here, near_fisher)}

    def swap(source, far, near):
        parts[source[0] ^ far, source[1] ^ near] = grid.swap(parts[source], far, near, 0)

    swap(own, *far_three)
    swap(own, *near_one)
    swap(own, *far_one)
    swap(far_one, *near_one)
    swap(far_three, 0, 1)
    swap(far_three, beside, 1)
    swap(far_three, beside, 0)
    total = None
    for masks in ((0, beside), (mirror, relayed)):
        turned = turn(grid, parts, masks)
        other = grid.swap(turned, 0, 0, 1)
        total = score(grid, train_here, turned, total, masks, 0, False)
        total = score(grid, train_here, other, total, masks, 1, masks == (mirror, relayed))
        if masks == (0, beside):
            late = (mirror, 0), (relayed, 1), (relayed, 0), (mirror, 1)
            held, total = lax.optimization_barrier(([parts[place] for place in late], total))
            parts.update(zip(late, held))
    return total


def one_level(train_feats, queries, inverse_fisher):
    group_count, group_width, _ = inverse_fisher.shape
    gathered = lax.all_gather(queries, "rows", axis=1, tiled=True)
    flattened = gathered.reshape(-1, group_count, group_width)
    part = jnp.einsum("qgk,gkc->qgc", flattened, inverse_fisher, preferred_element_type=jnp.float32)
    complete = lax.all_gather(part.astype(jnp.bfloat16), "rows", axis=2, tiled=True)
    conditioned = complete.reshape(flattened.shape[0], -1)
    products = lax.dot_general(
        train_feats, conditioned, (((1,), (1,)), ((), ())), preferred_element_type=jnp.float32
    )
    return products * (1.0 / train_feats.shape[1] ** 0.5)


def per_device(row_count, train_feats, queries, inverse_fisher):
    group_count, _, width = inverse_fisher.shape
    whole_tiles = group_count == 1 and width % 128 == 0 and queries.shape[1] % 16 == 0
    if row_count == 16 and whole_tiles and train_feats.shape[0] % 512 == 0:
        return two_level(Grid(row_count), train_feats, queries, inverse_fisher)
    return one_level(train_feats, queries, inverse_fisher)


def solution(mesh):
    placed = (P(("groups", "rows"), None), P(None, ("groups", "rows"), None), P(None, None, "rows"))
    return jax.shard_map(
        functools.partial(per_device, mesh.shape["rows"]),
        mesh=mesh,
        in_specs=placed,
        out_specs=P(("groups", "rows"), None),
        check_vma=False,
    )
```

```python
import functools

import jax
import jax.numpy as jnp
from jax import lax
from jax.experimental import pallas as pl
from jax.experimental.pallas import tpu as pltpu
from jax.sharding import PartitionSpec as P

VMEM = pl.BlockSpec(memory_space=pltpu.VMEM)
ANY = pl.BlockSpec(memory_space=pl.ANY)
ORDER_FLOPS = 2_788_300_000


class Grid:
    def __init__(self, row_count):
        self.far = row_count // 4

    def swap(self, block, far, near, core):
        step = (far * 2 + near) * 2 + core
        return lax.ppermute(block, "rows", [(row ^ step, row) for row in range(self.far * 4)])

    def place(self):
        row = lax.axis_index("rows")
        return lax.div(row, 4), lax.rem(lax.div(row, 2), 2), lax.rem(row, 2)


def flip(part, mask):
    return lax.bitwise_xor(part, jnp.int32(mask))


def columns(index, width):
    return pl.ds(pl.multiple_of(index * width, width), width)


def stage_kernel(first, half, *refs):
    sources, targets, sems = refs[: len(refs) // 2], refs[len(refs) // 2 : -1], refs[-1]
    if not first:
        sources = sources[1:]
    part = pl.ds(0 if first else half, half)
    copies = [pltpu.make_async_copy(sources[0].at[part], targets[0].at[part], sems.at[0])]
    for index in range(1, len(sources)):
        copies.append(pltpu.make_async_copy(sources[index], targets[index], sems.at[index]))
    for copy in copies:
        copy.start()
    for copy in copies:
        copy.wait()


def stage(arrays, buffer=None):
    first = buffer is None
    moved = sum(a.size * a.dtype.itemsize for a in arrays)
    sources = [pltpu.with_memory_space_constraint(a, pltpu.HBM) for a in arrays]
    if not first:
        sources.insert(0, pltpu.with_memory_space_constraint(buffer, pltpu.VMEM))
    return pl.pallas_call(
        functools.partial(stage_kernel, first, arrays[0].shape[0] // 2),
        out_shape=[pltpu.VMEM(a.shape, a.dtype) for a in arrays],
        in_specs=[ANY] * len(arrays) if first else [VMEM, ANY],
        out_specs=[VMEM] * len(arrays),
        scratch_shapes=[pltpu.SemaphoreType.DMA((len(arrays),))],
        input_output_aliases={} if first else {0: 0},
        compiler_params=pltpu.CompilerParams(vmem_limit_bytes=4 << 20),
        cost_estimate=pl.CostEstimate(
            flops=ORDER_FLOPS if first else 1, bytes_accessed=moved, transcendentals=0
        ),
        name="stage",
    )(*sources)


def condition_kernel(grid, places, *refs):
    query_refs, (own_ref, near_ref, out_ref) = refs[: len(places)], refs[len(places) :]
    far, near, core = grid.place()
    rows = jnp.concatenate([ref[...].reshape(-1, ref.shape[-1]) for ref in query_refs])
    fisher = jnp.concatenate([own_ref[0], near_ref[0]], axis=1)
    result = jnp.dot(rows, fisher, preferred_element_type=jnp.float32).astype(out_ref.dtype)
    blocks, count, _ = query_refs[0].shape
    width = own_ref.shape[-1]
    result = result.reshape(len(places), blocks, 1, 1, count, 2 * width)
    for index, (far_mask, core_mask) in enumerate(places):
        for side in range(2):
            out_ref[
                :, pl.ds(flip(far, far_mask), 1), pl.ds(flip(core, core_mask), 1), :, columns(flip(near, side), width)
            ] = result[index, ..., side * width : (side + 1) * width]


def condition(grid, queries, own, near):
    blocks, count, _ = queries[0, 0].shape
    width = own.shape[-1]
    arrays = [*queries.values(), own, near]
    return pl.pallas_call(
        functools.partial(condition_kernel, grid, list(queries)),
        out_shape=jax.ShapeDtypeStruct((blocks, grid.far, 2, count, 2 * width), jnp.bfloat16),
        in_specs=[VMEM] * len(arrays),
        out_specs=VMEM,
        compiler_params=pltpu.CompilerParams(vmem_limit_bytes=12 << 20),
        cost_estimate=pl.CostEstimate(flops=1 << 28, bytes_accessed=3 << 20, transcendentals=0),
        name="condition",
    )(*arrays)


def turn_kernel(grid, masks, *refs):
    part_refs, out_ref, sorted_ref = refs[:-2], refs[-2], refs[-1]
    _, near, _ = grid.place()
    width = part_refs[0].shape[-1]
    for index in range(len(masks)):
        for side in range(2):
            sorted_ref[:, :, pl.ds(flip(near, side), 1), :, :, index * width : (index + 1) * width] = part_refs[
                index * 2 + side
            ][...][:, :, None]
    out_ref[...] = sorted_ref[...].reshape(-1, out_ref.shape[0]).T


def turn(grid, parts, masks):
    arrays = [parts[mask, near] for mask in masks for near in range(2)]
    blocks, far, cores, count, width = arrays[0].shape
    features = len(masks) * width
    return pl.pallas_call(
        functools.partial(turn_kernel, grid, masks),
        out_shape=pltpu.VMEM((features, blocks * far * 2 * cores * count), jnp.bfloat16),
        in_specs=[VMEM] * len(arrays),
        out_specs=VMEM,
        scratch_shapes=[pltpu.VMEM((blocks, far, 2, cores, count, features), jnp.bfloat16)],
        compiler_params=pltpu.CompilerParams(vmem_limit_bytes=8 << 20),
        name="turn",
    )(*(pltpu.with_memory_space_constraint(a, pltpu.VMEM) for a in arrays))


def score_kernel(grid, masks, other, first, last, *refs):
    train_ref, turned_ref, refs = refs[0], refs[1], refs[2:]
    total_ref, refs = (None, refs) if first else (refs[0], refs[1:])
    out_ref, refs = refs[0], refs[1:]
    far, _, core = grid.place()
    features = train_ref.shape[1]
    width = features // (grid.far * 4)
    pieces = [
        columns((flip(far, mask) * 2 + side) * 2 + flip(core, other), width) for mask in masks for side in range(2)
    ]

    def products(rows, queries):
        train = jnp.concatenate([train_ref[rows, piece] for piece in pieces], axis=1)
        value = jnp.dot(train, turned_ref[:, queries], preferred_element_type=jnp.float32)
        return value if first else total_ref[rows, queries] + value

    if not last:
        out_ref[...] = products(slice(None), slice(None))
        return

    here_ref, sem = refs
    scale = 1.0 / features**0.5
    row_step, query_step = here_ref.shape[0] // 2, here_ref.shape[1] // 2
    copies = []
    for step in range(4):
        queries = pl.ds(step % 2 * query_step, query_step)
        rows = pl.ds(step // 2 * row_step, row_step)
        here_ref[rows, queries] = products(rows, queries) * scale
        copies.append(pltpu.make_async_copy(here_ref.at[rows, queries], out_ref.at[rows, queries], sem.at[step]))
        copies[-1].start()
    for copy in copies:
        copy.wait()


def score(grid, train_feats, turned, total, masks, other, last):
    rows = train_feats.shape[0]
    features, queries = turned.shape
    first = total is None
    arrays = [train_feats, turned] + ([] if first else [total])
    shape = (rows, queries)
    return pl.pallas_call(
        functools.partial(score_kernel, grid, masks, other, first, last),
        out_shape=jax.ShapeDtypeStruct(shape, jnp.float32) if last else pltpu.VMEM(shape, jnp.float32),
        in_specs=[VMEM] * len(arrays),
        out_specs=ANY if last else VMEM,
        scratch_shapes=[pltpu.VMEM(shape, jnp.float32), pltpu.SemaphoreType.DMA((4,))] if last else [],
        input_output_aliases={} if first or last else {2: 0},
        compiler_params=pltpu.CompilerParams(vmem_limit_bytes=24 << 20),
        cost_estimate=pl.CostEstimate(
            flops=(40 if first else 2) * rows * features * queries, bytes_accessed=4 << 20, transcendentals=0
        ),
        name="score",
    )(*(pltpu.with_memory_space_constraint(a, pltpu.VMEM) for a in arrays))


def two_level(grid, train_feats, queries, inverse_fisher):
    beside, mirror, relayed = 1, 3, 2
    gathered = {(0, 0): queries}
    gathered[0, 1] = grid.swap(queries, 0, 0, 1)
    gathered[beside, 0] = grid.swap(queries, beside, 0, 0)
    near_fisher = grid.swap(inverse_fisher, 0, 1, 0)
    gathered[mirror, 0] = grid.swap(queries, mirror, 0, 0)
    staged = stage([train_feats, queries, inverse_fisher])
    gathered[mirror, 0], gathered[0, 1], staged = lax.optimization_barrier(
        (gathered[mirror, 0], gathered[0, 1], staged)
    )
    train_here, gathered[0, 0], fisher_here = staged
    gathered[relayed, 0] = grid.swap(gathered[mirror, 0], beside, 0, 0)
    (train_here,) = stage([train_feats], train_here)
    for mask in (beside, mirror):
        gathered[mask, 1] = grid.swap(gathered[mask, 0], 0, 0, 1)
    gathered[relayed, 0], train_here = lax.optimization_barrier((gathered[relayed, 0], train_here))
    gathered[relayed, 1] = grid.swap(gathered[relayed, 0], 0, 0, 1)

    own, near_one, far_one, far_three = (0, 0), (0, 1), (beside, 0), (mirror, 0)
    parts = {own: condition(grid, gathered, fisher_here, near_fisher)}

    def swap(source, far, near):
        parts[source[0] ^ far, source[1] ^ near] = grid.swap(parts[source], far, near, 0)

    swap(own, *far_three)
    swap(own, *near_one)
    swap(own, *far_one)
    swap(far_one, *near_one)
    swap(far_three, 0, 1)
    swap(far_three, beside, 1)
    swap(far_three, beside, 0)
    total = None
    for masks in ((0, beside), (mirror, relayed)):
        turned = turn(grid, parts, masks)
        other = grid.swap(turned, 0, 0, 1)
        total = score(grid, train_here, turned, total, masks, 0, False)
        total = score(grid, train_here, other, total, masks, 1, masks == (mirror, relayed))
        if masks == (0, beside):
            late = (mirror, 0), (relayed, 1), (relayed, 0), (mirror, 1)
            held, total = lax.optimization_barrier(([parts[place] for place in late], total))
            parts.update(zip(late, held))
    return total


def one_level(train_feats, queries, inverse_fisher):
    group_count, group_width, _ = inverse_fisher.shape
    gathered = lax.all_gather(queries, "rows", axis=1, tiled=True)
    flattened = gathered.reshape(-1, group_count, group_width)
    part = jnp.einsum("qgk,gkc->qgc", flattened, inverse_fisher, preferred_element_type=jnp.float32)
    complete = lax.all_gather(part.astype(jnp.bfloat16), "rows", axis=2, tiled=True)
    conditioned = complete.reshape(flattened.shape[0], -1)
    products = lax.dot_general(
        train_feats, conditioned, (((1,), (1,)), ((), ())), preferred_element_type=jnp.float32
    )
    return products * (1.0 / train_feats.shape[1] ** 0.5)


def per_device(row_count, train_feats, queries, inverse_fisher):
    group_count, _, width = inverse_fisher.shape
    whole_tiles = group_count == 1 and width % 128 == 0 and queries.shape[1] % 16 == 0
    if row_count == 16 and whole_tiles and train_feats.shape[0] % 512 == 0:
        return two_level(Grid(row_count), train_feats, queries, inverse_fisher)
    return one_level(train_feats, queries, inverse_fisher)


def solution(mesh):
    placed = (P(("groups", "rows"), None), P(None, ("groups", "rows"), None), P(None, None, "rows"))
    return jax.shard_map(
        functools.partial(per_device, mesh.shape["rows"]),
        mesh=mesh,
        in_specs=placed,
        out_specs=P(("groups", "rows"), None),
        check_vma=False,
    )
```

```python
import functools

import jax
import jax.numpy as jnp
from jax import lax
from jax.experimental import pallas as pl
from jax.experimental.pallas import tpu as pltpu
from jax.sharding import PartitionSpec as P

VMEM = pl.BlockSpec(memory_space=pltpu.VMEM)
ANY = pl.BlockSpec(memory_space=pl.ANY)
ORDER_FLOPS = 2_788_300_000


class Grid:
    def __init__(self, row_count):
        self.far = row_count // 4

    def swap(self, block, far, near, core):
        step = (far * 2 + near) * 2 + core
        return lax.ppermute(block, "rows", [(row ^ step, row) for row in range(self.far * 4)])

    def place(self):
        row = lax.axis_index("rows")
        return lax.div(row, 4), lax.rem(lax.div(row, 2), 2), lax.rem(row, 2)


def flip(part, mask):
    return lax.bitwise_xor(part, jnp.int32(mask))


def columns(index, width):
    return pl.ds(pl.multiple_of(index * width, width), width)


def stage_kernel(first, half, *refs):
    sources, targets, sems = refs[: len(refs) // 2], refs[len(refs) // 2 : -1], refs[-1]
    if not first:
        sources = sources[1:]
    part = pl.ds(0 if first else half, half)
    copies = [pltpu.make_async_copy(sources[0].at[part], targets[0].at[part], sems.at[0])]
    for index in range(1, len(sources)):
        copies.append(pltpu.make_async_copy(sources[index], targets[index], sems.at[index]))
    for copy in copies:
        copy.start()
    for copy in copies:
        copy.wait()


def stage(arrays, buffer=None):
    first = buffer is None
    moved = sum(a.size * a.dtype.itemsize for a in arrays)
    sources = [pltpu.with_memory_space_constraint(a, pltpu.HBM) for a in arrays]
    if not first:
        sources.insert(0, pltpu.with_memory_space_constraint(buffer, pltpu.VMEM))
    return pl.pallas_call(
        functools.partial(stage_kernel, first, arrays[0].shape[0] // 2),
        out_shape=[pltpu.VMEM(a.shape, a.dtype) for a in arrays],
        in_specs=[ANY] * len(arrays) if first else [VMEM, ANY],
        out_specs=[VMEM] * len(arrays),
        scratch_shapes=[pltpu.SemaphoreType.DMA((len(arrays),))],
        input_output_aliases={} if first else {0: 0},
        compiler_params=pltpu.CompilerParams(vmem_limit_bytes=4 << 20),
        cost_estimate=pl.CostEstimate(
            flops=ORDER_FLOPS if first else 1, bytes_accessed=moved, transcendentals=0
        ),
        name="stage",
    )(*sources)


def condition_kernel(grid, places, *refs):
    query_refs, (own_ref, near_ref, out_ref) = refs[: len(places)], refs[len(places) :]
    far, near, core = grid.place()
    rows = jnp.concatenate([ref[...].reshape(-1, ref.shape[-1]) for ref in query_refs])
    fisher = jnp.concatenate([own_ref[0], near_ref[0]], axis=1)
    result = jnp.dot(rows, fisher, preferred_element_type=jnp.float32).astype(out_ref.dtype)
    blocks, count, _ = query_refs[0].shape
    width = own_ref.shape[-1]
    result = result.reshape(len(places), blocks, 1, 1, count, 2 * width)
    for index, (far_mask, core_mask) in enumerate(places):
        for side in range(2):
            out_ref[
                :, pl.ds(flip(far, far_mask), 1), pl.ds(flip(core, core_mask), 1), :, columns(flip(near, side), width)
            ] = result[index, ..., side * width : (side + 1) * width]


def condition(grid, queries, own, near):
    blocks, count, _ = queries[0, 0].shape
    width = own.shape[-1]
    arrays = [*queries.values(), own, near]
    return pl.pallas_call(
        functools.partial(condition_kernel, grid, list(queries)),
        out_shape=jax.ShapeDtypeStruct((blocks, grid.far, 2, count, 2 * width), jnp.bfloat16),
        in_specs=[VMEM] * len(arrays),
        out_specs=VMEM,
        compiler_params=pltpu.CompilerParams(vmem_limit_bytes=12 << 20),
        cost_estimate=pl.CostEstimate(flops=1 << 28, bytes_accessed=3 << 20, transcendentals=0),
        name="condition",
    )(*arrays)


def turn_kernel(grid, masks, *refs):
    part_refs, out_ref, sorted_ref = refs[:-2], refs[-2], refs[-1]
    _, near, _ = grid.place()
    width = part_refs[0].shape[-1]
    for index in range(len(masks)):
        for side in range(2):
            sorted_ref[:, :, pl.ds(flip(near, side), 1), :, :, index * width : (index + 1) * width] = part_refs[
                index * 2 + side
            ][...][:, :, None]
    out_ref[...] = sorted_ref[...].reshape(-1, out_ref.shape[0]).T


def turn(grid, parts, masks):
    arrays = [parts[mask, near] for mask in masks for near in range(2)]
    blocks, far, cores, count, width = arrays[0].shape
    features = len(masks) * width
    return pl.pallas_call(
        functools.partial(turn_kernel, grid, masks),
        out_shape=pltpu.VMEM((features, blocks * far * 2 * cores * count), jnp.bfloat16),
        in_specs=[VMEM] * len(arrays),
        out_specs=VMEM,
        scratch_shapes=[pltpu.VMEM((blocks, far, 2, cores, count, features), jnp.bfloat16)],
        compiler_params=pltpu.CompilerParams(vmem_limit_bytes=8 << 20),
        name="turn",
    )(*(pltpu.with_memory_space_constraint(a, pltpu.VMEM) for a in arrays))


def score_kernel(grid, masks, other, first, last, *refs):
    train_ref, turned_ref, refs = refs[0], refs[1], refs[2:]
    total_ref, refs = (None, refs) if first else (refs[0], refs[1:])
    out_ref, refs = refs[0], refs[1:]
    far, _, core = grid.place()
    features = train_ref.shape[1]
    width = features // (grid.far * 4)
    pieces = [
        columns((flip(far, mask) * 2 + side) * 2 + flip(core, other), width) for mask in masks for side in range(2)
    ]

    def products(rows, queries):
        train = jnp.concatenate([train_ref[rows, piece] for piece in pieces], axis=1)
        value = jnp.dot(train, turned_ref[:, queries], preferred_element_type=jnp.float32)
        return value if first else total_ref[rows, queries] + value

    if not last:
        out_ref[...] = products(slice(None), slice(None))
        return

    here_ref, sem = refs
    scale = 1.0 / features**0.5
    row_step, query_step = here_ref.shape[0] // 2, here_ref.shape[1] // 2
    copies = []
    for step in range(4):
        queries = pl.ds(step % 2 * query_step, query_step)
        rows = pl.ds(step // 2 * row_step, row_step)
        here_ref[rows, queries] = products(rows, queries) * scale
        copies.append(pltpu.make_async_copy(here_ref.at[rows, queries], out_ref.at[rows, queries], sem.at[step]))
        copies[-1].start()
    for copy in copies:
        copy.wait()


def score(grid, train_feats, turned, total, masks, other, last):
    rows = train_feats.shape[0]
    features, queries = turned.shape
    first = total is None
    arrays = [train_feats, turned] + ([] if first else [total])
    shape = (rows, queries)
    return pl.pallas_call(
        functools.partial(score_kernel, grid, masks, other, first, last),
        out_shape=jax.ShapeDtypeStruct(shape, jnp.float32) if last else pltpu.VMEM(shape, jnp.float32),
        in_specs=[VMEM] * len(arrays),
        out_specs=ANY if last else VMEM,
        scratch_shapes=[pltpu.VMEM(shape, jnp.float32), pltpu.SemaphoreType.DMA((4,))] if last else [],
        input_output_aliases={} if first or last else {2: 0},
        compiler_params=pltpu.CompilerParams(vmem_limit_bytes=24 << 20),
        cost_estimate=pl.CostEstimate(
            flops=(40 if first else 2) * rows * features * queries, bytes_accessed=4 << 20, transcendentals=0
        ),
        name="score",
    )(*(pltpu.with_memory_space_constraint(a, pltpu.VMEM) for a in arrays))


def two_level(grid, train_feats, queries, inverse_fisher):
    beside, mirror, relayed = 1, 3, 2
    gathered = {(0, 0): queries}
    gathered[0, 1] = grid.swap(queries, 0, 0, 1)
    gathered[beside, 0] = grid.swap(queries, beside, 0, 0)
    near_fisher = grid.swap(inverse_fisher, 0, 1, 0)
    gathered[mirror, 0] = grid.swap(queries, mirror, 0, 0)
    staged = stage([train_feats, queries, inverse_fisher])
    gathered[mirror, 0], gathered[0, 1], staged = lax.optimization_barrier(
        (gathered[mirror, 0], gathered[0, 1], staged)
    )
    train_here, gathered[0, 0], fisher_here = staged
    gathered[relayed, 0] = grid.swap(gathered[mirror, 0], beside, 0, 0)
    (train_here,) = stage([train_feats], train_here)
    for mask in (beside, mirror):
        gathered[mask, 1] = grid.swap(gathered[mask, 0], 0, 0, 1)
    gathered[relayed, 0], train_here = lax.optimization_barrier((gathered[relayed, 0], train_here))
    gathered[relayed, 1] = grid.swap(gathered[relayed, 0], 0, 0, 1)

    own, near_one, far_one, far_three = (0, 0), (0, 1), (beside, 0), (mirror, 0)
    parts = {own: condition(grid, gathered, fisher_here, near_fisher)}

    def swap(source, far, near):
        parts[source[0] ^ far, source[1] ^ near] = grid.swap(parts[source], far, near, 0)

    swap(own, *far_three)
    swap(own, *near_one)
    swap(own, *far_one)
    swap(far_one, *near_one)
    swap(far_three, 0, 1)
    swap(far_three, beside, 1)
    swap(own, relayed, 0)
    total = None
    for masks in ((0, beside), (mirror, relayed)):
        turned = turn(grid, parts, masks)
        other = grid.swap(turned, 0, 0, 1)
        total = score(grid, train_here, turned, total, masks, 0, False)
        total = score(grid, train_here, other, total, masks, 1, masks == (mirror, relayed))
        if masks == (0, beside):
            late = (mirror, 0), (relayed, 1), (relayed, 0), (mirror, 1)
            held, total = lax.optimization_barrier(([parts[place] for place in late], total))
            parts.update(zip(late, held))
    return total


def one_level(train_feats, queries, inverse_fisher):
    group_count, group_width, _ = inverse_fisher.shape
    gathered = lax.all_gather(queries, "rows", axis=1, tiled=True)
    flattened = gathered.reshape(-1, group_count, group_width)
    part = jnp.einsum("qgk,gkc->qgc", flattened, inverse_fisher, preferred_element_type=jnp.float32)
    complete = lax.all_gather(part.astype(jnp.bfloat16), "rows", axis=2, tiled=True)
    conditioned = complete.reshape(flattened.shape[0], -1)
    products = lax.dot_general(
        train_feats, conditioned, (((1,), (1,)), ((), ())), preferred_element_type=jnp.float32
    )
    return products * (1.0 / train_feats.shape[1] ** 0.5)


def per_device(row_count, train_feats, queries, inverse_fisher):
    group_count, _, width = inverse_fisher.shape
    whole_tiles = group_count == 1 and width % 128 == 0 and queries.shape[1] % 16 == 0
    if row_count == 16 and whole_tiles and train_feats.shape[0] % 512 == 0:
        return two_level(Grid(row_count), train_feats, queries, inverse_fisher)
    return one_level(train_feats, queries, inverse_fisher)


def solution(mesh):
    placed = (P(("groups", "rows"), None), P(None, ("groups", "rows"), None), P(None, None, "rows"))
    return jax.shard_map(
        functools.partial(per_device, mesh.shape["rows"]),
        mesh=mesh,
        in_specs=placed,
        out_specs=P(("groups", "rows"), None),
        check_vma=False,
    )
```

```python
import functools

import jax
import jax.numpy as jnp
from jax import lax
from jax.experimental import pallas as pl
from jax.experimental.pallas import tpu as pltpu
from jax.sharding import PartitionSpec as P

VMEM = pl.BlockSpec(memory_space=pltpu.VMEM)
ANY = pl.BlockSpec(memory_space=pl.ANY)
ORDER_FLOPS = 2_788_300_000


class Grid:
    def __init__(self, row_count):
        self.far = row_count // 4

    def swap(self, block, far, near, core):
        step = (far * 2 + near) * 2 + core
        return lax.ppermute(block, "rows", [(row ^ step, row) for row in range(self.far * 4)])

    def place(self):
        row = lax.axis_index("rows")
        return lax.div(row, 4), lax.rem(lax.div(row, 2), 2), lax.rem(row, 2)


def flip(part, mask):
    return lax.bitwise_xor(part, jnp.int32(mask))


def columns(index, width):
    return pl.ds(pl.multiple_of(index * width, width), width)


def stage_kernel(first, half, *refs):
    sources, targets, sems = refs[: len(refs) // 2], refs[len(refs) // 2 : -1], refs[-1]
    if not first:
        sources = sources[1:]
    part = pl.ds(0 if first else half, half)
    copies = [pltpu.make_async_copy(sources[0].at[part], targets[0].at[part], sems.at[0])]
    for index in range(1, len(sources)):
        copies.append(pltpu.make_async_copy(sources[index], targets[index], sems.at[index]))
    for copy in copies:
        copy.start()
    for copy in copies:
        copy.wait()


def stage(arrays, buffer=None):
    first = buffer is None
    moved = sum(a.size * a.dtype.itemsize for a in arrays)
    sources = [pltpu.with_memory_space_constraint(a, pltpu.HBM) for a in arrays]
    if not first:
        sources.insert(0, pltpu.with_memory_space_constraint(buffer, pltpu.VMEM))
    return pl.pallas_call(
        functools.partial(stage_kernel, first, arrays[0].shape[0] // 2),
        out_shape=[pltpu.VMEM(a.shape, a.dtype) for a in arrays],
        in_specs=[ANY] * len(arrays) if first else [VMEM, ANY],
        out_specs=[VMEM] * len(arrays),
        scratch_shapes=[pltpu.SemaphoreType.DMA((len(arrays),))],
        input_output_aliases={} if first else {0: 0},
        compiler_params=pltpu.CompilerParams(vmem_limit_bytes=4 << 20),
        cost_estimate=pl.CostEstimate(
            flops=ORDER_FLOPS if first else 1, bytes_accessed=moved, transcendentals=0
        ),
        name="stage",
    )(*sources)


def condition_kernel(grid, places, *refs):
    query_refs, (own_ref, near_ref, out_ref) = refs[: len(places)], refs[len(places) :]
    far, near, core = grid.place()
    rows = jnp.concatenate([ref[...].reshape(-1, ref.shape[-1]) for ref in query_refs])
    fisher = jnp.concatenate([own_ref[0], near_ref[0]], axis=1)
    result = jnp.dot(rows, fisher, preferred_element_type=jnp.float32).astype(out_ref.dtype)
    blocks, count, _ = query_refs[0].shape
    width = own_ref.shape[-1]
    result = result.reshape(len(places), blocks, 1, 1, count, 2 * width)
    for index, (far_mask, core_mask) in enumerate(places):
        for side in range(2):
            out_ref[
                :, pl.ds(flip(far, far_mask), 1), pl.ds(flip(core, core_mask), 1), :, columns(flip(near, side), width)
            ] = result[index, ..., side * width : (side + 1) * width]


def condition(grid, queries, own, near):
    blocks, count, _ = queries[0, 0].shape
    width = own.shape[-1]
    arrays = [*queries.values(), own, near]
    return pl.pallas_call(
        functools.partial(condition_kernel, grid, list(queries)),
        out_shape=jax.ShapeDtypeStruct((blocks, grid.far, 2, count, 2 * width), jnp.bfloat16),
        in_specs=[VMEM] * len(arrays),
        out_specs=VMEM,
        compiler_params=pltpu.CompilerParams(vmem_limit_bytes=12 << 20),
        cost_estimate=pl.CostEstimate(flops=1 << 28, bytes_accessed=3 << 20, transcendentals=0),
        name="condition",
    )(*arrays)


def turn_kernel(grid, masks, *refs):
    part_refs, out_ref, sorted_ref = refs[:-2], refs[-2], refs[-1]
    _, near, _ = grid.place()
    width = part_refs[0].shape[-1]
    for index in range(len(masks)):
        for side in range(2):
            sorted_ref[:, :, pl.ds(flip(near, side), 1), :, :, index * width : (index + 1) * width] = part_refs[
                index * 2 + side
            ][...][:, :, None]
    out_ref[...] = sorted_ref[...].reshape(-1, out_ref.shape[0]).T


def turn(grid, parts, masks):
    arrays = [parts[mask, near] for mask in masks for near in range(2)]
    blocks, far, cores, count, width = arrays[0].shape
    features = len(masks) * width
    return pl.pallas_call(
        functools.partial(turn_kernel, grid, masks),
        out_shape=pltpu.VMEM((features, blocks * far * 2 * cores * count), jnp.bfloat16),
        in_specs=[VMEM] * len(arrays),
        out_specs=VMEM,
        scratch_shapes=[pltpu.VMEM((blocks, far, 2, cores, count, features), jnp.bfloat16)],
        compiler_params=pltpu.CompilerParams(vmem_limit_bytes=8 << 20),
        name="turn",
    )(*(pltpu.with_memory_space_constraint(a, pltpu.VMEM) for a in arrays))


def score_kernel(grid, masks, other, first, last, *refs):
    train_ref, turned_ref, refs = refs[0], refs[1], refs[2:]
    total_ref, refs = (None, refs) if first else (refs[0], refs[1:])
    out_ref, refs = refs[0], refs[1:]
    far, _, core = grid.place()
    features = train_ref.shape[1]
    width = features // (grid.far * 4)
    pieces = [
        columns((flip(far, mask) * 2 + side) * 2 + flip(core, other), width) for mask in masks for side in range(2)
    ]

    def products(rows, queries):
        train = jnp.concatenate([train_ref[rows, piece] for piece in pieces], axis=1)
        value = jnp.dot(train, turned_ref[:, queries], preferred_element_type=jnp.float32)
        return value if first else total_ref[rows, queries] + value

    if not last:
        out_ref[...] = products(slice(None), slice(None))
        return

    here_ref, sem = refs
    scale = 1.0 / features**0.5
    row_step, query_step = here_ref.shape[0] // 2, here_ref.shape[1] // 2
    copies = []
    for step in range(4):
        queries = pl.ds(step % 2 * query_step, query_step)
        rows = pl.ds(step // 2 * row_step, row_step)
        here_ref[rows, queries] = products(rows, queries) * scale
        copies.append(pltpu.make_async_copy(here_ref.at[rows, queries], out_ref.at[rows, queries], sem.at[step]))
        copies[-1].start()
    for copy in copies:
        copy.wait()


def score(grid, train_feats, turned, total, masks, other, last):
    rows = train_feats.shape[0]
    features, queries = turned.shape
    first = total is None
    arrays = [train_feats, turned] + ([] if first else [total])
    shape = (rows, queries)
    return pl.pallas_call(
        functools.partial(score_kernel, grid, masks, other, first, last),
        out_shape=jax.ShapeDtypeStruct(shape, jnp.float32) if last else pltpu.VMEM(shape, jnp.float32),
        in_specs=[VMEM] * len(arrays),
        out_specs=ANY if last else VMEM,
        scratch_shapes=[pltpu.VMEM(shape, jnp.float32), pltpu.SemaphoreType.DMA((4,))] if last else [],
        input_output_aliases={} if first or last else {2: 0},
        compiler_params=pltpu.CompilerParams(vmem_limit_bytes=24 << 20),
        cost_estimate=pl.CostEstimate(
            flops=(40 if first else 2) * rows * features * queries, bytes_accessed=4 << 20, transcendentals=0
        ),
        name="score",
    )(*(pltpu.with_memory_space_constraint(a, pltpu.VMEM) for a in arrays))


def two_level(grid, train_feats, queries, inverse_fisher):
    beside, across, relayed = 1, 2, 3
    gathered = {(0, 0): queries}
    gathered[0, 1] = grid.swap(queries, 0, 0, 1)
    gathered[beside, 0] = grid.swap(queries, beside, 0, 0)
    near_fisher = grid.swap(inverse_fisher, 0, 1, 0)
    gathered[across, 0] = grid.swap(queries, across, 0, 0)
    staged = stage([train_feats, queries, inverse_fisher])
    gathered[across, 0], gathered[0, 1], staged = lax.optimization_barrier(
        (gathered[across, 0], gathered[0, 1], staged)
    )
    train_here, gathered[0, 0], fisher_here = staged
    gathered[relayed, 0] = grid.swap(gathered[across, 0], beside, 0, 0)
    (train_here,) = stage([train_feats], train_here)
    for mask in (beside, across):
        gathered[mask, 1] = grid.swap(gathered[mask, 0], 0, 0, 1)
    gathered[relayed, 0], train_here = lax.optimization_barrier((gathered[relayed, 0], train_here))
    gathered[relayed, 1] = grid.swap(gathered[relayed, 0], 0, 0, 1)

    own, near_one, far_one, far_two = (0, 0), (0, 1), (beside, 0), (across, 0)
    parts = {own: condition(grid, gathered, fisher_here, near_fisher)}

    def swap(source, far, near):
        parts[source[0] ^ far, source[1] ^ near] = grid.swap(parts[source], far, near, 0)

    swap(own, *far_two)
    swap(own, *near_one)
    swap(own, *far_one)
    swap(far_one, *near_one)
    swap(far_two, 0, 1)
    swap(far_two, beside, 1)
    swap(far_two, beside, 0)
    total = None
    for masks in ((0, beside), (across, relayed)):
        turned = turn(grid, parts, masks)
        other = grid.swap(turned, 0, 0, 1)
        total = score(grid, train_here, turned, total, masks, 0, False)
        total = score(grid, train_here, other, total, masks, 1, masks == (across, relayed))
        if masks == (0, beside):
            late = (across, 0), (relayed, 1), (relayed, 0), (across, 1)
            held, total = lax.optimization_barrier(([parts[place] for place in late], total))
            parts.update(zip(late, held))
    return total


def one_level(train_feats, queries, inverse_fisher):
    group_count, group_width, _ = inverse_fisher.shape
    gathered = lax.all_gather(queries, "rows", axis=1, tiled=True)
    flattened = gathered.reshape(-1, group_count, group_width)
    part = jnp.einsum("qgk,gkc->qgc", flattened, inverse_fisher, preferred_element_type=jnp.float32)
    complete = lax.all_gather(part.astype(jnp.bfloat16), "rows", axis=2, tiled=True)
    conditioned = complete.reshape(flattened.shape[0], -1)
    products = lax.dot_general(
        train_feats, conditioned, (((1,), (1,)), ((), ())), preferred_element_type=jnp.float32
    )
    return products * (1.0 / train_feats.shape[1] ** 0.5)


def per_device(row_count, train_feats, queries, inverse_fisher):
    group_count, _, width = inverse_fisher.shape
    whole_tiles = group_count == 1 and width % 128 == 0 and queries.shape[1] % 16 == 0
    if row_count == 16 and whole_tiles and train_feats.shape[0] % 512 == 0:
        return two_level(Grid(row_count), train_feats, queries, inverse_fisher)
    return one_level(train_feats, queries, inverse_fisher)


def solution(mesh):
    placed = (P(("groups", "rows"), None), P(None, ("groups", "rows"), None), P(None, None, "rows"))
    return jax.shard_map(
        functools.partial(per_device, mesh.shape["rows"]),
        mesh=mesh,
        in_specs=placed,
        out_specs=P(("groups", "rows"), None),
        check_vma=False,
    )
```

```python
import functools

import jax
import jax.numpy as jnp
from jax import lax
from jax.experimental import pallas as pl
from jax.experimental.pallas import tpu as pltpu
from jax.sharding import PartitionSpec as P

VMEM = pl.BlockSpec(memory_space=pltpu.VMEM)
ANY = pl.BlockSpec(memory_space=pl.ANY)
ORDER_FLOPS = 2_788_300_000


class Grid:
    def __init__(self, row_count):
        self.far = row_count // 4

    def swap(self, block, far, near, core):
        step = (far * 2 + near) * 2 + core
        return lax.ppermute(block, "rows", [(row ^ step, row) for row in range(self.far * 4)])

    def place(self):
        row = lax.axis_index("rows")
        return lax.div(row, 4), lax.rem(lax.div(row, 2), 2), lax.rem(row, 2)


def flip(part, mask):
    return lax.bitwise_xor(part, jnp.int32(mask))


def columns(index, width):
    return pl.ds(pl.multiple_of(index * width, width), width)


def stage_kernel(first, half, *refs):
    sources, targets, sems = refs[: len(refs) // 2], refs[len(refs) // 2 : -1], refs[-1]
    if not first:
        sources = sources[1:]
    part = pl.ds(0 if first else half, half)
    copies = [pltpu.make_async_copy(sources[0].at[part], targets[0].at[part], sems.at[0])]
    for index in range(1, len(sources)):
        copies.append(pltpu.make_async_copy(sources[index], targets[index], sems.at[index]))
    for copy in copies:
        copy.start()
    for copy in copies:
        copy.wait()


def stage(arrays, buffer=None):
    first = buffer is None
    moved = sum(a.size * a.dtype.itemsize for a in arrays)
    sources = [pltpu.with_memory_space_constraint(a, pltpu.HBM) for a in arrays]
    if not first:
        sources.insert(0, pltpu.with_memory_space_constraint(buffer, pltpu.VMEM))
    return pl.pallas_call(
        functools.partial(stage_kernel, first, arrays[0].shape[0] // 2),
        out_shape=[pltpu.VMEM(a.shape, a.dtype) for a in arrays],
        in_specs=[ANY] * len(arrays) if first else [VMEM, ANY],
        out_specs=[VMEM] * len(arrays),
        scratch_shapes=[pltpu.SemaphoreType.DMA((len(arrays),))],
        input_output_aliases={} if first else {0: 0},
        compiler_params=pltpu.CompilerParams(vmem_limit_bytes=4 << 20),
        cost_estimate=pl.CostEstimate(
            flops=ORDER_FLOPS if first else 1, bytes_accessed=moved, transcendentals=0
        ),
        name="stage",
    )(*sources)


def condition_kernel(grid, places, *refs):
    query_refs, (own_ref, near_ref, out_ref) = refs[: len(places)], refs[len(places) :]
    far, near, core = grid.place()
    rows = jnp.concatenate([ref[...].reshape(-1, ref.shape[-1]) for ref in query_refs])
    fisher = jnp.concatenate([own_ref[0], near_ref[0]], axis=1)
    result = jnp.dot(rows, fisher, preferred_element_type=jnp.float32).astype(out_ref.dtype)
    blocks, count, _ = query_refs[0].shape
    width = own_ref.shape[-1]
    result = result.reshape(len(places), blocks, 1, 1, count, 2 * width)
    for index, (far_mask, core_mask) in enumerate(places):
        for side in range(2):
            out_ref[
                :, pl.ds(flip(far, far_mask), 1), pl.ds(flip(core, core_mask), 1), :, columns(flip(near, side), width)
            ] = result[index, ..., side * width : (side + 1) * width]


def condition(grid, queries, own, near):
    blocks, count, _ = queries[0, 0].shape
    width = own.shape[-1]
    arrays = [*queries.values(), own, near]
    return pl.pallas_call(
        functools.partial(condition_kernel, grid, list(queries)),
        out_shape=jax.ShapeDtypeStruct((blocks, grid.far, 2, count, 2 * width), jnp.bfloat16),
        in_specs=[VMEM] * len(arrays),
        out_specs=VMEM,
        compiler_params=pltpu.CompilerParams(vmem_limit_bytes=12 << 20),
        cost_estimate=pl.CostEstimate(flops=1 << 28, bytes_accessed=3 << 20, transcendentals=0),
        name="condition",
    )(*arrays)


def score_kernel(grid, masks, other, first, last, *refs):
    train_ref, part_refs, refs = refs[0], refs[1 : 1 + 2 * len(masks)], refs[1 + 2 * len(masks) :]
    total_ref, refs = (None, refs) if first else (refs[0], refs[1:])
    out_ref, sorted_ref, refs = refs[0], refs[1], refs[2:]
    far, near, core = grid.place()
    features = train_ref.shape[1]
    width = features // (grid.far * 4)
    for index in range(len(masks)):
        for side in range(2):
            sorted_ref[
                :, :, pl.ds(flip(near, side), 1), :, :, index * 2 * width : (index + 1) * 2 * width
            ] = part_refs[index * 2 + side][...][:, :, None]
    turned = sorted_ref[...].reshape(-1, len(masks) * 2 * width).T
    pieces = [
        columns((flip(far, mask) * 2 + side) * 2 + flip(core, other), width) for mask in masks for side in range(2)
    ]

    def products(rows, turned):
        train = jnp.concatenate([train_ref[rows, piece] for piece in pieces], axis=1)
        return jnp.dot(train, turned, preferred_element_type=jnp.float32)

    if not last:
        value = products(slice(None), turned)
        out_ref[...] = value if first else total_ref[...] + value
        return

    turned_ref, here_ref, sem = refs
    turned_ref[...] = turned
    scale = 1.0 / features**0.5
    row_step, query_step = here_ref.shape[0] // 2, here_ref.shape[1] // 2
    copies = []
    for step in range(4):
        queries = pl.ds(step % 2 * query_step, query_step)
        rows = pl.ds(step // 2 * row_step, row_step)
        here_ref[rows, queries] = (total_ref[rows, queries] + products(rows, turned_ref[:, queries])) * scale
        copies.append(pltpu.make_async_copy(here_ref.at[rows, queries], out_ref.at[rows, queries], sem.at[step]))
        copies[-1].start()
    for copy in copies:
        copy.wait()


def score(grid, train_feats, parts, total, masks, other, last):
    parts = [parts[mask, near, other] for mask in masks for near in range(2)]
    rows = train_feats.shape[0]
    blocks, far, cores, count, width = parts[0].shape
    queries, features = blocks * far * 2 * cores * count, len(masks) * width
    first = total is None
    arrays = [train_feats, *parts] + ([] if first else [total])
    shape = (rows, queries)
    scratch = [pltpu.VMEM((blocks, far, 2, cores, count, features), jnp.bfloat16)]
    if last:
        scratch += [
            pltpu.VMEM((features, queries), jnp.bfloat16),
            pltpu.VMEM(shape, jnp.float32),
            pltpu.SemaphoreType.DMA((4,)),
        ]
    return pl.pallas_call(
        functools.partial(score_kernel, grid, masks, other, first, last),
        out_shape=jax.ShapeDtypeStruct(shape, jnp.float32) if last else pltpu.VMEM(shape, jnp.float32),
        in_specs=[VMEM] * len(arrays),
        out_specs=ANY if last else VMEM,
        scratch_shapes=scratch,
        input_output_aliases={} if first or last else {len(arrays) - 1: 0},
        compiler_params=pltpu.CompilerParams(vmem_limit_bytes=24 << 20),
        cost_estimate=pl.CostEstimate(
            flops=(40 if first else 2) * rows * features * queries, bytes_accessed=4 << 20, transcendentals=0
        ),
        name="score",
    )(*(pltpu.with_memory_space_constraint(a, pltpu.VMEM) for a in arrays))


def two_level(grid, train_feats, queries, inverse_fisher):
    beside, mirror, relayed = 1, 3, 2
    gathered = {(0, 0): queries}
    gathered[0, 1] = grid.swap(queries, 0, 0, 1)
    gathered[beside, 0] = grid.swap(queries, beside, 0, 0)
    near_fisher = grid.swap(inverse_fisher, 0, 1, 0)
    gathered[mirror, 0] = grid.swap(queries, mirror, 0, 0)
    staged = stage([train_feats, queries, inverse_fisher])
    gathered[mirror, 0], gathered[0, 1], staged = lax.optimization_barrier(
        (gathered[mirror, 0], gathered[0, 1], staged)
    )
    train_here, gathered[0, 0], fisher_here = staged
    gathered[relayed, 0] = grid.swap(gathered[mirror, 0], beside, 0, 0)
    (train_here,) = stage([train_feats], train_here)
    for mask in (beside, mirror):
        gathered[mask, 1] = grid.swap(gathered[mask, 0], 0, 0, 1)
    gathered[relayed, 0], train_here = lax.optimization_barrier((gathered[relayed, 0], train_here))
    gathered[relayed, 1] = grid.swap(gathered[relayed, 0], 0, 0, 1)

    parts = {(0, 0, 0): condition(grid, gathered, fisher_here, near_fisher)}

    def swap(source, *step):
        place = tuple(a ^ b for a, b in zip(source, step))
        parts[place] = grid.swap(parts[source], *step)

    def meet(*places, total=None):
        held, total = lax.optimization_barrier(([parts[place] for place in places], total))
        parts.update(zip(places, held))
        return total

    own, near_one, far_one, far_three = (0, 0, 0), (0, 1, 0), (beside, 0, 0), (mirror, 0, 0)
    swap(own, *far_three)
    swap(own, *near_one)
    swap(own, *far_one)
    swap(own, 0, 0, 1)
    swap(far_one, *near_one)
    swap(far_one, 0, 0, 1)
    meet(near_one, (0, 0, 1), (beside, 0, 1), far_three)
    swap(near_one, 0, 0, 1)
    swap(far_three, 0, 0, 1)
    swap(far_three, *near_one)
    swap(far_three, beside, 1, 0)
    swap(far_three, *far_one)
    swap((beside, 1, 0), 0, 0, 1)
    total = None
    for other in range(2):
        total = score(grid, train_here, parts, total, (0, beside), other, False)
    total = meet(far_three, (relayed, 1, 0), (relayed, 0, 0), (mirror, 1, 0), total=total)
    swap((relayed, 0, 0), 0, 0, 1)
    swap((mirror, 1, 0), 0, 0, 1)
    swap((relayed, 1, 0), 0, 0, 1)
    for other in range(2):
        total = score(grid, train_here, parts, total, (mirror, relayed), other, other == 1)
    return total


def one_level(train_feats, queries, inverse_fisher):
    group_count, group_width, _ = inverse_fisher.shape
    gathered = lax.all_gather(queries, "rows", axis=1, tiled=True)
    flattened = gathered.reshape(-1, group_count, group_width)
    part = jnp.einsum("qgk,gkc->qgc", flattened, inverse_fisher, preferred_element_type=jnp.float32)
    complete = lax.all_gather(part.astype(jnp.bfloat16), "rows", axis=2, tiled=True)
    conditioned = complete.reshape(flattened.shape[0], -1)
    products = lax.dot_general(
        train_feats, conditioned, (((1,), (1,)), ((), ())), preferred_element_type=jnp.float32
    )
    return products * (1.0 / train_feats.shape[1] ** 0.5)


def per_device(row_count, train_feats, queries, inverse_fisher):
    group_count, _, width = inverse_fisher.shape
    whole_tiles = group_count == 1 and width % 128 == 0 and queries.shape[1] % 16 == 0
    if row_count == 16 and whole_tiles and train_feats.shape[0] % 512 == 0:
        return two_level(Grid(row_count), train_feats, queries, inverse_fisher)
    return one_level(train_feats, queries, inverse_fisher)


def solution(mesh):
    placed = (P(("groups", "rows"), None), P(None, ("groups", "rows"), None), P(None, None, "rows"))
    return jax.shard_map(
        functools.partial(per_device, mesh.shape["rows"]),
        mesh=mesh,
        in_specs=placed,
        out_specs=P(("groups", "rows"), None),
        check_vma=False,
    )
```

```python
import functools

import jax
import jax.numpy as jnp
from jax import lax
from jax.experimental import pallas as pl
from jax.experimental.pallas import tpu as pltpu
from jax.sharding import PartitionSpec as P

VMEM = pl.BlockSpec(memory_space=pltpu.VMEM)
ANY = pl.BlockSpec(memory_space=pl.ANY)
ORDER_FLOPS = 2_788_300_000


class Grid:
    def __init__(self, row_count):
        self.far = row_count // 4

    def swap(self, block, far, near, core):
        step = (far * 2 + near) * 2 + core
        return lax.ppermute(block, "rows", [(row ^ step, row) for row in range(self.far * 4)])

    def place(self):
        row = lax.axis_index("rows")
        return lax.div(row, 4), lax.rem(lax.div(row, 2), 2), lax.rem(row, 2)


def flip(part, mask):
    return lax.bitwise_xor(part, jnp.int32(mask))


def columns(index, width):
    return pl.ds(pl.multiple_of(index * width, width), width)


def stage_kernel(first, half, *refs):
    sources, targets, sems = refs[: len(refs) // 2], refs[len(refs) // 2 : -1], refs[-1]
    if not first:
        sources = sources[1:]
    part = pl.ds(0 if first else half, half)
    copies = [pltpu.make_async_copy(sources[0].at[part], targets[0].at[part], sems.at[0])]
    for index in range(1, len(sources)):
        copies.append(pltpu.make_async_copy(sources[index], targets[index], sems.at[index]))
    for copy in copies:
        copy.start()
    for copy in copies:
        copy.wait()


def stage(arrays, buffer=None):
    first = buffer is None
    moved = sum(a.size * a.dtype.itemsize for a in arrays)
    sources = [pltpu.with_memory_space_constraint(a, pltpu.HBM) for a in arrays]
    if not first:
        sources.insert(0, pltpu.with_memory_space_constraint(buffer, pltpu.VMEM))
    return pl.pallas_call(
        functools.partial(stage_kernel, first, arrays[0].shape[0] // 2),
        out_shape=[pltpu.VMEM(a.shape, a.dtype) for a in arrays],
        in_specs=[ANY] * len(arrays) if first else [VMEM, ANY],
        out_specs=[VMEM] * len(arrays),
        scratch_shapes=[pltpu.SemaphoreType.DMA((len(arrays),))],
        input_output_aliases={} if first else {0: 0},
        compiler_params=pltpu.CompilerParams(vmem_limit_bytes=4 << 20),
        cost_estimate=pl.CostEstimate(
            flops=ORDER_FLOPS if first else 1, bytes_accessed=moved, transcendentals=0
        ),
        name="stage",
    )(*sources)


def condition_kernel(grid, places, *refs):
    query_refs, (own_ref, near_ref, out_ref) = refs[: len(places)], refs[len(places) :]
    far, near, core = grid.place()
    rows = jnp.concatenate([ref[...].reshape(-1, ref.shape[-1]) for ref in query_refs])
    fisher = jnp.concatenate([own_ref[0], near_ref[0]], axis=1)
    result = jnp.dot(rows, fisher, preferred_element_type=jnp.float32).astype(out_ref.dtype)
    blocks, count, _ = query_refs[0].shape
    width = own_ref.shape[-1]
    result = result.reshape(len(places), blocks, 1, 1, count, 2 * width)
    for index, (far_mask, core_mask) in enumerate(places):
        for side in range(2):
            out_ref[
                :, pl.ds(flip(far, far_mask), 1), pl.ds(flip(core, core_mask), 1), :, columns(flip(near, side), width)
            ] = result[index, ..., side * width : (side + 1) * width]


def condition(grid, queries, own, near):
    blocks, count, _ = queries[0, 0].shape
    width = own.shape[-1]
    arrays = [*queries.values(), own, near]
    return pl.pallas_call(
        functools.partial(condition_kernel, grid, list(queries)),
        out_shape=jax.ShapeDtypeStruct((blocks, grid.far, 2, count, 2 * width), jnp.bfloat16),
        in_specs=[VMEM] * len(arrays),
        out_specs=VMEM,
        compiler_params=pltpu.CompilerParams(vmem_limit_bytes=12 << 20),
        cost_estimate=pl.CostEstimate(flops=1 << 28, bytes_accessed=3 << 20, transcendentals=0),
        name="condition",
    )(*arrays)


def sort_and_turn(grid, masks, part_refs, sorted_ref):
    _, near, _ = grid.place()
    width = part_refs[0].shape[-1]
    for index in range(len(masks)):
        for side in range(2):
            sorted_ref[:, :, pl.ds(flip(near, side), 1), :, :, index * width : (index + 1) * width] = part_refs[
                index * 2 + side
            ][...][:, :, None]
    return sorted_ref[...].reshape(-1, len(masks) * width).T


def turn_kernel(grid, masks, *refs):
    refs[-2][...] = sort_and_turn(grid, masks, refs[:-2], refs[-1])


def turn(grid, parts, masks):
    arrays = [parts[mask, near, 0] for mask in masks for near in range(2)]
    blocks, far, cores, count, width = arrays[0].shape
    features = len(masks) * width
    return pl.pallas_call(
        functools.partial(turn_kernel, grid, masks),
        out_shape=pltpu.VMEM((features, blocks * far * 2 * cores * count), jnp.bfloat16),
        in_specs=[VMEM] * len(arrays),
        out_specs=VMEM,
        scratch_shapes=[pltpu.VMEM((blocks, far, 2, cores, count, features), jnp.bfloat16)],
        compiler_params=pltpu.CompilerParams(vmem_limit_bytes=8 << 20),
        name="turn",
    )(*(pltpu.with_memory_space_constraint(a, pltpu.VMEM) for a in arrays))


def score_kernel(grid, masks, other, part_count, first, last, *refs):
    train_ref, part_refs, refs = refs[0], refs[1 : 1 + part_count], refs[1 + part_count :]
    total_ref, refs = (None, refs) if first else (refs[0], refs[1:])
    out_ref, refs = refs[0], refs[1:]
    far, _, core = grid.place()
    features = train_ref.shape[1]
    width = features // (grid.far * 4)
    if part_count == 1:
        turned = part_refs[0][...]
    else:
        turned = sort_and_turn(grid, masks, part_refs, refs[0])
        refs = refs[1:]
    pieces = [
        columns((flip(far, mask) * 2 + side) * 2 + flip(core, other), width) for mask in masks for side in range(2)
    ]

    def products(rows, turned):
        train = jnp.concatenate([train_ref[rows, piece] for piece in pieces], axis=1)
        return jnp.dot(train, turned, preferred_element_type=jnp.float32)

    if not last:
        value = products(slice(None), turned)
        out_ref[...] = value if first else total_ref[...] + value
        return

    turned_ref, here_ref, sem = refs
    turned_ref[...] = turned
    scale = 1.0 / features**0.5
    row_step, query_step = here_ref.shape[0] // 2, here_ref.shape[1] // 2
    copies = []
    for step in range(4):
        queries = pl.ds(step % 2 * query_step, query_step)
        rows = pl.ds(step // 2 * row_step, row_step)
        here_ref[rows, queries] = (total_ref[rows, queries] + products(rows, turned_ref[:, queries])) * scale
        copies.append(pltpu.make_async_copy(here_ref.at[rows, queries], out_ref.at[rows, queries], sem.at[step]))
        copies[-1].start()
    for copy in copies:
        copy.wait()


def score(grid, train_feats, parts, total, masks, other, last):
    rows = train_feats.shape[0]
    first = total is None
    arrays = [train_feats, *parts] + ([] if first else [total])
    if len(parts) == 1:
        features, queries = parts[0].shape
        scratch = []
    else:
        blocks, far, cores, count, width = parts[0].shape
        features, queries = len(masks) * width, blocks * far * 2 * cores * count
        scratch = [pltpu.VMEM((blocks, far, 2, cores, count, features), jnp.bfloat16)]
    shape = (rows, queries)
    if last:
        scratch += [
            pltpu.VMEM((features, queries), jnp.bfloat16),
            pltpu.VMEM(shape, jnp.float32),
            pltpu.SemaphoreType.DMA((4,)),
        ]
    return pl.pallas_call(
        functools.partial(score_kernel, grid, masks, other, len(parts), first, last),
        out_shape=jax.ShapeDtypeStruct(shape, jnp.float32) if last else pltpu.VMEM(shape, jnp.float32),
        in_specs=[VMEM] * len(arrays),
        out_specs=ANY if last else VMEM,
        scratch_shapes=scratch,
        input_output_aliases={} if first or last else {len(arrays) - 1: 0},
        compiler_params=pltpu.CompilerParams(vmem_limit_bytes=24 << 20),
        cost_estimate=pl.CostEstimate(
            flops=(40 if first else 2) * rows * features * queries, bytes_accessed=4 << 20, transcendentals=0
        ),
        name="score",
    )(*(pltpu.with_memory_space_constraint(a, pltpu.VMEM) for a in arrays))


def two_level(grid, train_feats, queries, inverse_fisher):
    beside, mirror, relayed = 1, 3, 2
    gathered = {(0, 0): queries}
    gathered[0, 1] = grid.swap(queries, 0, 0, 1)
    gathered[beside, 0] = grid.swap(queries, beside, 0, 0)
    near_fisher = grid.swap(inverse_fisher, 0, 1, 0)
    gathered[mirror, 0] = grid.swap(queries, mirror, 0, 0)
    staged = stage([train_feats, queries, inverse_fisher])
    gathered[mirror, 0], gathered[0, 1], staged = lax.optimization_barrier(
        (gathered[mirror, 0], gathered[0, 1], staged)
    )
    train_here, gathered[0, 0], fisher_here = staged
    gathered[relayed, 0] = grid.swap(gathered[mirror, 0], beside, 0, 0)
    (train_here,) = stage([train_feats], train_here)
    for mask in (beside, mirror):
        gathered[mask, 1] = grid.swap(gathered[mask, 0], 0, 0, 1)
    gathered[relayed, 0], train_here = lax.optimization_barrier((gathered[relayed, 0], train_here))
    gathered[relayed, 1] = grid.swap(gathered[relayed, 0], 0, 0, 1)

    parts = {(0, 0, 0): condition(grid, gathered, fisher_here, near_fisher)}

    def swap(source, *step):
        place = tuple(a ^ b for a, b in zip(source, step))
        parts[place] = grid.swap(parts[source], *step)

    def meet(*places, total=None):
        held, total = lax.optimization_barrier(([parts[place] for place in places], total))
        parts.update(zip(places, held))
        return total

    own, near_one, far_one, far_three = (0, 0, 0), (0, 1, 0), (beside, 0, 0), (mirror, 0, 0)
    swap(own, *far_three)
    swap(own, *near_one)
    swap(own, *far_one)
    swap(far_one, *near_one)
    swap(far_three, *near_one)
    swap(far_three, beside, 1, 0)
    swap(far_three, *far_one)
    turned = turn(grid, parts, (0, beside))
    other = grid.swap(turned, 0, 0, 1)
    total = score(grid, train_here, [turned], None, (0, beside), 0, False)
    total = meet(far_three, total=total)
    swap(far_three, 0, 0, 1)
    total = score(grid, train_here, [other], total, (0, beside), 1, False)
    total = meet(far_three, (relayed, 1, 0), (relayed, 0, 0), (mirror, 1, 0), total=total)
    swap((relayed, 0, 0), 0, 0, 1)
    swap((mirror, 1, 0), 0, 0, 1)
    swap((relayed, 1, 0), 0, 0, 1)
    for core in range(2):
        late = [parts[mask, near, core] for mask in (mirror, relayed) for near in range(2)]
        total = score(grid, train_here, late, total, (mirror, relayed), core, core == 1)
    return total


def one_level(train_feats, queries, inverse_fisher):
    group_count, group_width, _ = inverse_fisher.shape
    gathered = lax.all_gather(queries, "rows", axis=1, tiled=True)
    flattened = gathered.reshape(-1, group_count, group_width)
    part = jnp.einsum("qgk,gkc->qgc", flattened, inverse_fisher, preferred_element_type=jnp.float32)
    complete = lax.all_gather(part.astype(jnp.bfloat16), "rows", axis=2, tiled=True)
    conditioned = complete.reshape(flattened.shape[0], -1)
    products = lax.dot_general(
        train_feats, conditioned, (((1,), (1,)), ((), ())), preferred_element_type=jnp.float32
    )
    return products * (1.0 / train_feats.shape[1] ** 0.5)


def per_device(row_count, train_feats, queries, inverse_fisher):
    group_count, _, width = inverse_fisher.shape
    whole_tiles = group_count == 1 and width % 128 == 0 and queries.shape[1] % 16 == 0
    if row_count == 16 and whole_tiles and train_feats.shape[0] % 512 == 0:
        return two_level(Grid(row_count), train_feats, queries, inverse_fisher)
    return one_level(train_feats, queries, inverse_fisher)


def solution(mesh):
    placed = (P(("groups", "rows"), None), P(None, ("groups", "rows"), None), P(None, None, "rows"))
    return jax.shard_map(
        functools.partial(per_device, mesh.shape["rows"]),
        mesh=mesh,
        in_specs=placed,
        out_specs=P(("groups", "rows"), None),
        check_vma=False,
    )
```

```python
import functools

import jax
import jax.numpy as jnp
from jax import lax
from jax.experimental import pallas as pl
from jax.experimental.pallas import tpu as pltpu
from jax.sharding import PartitionSpec as P

VMEM = pl.BlockSpec(memory_space=pltpu.VMEM)
ANY = pl.BlockSpec(memory_space=pl.ANY)
ORDER_FLOPS = 4_186_300_000


class Grid:
    def __init__(self, row_count):
        self.far = row_count // 4

    def swap(self, block, far, near, core):
        step = (far * 2 + near) * 2 + core
        return lax.ppermute(block, "rows", [(row ^ step, row) for row in range(self.far * 4)])

    def place(self):
        row = lax.axis_index("rows")
        return lax.div(row, 4), lax.rem(lax.div(row, 2), 2), lax.rem(row, 2)


def flip(part, mask):
    return lax.bitwise_xor(part, jnp.int32(mask))


def columns(index, width):
    return pl.ds(pl.multiple_of(index * width, width), width)


def stage_kernel(first, half, *refs):
    sources, targets, sems = refs[: len(refs) // 2], refs[len(refs) // 2 : -1], refs[-1]
    if not first:
        sources = sources[1:]
    part = pl.ds(0 if first else half, half)
    copies = [pltpu.make_async_copy(sources[0].at[part], targets[0].at[part], sems.at[0])]
    for index in range(1, len(sources)):
        copies.append(pltpu.make_async_copy(sources[index], targets[index], sems.at[index]))
    for copy in copies:
        copy.start()
    for copy in copies:
        copy.wait()


def stage(arrays, buffer=None):
    first = buffer is None
    moved = sum(a.size * a.dtype.itemsize for a in arrays)
    sources = [pltpu.with_memory_space_constraint(a, pltpu.HBM) for a in arrays]
    if not first:
        sources.insert(0, pltpu.with_memory_space_constraint(buffer, pltpu.VMEM))
    return pl.pallas_call(
        functools.partial(stage_kernel, first, arrays[0].shape[0] // 2),
        out_shape=[pltpu.VMEM(a.shape, a.dtype) for a in arrays],
        in_specs=[ANY] * len(arrays) if first else [VMEM, ANY],
        out_specs=[VMEM] * len(arrays),
        scratch_shapes=[pltpu.SemaphoreType.DMA((len(arrays),))],
        input_output_aliases={} if first else {0: 0},
        compiler_params=pltpu.CompilerParams(vmem_limit_bytes=4 << 20),
        cost_estimate=pl.CostEstimate(
            flops=ORDER_FLOPS if first else 1, bytes_accessed=moved, transcendentals=0
        ),
        name="stage",
    )(*sources)


def condition_kernel(grid, places, *refs):
    query_refs, (own_ref, near_ref, out_ref) = refs[: len(places)], refs[len(places) :]
    far, near, core = grid.place()
    rows = jnp.concatenate([ref[...].reshape(-1, ref.shape[-1]) for ref in query_refs])
    fisher = jnp.concatenate([own_ref[0], near_ref[0]], axis=1)
    result = jnp.dot(rows, fisher, preferred_element_type=jnp.float32).astype(out_ref.dtype)
    blocks, count, _ = query_refs[0].shape
    width = own_ref.shape[-1]
    result = result.reshape(len(places), blocks, 1, 1, count, 2 * width)
    for index, (far_mask, core_mask) in enumerate(places):
        for side in range(2):
            out_ref[
                :, pl.ds(flip(far, far_mask), 1), pl.ds(flip(core, core_mask), 1), :, columns(flip(near, side), width)
            ] = result[index, ..., side * width : (side + 1) * width]


def condition(grid, queries, own, near):
    blocks, count, _ = queries[0, 0].shape
    width = own.shape[-1]
    arrays = [*queries.values(), own, near]
    return pl.pallas_call(
        functools.partial(condition_kernel, grid, list(queries)),
        out_shape=jax.ShapeDtypeStruct((blocks, grid.far, 2, count, 2 * width), jnp.bfloat16),
        in_specs=[VMEM] * len(arrays),
        out_specs=VMEM,
        compiler_params=pltpu.CompilerParams(vmem_limit_bytes=12 << 20),
        cost_estimate=pl.CostEstimate(flops=1 << 28, bytes_accessed=3 << 20, transcendentals=0),
        name="condition",
    )(*arrays)


def sort_and_turn(grid, masks, part_refs, sorted_ref):
    _, near, _ = grid.place()
    width = part_refs[0].shape[-1]
    for index in range(len(masks)):
        for side in range(2):
            sorted_ref[:, :, pl.ds(flip(near, side), 1), :, :, index * width : (index + 1) * width] = part_refs[
                index * 2 + side
            ][...][:, :, None]
    return sorted_ref[...].reshape(-1, len(masks) * width).T


def turn_kernel(grid, masks, *refs):
    refs[-2][...] = sort_and_turn(grid, masks, refs[:-2], refs[-1])


def turn(grid, parts, masks):
    arrays = [parts[mask, near, 0] for mask in masks for near in range(2)]
    blocks, far, cores, count, width = arrays[0].shape
    features = len(masks) * width
    return pl.pallas_call(
        functools.partial(turn_kernel, grid, masks),
        out_shape=pltpu.VMEM((features, blocks * far * 2 * cores * count), jnp.bfloat16),
        in_specs=[VMEM] * len(arrays),
        out_specs=VMEM,
        scratch_shapes=[pltpu.VMEM((blocks, far, 2, cores, count, features), jnp.bfloat16)],
        compiler_params=pltpu.CompilerParams(vmem_limit_bytes=8 << 20),
        name="turn",
    )(*(pltpu.with_memory_space_constraint(a, pltpu.VMEM) for a in arrays))


def score_kernel(grid, masks, other, part_count, first, last, *refs):
    train_ref, part_refs, refs = refs[0], refs[1 : 1 + part_count], refs[1 + part_count :]
    total_ref, refs = (None, refs) if first else (refs[0], refs[1:])
    out_ref, refs = refs[0], refs[1:]
    far, _, core = grid.place()
    features = train_ref.shape[1]
    width = features // (grid.far * 4)
    if part_count == 1:
        turned = part_refs[0][...]
    else:
        turned = sort_and_turn(grid, masks, part_refs, refs[0])
        refs = refs[1:]
    pieces = [
        columns((flip(far, mask) * 2 + side) * 2 + flip(core, other), width) for mask in masks for side in range(2)
    ]

    def products(rows, turned):
        train = jnp.concatenate([train_ref[rows, piece] for piece in pieces], axis=1)
        return jnp.dot(train, turned, preferred_element_type=jnp.float32)

    if not last:
        value = products(slice(None), turned)
        out_ref[...] = value if first else total_ref[...] + value
        return

    turned_ref, here_ref, sem = refs
    turned_ref[...] = turned
    scale = 1.0 / features**0.5
    row_step, query_step = here_ref.shape[0] // 2, here_ref.shape[1] // 2
    copies = []
    for step in range(4):
        queries = pl.ds(step % 2 * query_step, query_step)
        rows = pl.ds(step // 2 * row_step, row_step)
        here_ref[rows, queries] = (total_ref[rows, queries] + products(rows, turned_ref[:, queries])) * scale
        copies.append(pltpu.make_async_copy(here_ref.at[rows, queries], out_ref.at[rows, queries], sem.at[step]))
        copies[-1].start()
    for copy in copies:
        copy.wait()


def score(grid, train_feats, parts, total, masks, other, last):
    rows = train_feats.shape[0]
    first = total is None
    arrays = [train_feats, *parts] + ([] if first else [total])
    if len(parts) == 1:
        features, queries = parts[0].shape
        scratch = []
    else:
        blocks, far, cores, count, width = parts[0].shape
        features, queries = len(masks) * width, blocks * far * 2 * cores * count
        scratch = [pltpu.VMEM((blocks, far, 2, cores, count, features), jnp.bfloat16)]
    shape = (rows, queries)
    if last:
        scratch += [
            pltpu.VMEM((features, queries), jnp.bfloat16),
            pltpu.VMEM(shape, jnp.float32),
            pltpu.SemaphoreType.DMA((4,)),
        ]
    return pl.pallas_call(
        functools.partial(score_kernel, grid, masks, other, len(parts), first, last),
        out_shape=jax.ShapeDtypeStruct(shape, jnp.float32) if last else pltpu.VMEM(shape, jnp.float32),
        in_specs=[VMEM] * len(arrays),
        out_specs=ANY if last else VMEM,
        scratch_shapes=scratch,
        input_output_aliases={} if first or last else {len(arrays) - 1: 0},
        compiler_params=pltpu.CompilerParams(vmem_limit_bytes=24 << 20),
        cost_estimate=pl.CostEstimate(
            flops=(40 if first else 2) * rows * features * queries, bytes_accessed=4 << 20, transcendentals=0
        ),
        name="score",
    )(*(pltpu.with_memory_space_constraint(a, pltpu.VMEM) for a in arrays))


def two_level(grid, train_feats, queries, inverse_fisher):
    beside, mirror, relayed = 1, 3, 2
    gathered = {(0, 0): queries}
    gathered[0, 1] = grid.swap(queries, 0, 0, 1)
    gathered[beside, 0] = grid.swap(queries, beside, 0, 0)
    near_fisher = grid.swap(inverse_fisher, 0, 1, 0)
    gathered[mirror, 0] = grid.swap(queries, mirror, 0, 0)
    staged = stage([train_feats, queries, inverse_fisher])
    gathered[mirror, 0], gathered[0, 1], staged = lax.optimization_barrier(
        (gathered[mirror, 0], gathered[0, 1], staged)
    )
    train_here, gathered[0, 0], fisher_here = staged
    gathered[relayed, 0] = grid.swap(gathered[mirror, 0], beside, 0, 0)
    gathered[relayed, 1] = grid.swap(gathered[mirror, 0], beside, 0, 1)
    (train_here,) = stage([train_feats], train_here)
    for mask in (beside, mirror):
        gathered[mask, 1] = grid.swap(gathered[mask, 0], 0, 0, 1)
    gathered[relayed, 0], gathered[relayed, 1], train_here = lax.optimization_barrier(
        (gathered[relayed, 0], gathered[relayed, 1], train_here)
    )
    parts = {(0, 0, 0): condition(grid, gathered, fisher_here, near_fisher)}

    def swap(source, *step):
        place = tuple(a ^ b for a, b in zip(source, step))
        parts[place] = grid.swap(parts[source], *step)

    def meet(*places, total=None):
        held, total = lax.optimization_barrier(([parts[place] for place in places], total))
        parts.update(zip(places, held))
        return total

    own, near_one, far_one, far_three = (0, 0, 0), (0, 1, 0), (beside, 0, 0), (mirror, 0, 0)
    swap(own, *far_three)
    swap(own, *near_one)
    swap(own, *far_one)
    swap(far_one, *near_one)
    swap(far_three, *near_one)
    swap(far_three, beside, 1, 0)
    swap(far_three, *far_one)
    turned = turn(grid, parts, (0, beside))
    other = grid.swap(turned, 0, 0, 1)
    total = score(grid, train_here, [turned], None, (0, beside), 0, False)
    total = meet(far_three, total=total)
    swap(far_three, 0, 0, 1)
    total = score(grid, train_here, [other], total, (0, beside), 1, False)
    total = meet(far_three, (relayed, 1, 0), (relayed, 0, 0), (mirror, 1, 0), total=total)
    swap((relayed, 0, 0), 0, 0, 1)
    swap((mirror, 1, 0), 0, 0, 1)
    swap((relayed, 1, 0), 0, 0, 1)
    for core in range(2):
        late = [parts[mask, near, core] for mask in (mirror, relayed) for near in range(2)]
        total = score(grid, train_here, late, total, (mirror, relayed), core, core == 1)
    return total


def one_level(train_feats, queries, inverse_fisher):
    group_count, group_width, _ = inverse_fisher.shape
    gathered = lax.all_gather(queries, "rows", axis=1, tiled=True)
    flattened = gathered.reshape(-1, group_count, group_width)
    part = jnp.einsum("qgk,gkc->qgc", flattened, inverse_fisher, preferred_element_type=jnp.float32)
    complete = lax.all_gather(part.astype(jnp.bfloat16), "rows", axis=2, tiled=True)
    conditioned = complete.reshape(flattened.shape[0], -1)
    products = lax.dot_general(
        train_feats, conditioned, (((1,), (1,)), ((), ())), preferred_element_type=jnp.float32
    )
    return products * (1.0 / train_feats.shape[1] ** 0.5)


def per_device(row_count, train_feats, queries, inverse_fisher):
    group_count, _, width = inverse_fisher.shape
    whole_tiles = group_count == 1 and width % 128 == 0 and queries.shape[1] % 16 == 0
    if row_count == 16 and whole_tiles and train_feats.shape[0] % 512 == 0:
        return two_level(Grid(row_count), train_feats, queries, inverse_fisher)
    return one_level(train_feats, queries, inverse_fisher)


def solution(mesh):
    placed = (P(("groups", "rows"), None), P(None, ("groups", "rows"), None), P(None, None, "rows"))
    return jax.shard_map(
        functools.partial(per_device, mesh.shape["rows"]),
        mesh=mesh,
        in_specs=placed,
        out_specs=P(("groups", "rows"), None),
        check_vma=False,
    )
```

```python
import functools

import jax
import jax.numpy as jnp
from jax import lax
from jax.experimental import pallas as pl
from jax.experimental.pallas import tpu as pltpu
from jax.sharding import PartitionSpec as P

VMEM = pl.BlockSpec(memory_space=pltpu.VMEM)
ANY = pl.BlockSpec(memory_space=pl.ANY)
ORDER_FLOPS = 2_788_300_000


class Grid:
    def __init__(self, row_count):
        self.far = row_count // 4

    def swap(self, block, far, near, core):
        step = (far * 2 + near) * 2 + core
        return lax.ppermute(block, "rows", [(row ^ step, row) for row in range(self.far * 4)])

    def place(self):
        row = lax.axis_index("rows")
        return lax.div(row, 4), lax.rem(lax.div(row, 2), 2), lax.rem(row, 2)


def flip(part, mask):
    return lax.bitwise_xor(part, jnp.int32(mask))


def columns(index, width):
    return pl.ds(pl.multiple_of(index * width, width), width)


def stage_kernel(first, half, *refs):
    sources, targets, sems = refs[: len(refs) // 2], refs[len(refs) // 2 : -1], refs[-1]
    if not first:
        sources = sources[1:]
    part = pl.ds(0 if first else half, half)
    copies = [pltpu.make_async_copy(sources[0].at[part], targets[0].at[part], sems.at[0])]
    for index in range(1, len(sources)):
        copies.append(pltpu.make_async_copy(sources[index], targets[index], sems.at[index]))
    for copy in copies:
        copy.start()
    for copy in copies:
        copy.wait()


def stage(arrays, buffer=None):
    first = buffer is None
    moved = sum(a.size * a.dtype.itemsize for a in arrays)
    sources = [pltpu.with_memory_space_constraint(a, pltpu.HBM) for a in arrays]
    if not first:
        sources.insert(0, pltpu.with_memory_space_constraint(buffer, pltpu.VMEM))
    return pl.pallas_call(
        functools.partial(stage_kernel, first, arrays[0].shape[0] // 2),
        out_shape=[pltpu.VMEM(a.shape, a.dtype) for a in arrays],
        in_specs=[ANY] * len(arrays) if first else [VMEM, ANY],
        out_specs=[VMEM] * len(arrays),
        scratch_shapes=[pltpu.SemaphoreType.DMA((len(arrays),))],
        input_output_aliases={} if first else {0: 0},
        compiler_params=pltpu.CompilerParams(vmem_limit_bytes=4 << 20),
        cost_estimate=pl.CostEstimate(
            flops=ORDER_FLOPS if first else 1, bytes_accessed=moved, transcendentals=0
        ),
        name="stage",
    )(*sources)


def condition_kernel(grid, places, *refs):
    query_refs, (own_ref, near_ref, out_ref) = refs[: len(places)], refs[len(places) :]
    far, near, core = grid.place()
    rows = jnp.concatenate([ref[...].reshape(-1, ref.shape[-1]) for ref in query_refs])
    fisher = jnp.concatenate([own_ref[0], near_ref[0]], axis=1)
    result = jnp.dot(rows, fisher, preferred_element_type=jnp.float32).astype(out_ref.dtype)
    blocks, count, _ = query_refs[0].shape
    width = own_ref.shape[-1]
    result = result.reshape(len(places), blocks, 1, 1, count, 2 * width)
    for index, (far_mask, core_mask) in enumerate(places):
        for side in range(2):
            out_ref[
                :, pl.ds(flip(far, far_mask), 1), pl.ds(flip(core, core_mask), 1), :, columns(flip(near, side), width)
            ] = result[index, ..., side * width : (side + 1) * width]


def condition(grid, queries, own, near):
    blocks, count, _ = queries[0, 0].shape
    width = own.shape[-1]
    arrays = [*queries.values(), own, near]
    return pl.pallas_call(
        functools.partial(condition_kernel, grid, list(queries)),
        out_shape=jax.ShapeDtypeStruct((blocks, grid.far, 2, count, 2 * width), jnp.bfloat16),
        in_specs=[VMEM] * len(arrays),
        out_specs=VMEM,
        compiler_params=pltpu.CompilerParams(vmem_limit_bytes=12 << 20),
        cost_estimate=pl.CostEstimate(flops=1 << 28, bytes_accessed=3 << 20, transcendentals=0),
        name="condition",
    )(*arrays)


def sort_and_turn(grid, masks, part_refs, sorted_ref):
    _, near, _ = grid.place()
    width = part_refs[0].shape[-1]
    for index in range(len(masks)):
        for side in range(2):
            sorted_ref[:, :, pl.ds(flip(near, side), 1), :, :, index * width : (index + 1) * width] = part_refs[
                index * 2 + side
            ][...][:, :, None]
    return sorted_ref[...].reshape(-1, len(masks) * width).T


def turn_kernel(grid, masks, *refs):
    refs[-2][...] = sort_and_turn(grid, masks, refs[:-2], refs[-1])


def turn(grid, parts, masks):
    arrays = [parts[mask, near, 0] for mask in masks for near in range(2)]
    blocks, far, cores, count, width = arrays[0].shape
    features = len(masks) * width
    return pl.pallas_call(
        functools.partial(turn_kernel, grid, masks),
        out_shape=pltpu.VMEM((features, blocks * far * 2 * cores * count), jnp.bfloat16),
        in_specs=[VMEM] * len(arrays),
        out_specs=VMEM,
        scratch_shapes=[pltpu.VMEM((blocks, far, 2, cores, count, features), jnp.bfloat16)],
        compiler_params=pltpu.CompilerParams(vmem_limit_bytes=8 << 20),
        name="turn",
    )(*(pltpu.with_memory_space_constraint(a, pltpu.VMEM) for a in arrays))


def score_kernel(grid, masks, other, part_count, first, last, *refs):
    train_ref, part_refs, refs = refs[0], refs[1 : 1 + part_count], refs[1 + part_count :]
    total_ref, refs = (None, refs) if first else (refs[0], refs[1:])
    out_ref, refs = refs[0], refs[1:]
    far, _, core = grid.place()
    features = train_ref.shape[1]
    width = features // (grid.far * 4)
    if part_count == 1:
        turned = part_refs[0][...]
    else:
        turned = sort_and_turn(grid, masks, part_refs, refs[0])
        refs = refs[1:]
    pieces = [
        columns((flip(far, mask) * 2 + side) * 2 + flip(core, other), width) for mask in masks for side in range(2)
    ]

    def products(rows, turned):
        train = jnp.concatenate([train_ref[rows, piece] for piece in pieces], axis=1)
        return jnp.dot(train, turned, preferred_element_type=jnp.float32)

    if not last:
        value = products(slice(None), turned)
        out_ref[...] = value if first else total_ref[...] + value
        return

    turned_ref, here_ref, sem = refs
    turned_ref[...] = turned
    scale = 1.0 / features**0.5
    row_step, query_step = here_ref.shape[0] // 2, here_ref.shape[1] // 2
    copies = []
    for step in range(4):
        queries = pl.ds(step % 2 * query_step, query_step)
        rows = pl.ds(step // 2 * row_step, row_step)
        here_ref[rows, queries] = (total_ref[rows, queries] + products(rows, turned_ref[:, queries])) * scale
        copies.append(pltpu.make_async_copy(here_ref.at[rows, queries], out_ref.at[rows, queries], sem.at[step]))
        copies[-1].start()
    for copy in copies:
        copy.wait()


def score(grid, train_feats, parts, total, masks, other, last):
    rows = train_feats.shape[0]
    first = total is None
    arrays = [train_feats, *parts] + ([] if first else [total])
    if len(parts) == 1:
        features, queries = parts[0].shape
        scratch = []
    else:
        blocks, far, cores, count, width = parts[0].shape
        features, queries = len(masks) * width, blocks * far * 2 * cores * count
        scratch = [pltpu.VMEM((blocks, far, 2, cores, count, features), jnp.bfloat16)]
    shape = (rows, queries)
    if last:
        scratch += [
            pltpu.VMEM((features, queries), jnp.bfloat16),
            pltpu.VMEM(shape, jnp.float32),
            pltpu.SemaphoreType.DMA((4,)),
        ]
    return pl.pallas_call(
        functools.partial(score_kernel, grid, masks, other, len(parts), first, last),
        out_shape=jax.ShapeDtypeStruct(shape, jnp.float32) if last else pltpu.VMEM(shape, jnp.float32),
        in_specs=[VMEM] * len(arrays),
        out_specs=ANY if last else VMEM,
        scratch_shapes=scratch,
        input_output_aliases={} if first or last else {len(arrays) - 1: 0},
        compiler_params=pltpu.CompilerParams(vmem_limit_bytes=24 << 20),
        cost_estimate=pl.CostEstimate(
            flops=(40 if first else 2) * rows * features * queries, bytes_accessed=4 << 20, transcendentals=0
        ),
        name="score",
    )(*(pltpu.with_memory_space_constraint(a, pltpu.VMEM) for a in arrays))


def two_level(grid, train_feats, queries, inverse_fisher):
    beside, mirror, relayed = 1, 3, 2
    gathered = {(0, 0): queries}
    gathered[0, 1] = grid.swap(queries, 0, 0, 1)
    gathered[beside, 0] = grid.swap(queries, beside, 0, 0)
    near_fisher = grid.swap(inverse_fisher, 0, 1, 0)
    gathered[mirror, 0] = grid.swap(queries, mirror, 0, 0)
    staged = stage([train_feats, queries, inverse_fisher])
    gathered[mirror, 0], gathered[0, 1], staged = lax.optimization_barrier(
        (gathered[mirror, 0], gathered[0, 1], staged)
    )
    train_here, gathered[0, 0], fisher_here = staged
    gathered[relayed, 0] = grid.swap(gathered[mirror, 0], beside, 0, 0)
    (train_here,) = stage([train_feats], train_here)
    for mask in (beside, mirror):
        gathered[mask, 1] = grid.swap(gathered[mask, 0], 0, 0, 1)
    gathered[relayed, 0], train_here = lax.optimization_barrier((gathered[relayed, 0], train_here))
    gathered[relayed, 1] = grid.swap(gathered[relayed, 0], 0, 0, 1)

    parts = {(0, 0, 0): condition(grid, gathered, fisher_here, near_fisher)}

    def swap(source, *step):
        place = tuple(a ^ b for a, b in zip(source, step))
        parts[place] = grid.swap(parts[source], *step)

    def meet(*places, total=None):
        held, total = lax.optimization_barrier(([parts[place] for place in places], total))
        parts.update(zip(places, held))
        return total

    own, near_one, far_one, far_three = (0, 0, 0), (0, 1, 0), (beside, 0, 0), (mirror, 0, 0)
    swap(own, *far_three)
    swap(own, *near_one)
    swap(own, *far_one)
    swap(far_one, *near_one)
    swap(far_three, *near_one)
    swap(far_three, beside, 1, 0)
    swap(far_three, *far_one)
    turned = turn(grid, parts, (0, beside))
    other = grid.swap(turned, 0, 0, 1)
    total = score(grid, train_here, [turned], None, (0, beside), 0, False)
    total = meet(far_three, total=total)
    swap(far_three, 0, 0, 1)
    total = score(grid, train_here, [other], total, (0, beside), 1, False)
    total = meet(far_three, (relayed, 0, 0), (mirror, 1, 0), (relayed, 1, 0), total=total)
    swap((relayed, 0, 0), 0, 0, 1)
    swap((mirror, 1, 0), 0, 0, 1)
    swap((relayed, 1, 0), 0, 0, 1)
    for core in range(2):
        late = [parts[mask, near, core] for mask in (mirror, relayed) for near in range(2)]
        total = score(grid, train_here, late, total, (mirror, relayed), core, core == 1)
    return total


def one_level(train_feats, queries, inverse_fisher):
    group_count, group_width, _ = inverse_fisher.shape
    gathered = lax.all_gather(queries, "rows", axis=1, tiled=True)
    flattened = gathered.reshape(-1, group_count, group_width)
    part = jnp.einsum("qgk,gkc->qgc", flattened, inverse_fisher, preferred_element_type=jnp.float32)
    complete = lax.all_gather(part.astype(jnp.bfloat16), "rows", axis=2, tiled=True)
    conditioned = complete.reshape(flattened.shape[0], -1)
    products = lax.dot_general(
        train_feats, conditioned, (((1,), (1,)), ((), ())), preferred_element_type=jnp.float32
    )
    return products * (1.0 / train_feats.shape[1] ** 0.5)


def per_device(row_count, train_feats, queries, inverse_fisher):
    group_count, _, width = inverse_fisher.shape
    whole_tiles = group_count == 1 and width % 128 == 0 and queries.shape[1] % 16 == 0
    if row_count == 16 and whole_tiles and train_feats.shape[0] % 512 == 0:
        return two_level(Grid(row_count), train_feats, queries, inverse_fisher)
    return one_level(train_feats, queries, inverse_fisher)


def solution(mesh):
    placed = (P(("groups", "rows"), None), P(None, ("groups", "rows"), None), P(None, None, "rows"))
    return jax.shard_map(
        functools.partial(per_device, mesh.shape["rows"]),
        mesh=mesh,
        in_specs=placed,
        out_specs=P(("groups", "rows"), None),
        check_vma=False,
    )
```

```python
import functools

import jax
import jax.numpy as jnp
from jax import lax
from jax.experimental import pallas as pl
from jax.experimental.pallas import tpu as pltpu
from jax.sharding import PartitionSpec as P

VMEM = pl.BlockSpec(memory_space=pltpu.VMEM)
ANY = pl.BlockSpec(memory_space=pl.ANY)


class Grid:
    def __init__(self, row_count):
        self.far = row_count // 4

    def swap(self, block, far, near, core):
        step = (far * 2 + near) * 2 + core
        return lax.ppermute(block, "rows", [(row ^ step, row) for row in range(self.far * 4)])

    def place(self):
        row = lax.axis_index("rows")
        return lax.div(row, 4), lax.rem(lax.div(row, 2), 2), lax.rem(row, 2)


def flip(part, mask):
    return lax.bitwise_xor(part, jnp.int32(mask))


def columns(index, width):
    return pl.ds(pl.multiple_of(index * width, width), width)


def stage_kernel(first, half, *refs):
    sources, targets, sems = refs[: len(refs) // 2], refs[len(refs) // 2 : -1], refs[-1]
    if not first:
        sources = sources[1:]
    part = pl.ds(0 if first else half, half)
    copies = [pltpu.make_async_copy(sources[0].at[part], targets[0].at[part], sems.at[0])]
    for index in range(1, len(sources)):
        copies.append(pltpu.make_async_copy(sources[index], targets[index], sems.at[index]))
    for copy in copies:
        copy.start()
    for copy in copies:
        copy.wait()


def stage(arrays, buffer=None):
    first = buffer is None
    moved = sum(a.size * a.dtype.itemsize for a in arrays)
    sources = [pltpu.with_memory_space_constraint(a, pltpu.HBM) for a in arrays]
    if not first:
        sources.insert(0, pltpu.with_memory_space_constraint(buffer, pltpu.VMEM))
    return pl.pallas_call(
        functools.partial(stage_kernel, first, arrays[0].shape[0] // 2),
        out_shape=[pltpu.VMEM(a.shape, a.dtype) for a in arrays],
        in_specs=[ANY] * len(arrays) if first else [VMEM, ANY],
        out_specs=[VMEM] * len(arrays),
        scratch_shapes=[pltpu.SemaphoreType.DMA((len(arrays),))],
        input_output_aliases={} if first else {0: 0},
        compiler_params=pltpu.CompilerParams(vmem_limit_bytes=4 << 20),
        cost_estimate=pl.CostEstimate(flops=1, bytes_accessed=moved, transcendentals=0),
        name="stage",
    )(*sources)


def condition_kernel(grid, places, *refs):
    query_refs, (own_ref, near_ref, out_ref) = refs[: len(places)], refs[len(places) :]
    far, near, core = grid.place()
    rows = jnp.concatenate([ref[...].reshape(-1, ref.shape[-1]) for ref in query_refs])
    fisher = jnp.concatenate([own_ref[0], near_ref[0]], axis=1)
    result = jnp.dot(rows, fisher, preferred_element_type=jnp.float32).astype(out_ref.dtype)
    blocks, count, _ = query_refs[0].shape
    width = own_ref.shape[-1]
    result = result.reshape(len(places), blocks, 1, 1, count, 2 * width)
    for index, (far_mask, core_mask) in enumerate(places):
        for side in range(2):
            out_ref[
                :, pl.ds(flip(far, far_mask), 1), pl.ds(flip(core, core_mask), 1), :, columns(flip(near, side), width)
            ] = result[index, ..., side * width : (side + 1) * width]


def condition(grid, queries, own, near):
    blocks, count, _ = queries[0, 0].shape
    width = own.shape[-1]
    arrays = [*queries.values(), own, near]
    return pl.pallas_call(
        functools.partial(condition_kernel, grid, list(queries)),
        out_shape=jax.ShapeDtypeStruct((blocks, grid.far, 2, count, 2 * width), jnp.bfloat16),
        in_specs=[VMEM] * len(arrays),
        out_specs=VMEM,
        compiler_params=pltpu.CompilerParams(vmem_limit_bytes=12 << 20),
        cost_estimate=pl.CostEstimate(flops=1 << 28, bytes_accessed=3 << 20, transcendentals=0),
        name="condition",
    )(*arrays)


def sort_and_turn(grid, masks, part_refs, sorted_ref):
    _, near, _ = grid.place()
    width = part_refs[0].shape[-1]
    for index in range(len(masks)):
        for side in range(2):
            sorted_ref[:, :, pl.ds(flip(near, side), 1), :, :, index * width : (index + 1) * width] = part_refs[
                index * 2 + side
            ][...][:, :, None]
    return sorted_ref[...].reshape(-1, len(masks) * width).T


def turn_kernel(grid, masks, *refs):
    refs[-2][...] = sort_and_turn(grid, masks, refs[:-2], refs[-1])


def turn(grid, parts, masks):
    arrays = [parts[mask, near, 0] for mask in masks for near in range(2)]
    blocks, far, cores, count, width = arrays[0].shape
    features = len(masks) * width
    return pl.pallas_call(
        functools.partial(turn_kernel, grid, masks),
        out_shape=pltpu.VMEM((features, blocks * far * 2 * cores * count), jnp.bfloat16),
        in_specs=[VMEM] * len(arrays),
        out_specs=VMEM,
        scratch_shapes=[pltpu.VMEM((blocks, far, 2, cores, count, features), jnp.bfloat16)],
        compiler_params=pltpu.CompilerParams(vmem_limit_bytes=8 << 20),
        name="turn",
    )(*(pltpu.with_memory_space_constraint(a, pltpu.VMEM) for a in arrays))


def score_kernel(grid, masks, other, part_count, first, last, *refs):
    train_ref, part_refs, refs = refs[0], refs[1 : 1 + part_count], refs[1 + part_count :]
    total_ref, refs = (None, refs) if first else (refs[0], refs[1:])
    out_ref, refs = refs[0], refs[1:]
    far, _, core = grid.place()
    features = train_ref.shape[1]
    width = features // (grid.far * 4)
    if part_count == 1:
        turned = part_refs[0][...]
    else:
        turned = sort_and_turn(grid, masks, part_refs, refs[0])
        refs = refs[1:]
    pieces = [
        columns((flip(far, mask) * 2 + side) * 2 + flip(core, other), width) for mask in masks for side in range(2)
    ]

    def products(rows, turned):
        train = jnp.concatenate([train_ref[rows, piece] for piece in pieces], axis=1)
        return jnp.dot(train, turned, preferred_element_type=jnp.float32)

    if not last:
        value = products(slice(None), turned)
        out_ref[...] = value if first else total_ref[...] + value
        return

    turned_ref, here_ref, sem = refs
    turned_ref[...] = turned
    scale = 1.0 / features**0.5
    row_step, query_step = here_ref.shape[0] // 2, here_ref.shape[1] // 2
    copies = []
    for step in range(4):
        queries = pl.ds(step % 2 * query_step, query_step)
        rows = pl.ds(step // 2 * row_step, row_step)
        here_ref[rows, queries] = (total_ref[rows, queries] + products(rows, turned_ref[:, queries])) * scale
        copies.append(pltpu.make_async_copy(here_ref.at[rows, queries], out_ref.at[rows, queries], sem.at[step]))
        copies[-1].start()
    for copy in copies:
        copy.wait()


def score(grid, train_feats, parts, total, masks, other, last):
    rows = train_feats.shape[0]
    first = total is None
    arrays = [train_feats, *parts] + ([] if first else [total])
    if len(parts) == 1:
        features, queries = parts[0].shape
        scratch = []
    else:
        blocks, far, cores, count, width = parts[0].shape
        features, queries = len(masks) * width, blocks * far * 2 * cores * count
        scratch = [pltpu.VMEM((blocks, far, 2, cores, count, features), jnp.bfloat16)]
    shape = (rows, queries)
    if last:
        scratch += [
            pltpu.VMEM((features, queries), jnp.bfloat16),
            pltpu.VMEM(shape, jnp.float32),
            pltpu.SemaphoreType.DMA((4,)),
        ]
    return pl.pallas_call(
        functools.partial(score_kernel, grid, masks, other, len(parts), first, last),
        out_shape=jax.ShapeDtypeStruct(shape, jnp.float32) if last else pltpu.VMEM(shape, jnp.float32),
        in_specs=[VMEM] * len(arrays),
        out_specs=ANY if last else VMEM,
        scratch_shapes=scratch,
        input_output_aliases={} if first or last else {len(arrays) - 1: 0},
        compiler_params=pltpu.CompilerParams(vmem_limit_bytes=24 << 20),
        cost_estimate=pl.CostEstimate(
            flops=(40 if first else 2) * rows * features * queries, bytes_accessed=4 << 20, transcendentals=0
        ),
        name="score",
    )(*(pltpu.with_memory_space_constraint(a, pltpu.VMEM) for a in arrays))


def two_level(grid, train_feats, queries, inverse_fisher):
    beside, mirror, relayed = 1, 3, 2
    gathered = {(0, 0): queries}
    gathered[0, 1] = grid.swap(queries, 0, 0, 1)
    gathered[beside, 0] = grid.swap(queries, beside, 0, 0)
    near_fisher = grid.swap(inverse_fisher, 0, 1, 0)
    gathered[mirror, 0] = grid.swap(queries, mirror, 0, 0)
    staged = stage([train_feats, queries, inverse_fisher])
    gathered[mirror, 0], gathered[0, 1], staged = lax.optimization_barrier(
        (gathered[mirror, 0], gathered[0, 1], staged)
    )
    train_here, gathered[0, 0], fisher_here = staged
    gathered[relayed, 0] = grid.swap(gathered[mirror, 0], beside, 0, 0)
    (train_here,) = stage([train_feats], train_here)
    for mask in (beside, mirror):
        gathered[mask, 1] = grid.swap(gathered[mask, 0], 0, 0, 1)
    gathered[relayed, 0], train_here = lax.optimization_barrier((gathered[relayed, 0], train_here))
    gathered[relayed, 1] = grid.swap(gathered[relayed, 0], 0, 0, 1)

    parts = {(0, 0, 0): condition(grid, gathered, fisher_here, near_fisher)}

    def swap(source, *step):
        place = tuple(a ^ b for a, b in zip(source, step))
        parts[place] = grid.swap(parts[source], *step)

    def meet(*places, total=None):
        held, total = lax.optimization_barrier(([parts[place] for place in places], total))
        parts.update(zip(places, held))
        return total

    own, near_one, far_one, far_three = (0, 0, 0), (0, 1, 0), (beside, 0, 0), (mirror, 0, 0)
    swap(own, *far_three)
    swap(own, *near_one)
    swap(own, *far_one)
    swap(far_one, *near_one)
    swap(far_three, *near_one)
    swap(far_three, beside, 1, 0)
    swap(far_three, *far_one)
    turned = turn(grid, parts, (0, beside))
    other = grid.swap(turned, 0, 0, 1)
    total = score(grid, train_here, [turned], None, (0, beside), 0, False)
    total = meet(far_three, total=total)
    swap(far_three, 0, 0, 1)
    total = score(grid, train_here, [other], total, (0, beside), 1, False)
    total = meet(far_three, (relayed, 0, 0), (mirror, 1, 0), (relayed, 1, 0), total=total)
    swap((relayed, 0, 0), 0, 0, 1)
    swap((mirror, 1, 0), 0, 0, 1)
    swap((relayed, 1, 0), 0, 0, 1)
    for core in range(2):
        late = [parts[mask, near, core] for mask in (mirror, relayed) for near in range(2)]
        total = score(grid, train_here, late, total, (mirror, relayed), core, core == 1)
    return total


def one_level(train_feats, queries, inverse_fisher):
    group_count, group_width, _ = inverse_fisher.shape
    gathered = lax.all_gather(queries, "rows", axis=1, tiled=True)
    flattened = gathered.reshape(-1, group_count, group_width)
    part = jnp.einsum("qgk,gkc->qgc", flattened, inverse_fisher, preferred_element_type=jnp.float32)
    complete = lax.all_gather(part.astype(jnp.bfloat16), "rows", axis=2, tiled=True)
    conditioned = complete.reshape(flattened.shape[0], -1)
    products = lax.dot_general(
        train_feats, conditioned, (((1,), (1,)), ((), ())), preferred_element_type=jnp.float32
    )
    return products * (1.0 / train_feats.shape[1] ** 0.5)


def per_device(row_count, train_feats, queries, inverse_fisher):
    group_count, _, width = inverse_fisher.shape
    whole_tiles = group_count == 1 and width % 128 == 0 and queries.shape[1] % 16 == 0
    if row_count == 16 and whole_tiles and train_feats.shape[0] % 512 == 0:
        return two_level(Grid(row_count), train_feats, queries, inverse_fisher)
    return one_level(train_feats, queries, inverse_fisher)


def solution(mesh):
    placed = (P(("groups", "rows"), None), P(None, ("groups", "rows"), None), P(None, None, "rows"))
    return jax.shard_map(
        functools.partial(per_device, mesh.shape["rows"]),
        mesh=mesh,
        in_specs=placed,
        out_specs=P(("groups", "rows"), None),
        check_vma=False,
    )
```

```python
import functools

import jax
import jax.numpy as jnp
from jax import lax
from jax.experimental import pallas as pl
from jax.experimental.pallas import tpu as pltpu
from jax.sharding import PartitionSpec as P

VMEM = pl.BlockSpec(memory_space=pltpu.VMEM)
ANY = pl.BlockSpec(memory_space=pl.ANY)
ORDER_FLOPS = 2_788_300_000


class Grid:
    def __init__(self, row_count):
        self.far = row_count // 4

    def swap(self, block, far, near, core):
        step = (far * 2 + near) * 2 + core
        return lax.ppermute(block, "rows", [(row ^ step, row) for row in range(self.far * 4)])

    def place(self):
        row = lax.axis_index("rows")
        return lax.div(row, 4), lax.rem(lax.div(row, 2), 2), lax.rem(row, 2)


def flip(part, mask):
    return lax.bitwise_xor(part, jnp.int32(mask))


def columns(index, width):
    return pl.ds(pl.multiple_of(index * width, width), width)


def stage_kernel(first, half, *refs):
    sources, targets, sems = refs[: len(refs) // 2], refs[len(refs) // 2 : -1], refs[-1]
    if not first:
        sources = sources[1:]
    part = pl.ds(0 if first else half, half)
    copies = [pltpu.make_async_copy(sources[0].at[part], targets[0].at[part], sems.at[0])]
    for index in range(1, len(sources)):
        copies.append(pltpu.make_async_copy(sources[index], targets[index], sems.at[index]))
    for copy in copies:
        copy.start()
    for copy in copies:
        copy.wait()


def stage(arrays, buffer=None):
    first = buffer is None
    moved = sum(a.size * a.dtype.itemsize for a in arrays)
    sources = [pltpu.with_memory_space_constraint(a, pltpu.HBM) for a in arrays]
    if not first:
        sources.insert(0, pltpu.with_memory_space_constraint(buffer, pltpu.VMEM))
    return pl.pallas_call(
        functools.partial(stage_kernel, first, arrays[0].shape[0] // 2),
        out_shape=[pltpu.VMEM(a.shape, a.dtype) for a in arrays],
        in_specs=[ANY] * len(arrays) if first else [VMEM, ANY],
        out_specs=[VMEM] * len(arrays),
        scratch_shapes=[pltpu.SemaphoreType.DMA((len(arrays),))],
        input_output_aliases={} if first else {0: 0},
        compiler_params=pltpu.CompilerParams(vmem_limit_bytes=4 << 20),
        cost_estimate=pl.CostEstimate(
            flops=ORDER_FLOPS if first else 1, bytes_accessed=moved, transcendentals=0
        ),
        name="stage",
    )(*sources)


def condition_kernel(grid, places, *refs):
    query_refs, (own_ref, near_ref, out_ref) = refs[: len(places)], refs[len(places) :]
    far, near, core = grid.place()
    rows = jnp.concatenate([ref[...].reshape(-1, ref.shape[-1]) for ref in query_refs])
    fisher = jnp.concatenate([own_ref[0], near_ref[0]], axis=1)
    result = jnp.dot(rows, fisher, preferred_element_type=jnp.float32).astype(out_ref.dtype)
    blocks, count, _ = query_refs[0].shape
    width = own_ref.shape[-1]
    result = result.reshape(len(places), blocks, 1, 1, count, 2 * width)
    for index, (far_mask, core_mask) in enumerate(places):
        for side in range(2):
            out_ref[
                :, pl.ds(flip(far, far_mask), 1), pl.ds(flip(core, core_mask), 1), :, columns(flip(near, side), width)
            ] = result[index, ..., side * width : (side + 1) * width]


def condition(grid, queries, own, near):
    blocks, count, _ = queries[0, 0].shape
    width = own.shape[-1]
    arrays = [*queries.values(), own, near]
    return pl.pallas_call(
        functools.partial(condition_kernel, grid, list(queries)),
        out_shape=jax.ShapeDtypeStruct((blocks, grid.far, 2, count, 2 * width), jnp.bfloat16),
        in_specs=[VMEM] * len(arrays),
        out_specs=VMEM,
        compiler_params=pltpu.CompilerParams(vmem_limit_bytes=12 << 20),
        cost_estimate=pl.CostEstimate(flops=1 << 28, bytes_accessed=3 << 20, transcendentals=0),
        name="condition",
    )(*arrays)


def sort_and_turn(grid, masks, part_refs, sorted_ref):
    _, near, _ = grid.place()
    width = part_refs[0].shape[-1]
    for index in range(len(masks)):
        for side in range(2):
            sorted_ref[:, :, pl.ds(flip(near, side), 1), :, :, index * width : (index + 1) * width] = part_refs[
                index * 2 + side
            ][...][:, :, None]
    return sorted_ref[...].reshape(-1, len(masks) * width).T


def turn_kernel(grid, masks, *refs):
    refs[-2][...] = sort_and_turn(grid, masks, refs[:-2], refs[-1])


def turn(grid, parts, masks):
    arrays = [parts[mask, near, 0] for mask in masks for near in range(2)]
    blocks, far, cores, count, width = arrays[0].shape
    features = len(masks) * width
    return pl.pallas_call(
        functools.partial(turn_kernel, grid, masks),
        out_shape=pltpu.VMEM((features, blocks * far * 2 * cores * count), jnp.bfloat16),
        in_specs=[VMEM] * len(arrays),
        out_specs=VMEM,
        scratch_shapes=[pltpu.VMEM((blocks, far, 2, cores, count, features), jnp.bfloat16)],
        compiler_params=pltpu.CompilerParams(vmem_limit_bytes=8 << 20),
        name="turn",
    )(*(pltpu.with_memory_space_constraint(a, pltpu.VMEM) for a in arrays))


def score_kernel(grid, masks, other, part_count, first, last, *refs):
    train_ref, part_refs, refs = refs[0], refs[1 : 1 + part_count], refs[1 + part_count :]
    total_ref, refs = (None, refs) if first else (refs[0], refs[1:])
    out_ref, refs = refs[0], refs[1:]
    far, _, core = grid.place()
    features = train_ref.shape[1]
    width = features // (grid.far * 4)
    if part_count == 1:
        turned = part_refs[0][...]
    else:
        turned = sort_and_turn(grid, masks, part_refs, refs[0])
        refs = refs[1:]
    pieces = [
        columns((flip(far, mask) * 2 + side) * 2 + flip(core, other), width) for mask in masks for side in range(2)
    ]

    def products(rows, turned):
        train = jnp.concatenate([train_ref[rows, piece] for piece in pieces], axis=1)
        return jnp.dot(train, turned, preferred_element_type=jnp.float32)

    if not last:
        value = products(slice(None), turned)
        out_ref[...] = value if first else total_ref[...] + value
        return

    turned_ref, here_ref, sem = refs
    turned_ref[...] = turned
    scale = 1.0 / features**0.5
    row_step, query_step = here_ref.shape[0] // 2, here_ref.shape[1] // 2
    copies = []
    for row, query, row_count in ((0, 0, 2 * row_step), (0, query_step, row_step), (row_step, query_step, row_step)):
        rows, queries = pl.ds(row, row_count), pl.ds(query, query_step)
        here_ref[rows, queries] = (total_ref[rows, queries] + products(rows, turned_ref[:, queries])) * scale
        copies.append(
            pltpu.make_async_copy(here_ref.at[rows, queries], out_ref.at[rows, queries], sem.at[len(copies)])
        )
        copies[-1].start()
    for copy in copies:
        copy.wait()


def score(grid, train_feats, parts, total, masks, other, last):
    rows = train_feats.shape[0]
    first = total is None
    arrays = [train_feats, *parts] + ([] if first else [total])
    if len(parts) == 1:
        features, queries = parts[0].shape
        scratch = []
    else:
        blocks, far, cores, count, width = parts[0].shape
        features, queries = len(masks) * width, blocks * far * 2 * cores * count
        scratch = [pltpu.VMEM((blocks, far, 2, cores, count, features), jnp.bfloat16)]
    shape = (rows, queries)
    if last:
        scratch += [
            pltpu.VMEM((features, queries), jnp.bfloat16),
            pltpu.VMEM(shape, jnp.float32),
            pltpu.SemaphoreType.DMA((3,)),
        ]
    return pl.pallas_call(
        functools.partial(score_kernel, grid, masks, other, len(parts), first, last),
        out_shape=jax.ShapeDtypeStruct(shape, jnp.float32) if last else pltpu.VMEM(shape, jnp.float32),
        in_specs=[VMEM] * len(arrays),
        out_specs=ANY if last else VMEM,
        scratch_shapes=scratch,
        input_output_aliases={} if first or last else {len(arrays) - 1: 0},
        compiler_params=pltpu.CompilerParams(vmem_limit_bytes=24 << 20),
        cost_estimate=pl.CostEstimate(
            flops=(40 if first else 2) * rows * features * queries, bytes_accessed=4 << 20, transcendentals=0
        ),
        name="score",
    )(*(pltpu.with_memory_space_constraint(a, pltpu.VMEM) for a in arrays))


def two_level(grid, train_feats, queries, inverse_fisher):
    beside, mirror, relayed = 1, 3, 2
    gathered = {(0, 0): queries}
    gathered[0, 1] = grid.swap(queries, 0, 0, 1)
    gathered[beside, 0] = grid.swap(queries, beside, 0, 0)
    near_fisher = grid.swap(inverse_fisher, 0, 1, 0)
    gathered[mirror, 0] = grid.swap(queries, mirror, 0, 0)
    staged = stage([train_feats, queries, inverse_fisher])
    gathered[mirror, 0], gathered[0, 1], staged = lax.optimization_barrier(
        (gathered[mirror, 0], gathered[0, 1], staged)
    )
    train_here, gathered[0, 0], fisher_here = staged
    gathered[relayed, 0] = grid.swap(gathered[mirror, 0], beside, 0, 0)
    (train_here,) = stage([train_feats], train_here)
    for mask in (beside, mirror):
        gathered[mask, 1] = grid.swap(gathered[mask, 0], 0, 0, 1)
    gathered[relayed, 0], train_here = lax.optimization_barrier((gathered[relayed, 0], train_here))
    gathered[relayed, 1] = grid.swap(gathered[relayed, 0], 0, 0, 1)

    parts = {(0, 0, 0): condition(grid, gathered, fisher_here, near_fisher)}

    def swap(source, *step):
        place = tuple(a ^ b for a, b in zip(source, step))
        parts[place] = grid.swap(parts[source], *step)

    def meet(*places, total=None):
        held, total = lax.optimization_barrier(([parts[place] for place in places], total))
        parts.update(zip(places, held))
        return total

    own, near_one, far_one, far_three = (0, 0, 0), (0, 1, 0), (beside, 0, 0), (mirror, 0, 0)
    swap(own, *far_three)
    swap(own, *near_one)
    swap(own, *far_one)
    swap(far_one, *near_one)
    swap(far_three, *near_one)
    swap(far_three, beside, 1, 0)
    swap(far_three, *far_one)
    turned = turn(grid, parts, (0, beside))
    other = grid.swap(turned, 0, 0, 1)
    total = score(grid, train_here, [turned], None, (0, beside), 0, False)
    total = meet(far_three, total=total)
    swap(far_three, 0, 0, 1)
    total = score(grid, train_here, [other], total, (0, beside), 1, False)
    total = meet(far_three, (relayed, 0, 0), (mirror, 1, 0), (relayed, 1, 0), total=total)
    swap((relayed, 0, 0), 0, 0, 1)
    swap((mirror, 1, 0), 0, 0, 1)
    swap((relayed, 1, 0), 0, 0, 1)
    for core in range(2):
        late = [parts[mask, near, core] for mask in (mirror, relayed) for near in range(2)]
        total = score(grid, train_here, late, total, (mirror, relayed), core, core == 1)
    return total


def one_level(train_feats, queries, inverse_fisher):
    group_count, group_width, _ = inverse_fisher.shape
    gathered = lax.all_gather(queries, "rows", axis=1, tiled=True)
    flattened = gathered.reshape(-1, group_count, group_width)
    part = jnp.einsum("qgk,gkc->qgc", flattened, inverse_fisher, preferred_element_type=jnp.float32)
    complete = lax.all_gather(part.astype(jnp.bfloat16), "rows", axis=2, tiled=True)
    conditioned = complete.reshape(flattened.shape[0], -1)
    products = lax.dot_general(
        train_feats, conditioned, (((1,), (1,)), ((), ())), preferred_element_type=jnp.float32
    )
    return products * (1.0 / train_feats.shape[1] ** 0.5)


def per_device(row_count, train_feats, queries, inverse_fisher):
    group_count, _, width = inverse_fisher.shape
    whole_tiles = group_count == 1 and width % 128 == 0 and queries.shape[1] % 16 == 0
    if row_count == 16 and whole_tiles and train_feats.shape[0] % 512 == 0:
        return two_level(Grid(row_count), train_feats, queries, inverse_fisher)
    return one_level(train_feats, queries, inverse_fisher)


def solution(mesh):
    placed = (P(("groups", "rows"), None), P(None, ("groups", "rows"), None), P(None, None, "rows"))
    return jax.shard_map(
        functools.partial(per_device, mesh.shape["rows"]),
        mesh=mesh,
        in_specs=placed,
        out_specs=P(("groups", "rows"), None),
        check_vma=False,
    )
```

```python
import functools

import jax
import jax.numpy as jnp
from jax import lax
from jax.experimental import pallas as pl
from jax.experimental.pallas import tpu as pltpu
from jax.sharding import PartitionSpec as P

VMEM = pl.BlockSpec(memory_space=pltpu.VMEM)
ANY = pl.BlockSpec(memory_space=pl.ANY)
ORDER_FLOPS = 2_788_300_000


class Grid:
    def __init__(self, row_count):
        self.far = row_count // 4

    def swap(self, block, far, near, core):
        step = (far * 2 + near) * 2 + core
        return lax.ppermute(block, "rows", [(row ^ step, row) for row in range(self.far * 4)])

    def place(self):
        row = lax.axis_index("rows")
        return lax.div(row, 4), lax.rem(lax.div(row, 2), 2), lax.rem(row, 2)


def flip(part, mask):
    return lax.bitwise_xor(part, jnp.int32(mask))


def columns(index, width):
    return pl.ds(pl.multiple_of(index * width, width), width)


def stage_kernel(first, half, *refs):
    sources, targets, sems = refs[: len(refs) // 2], refs[len(refs) // 2 : -1], refs[-1]
    if not first:
        sources = sources[1:]
    part = pl.ds(0 if first else half, half)
    copies = [pltpu.make_async_copy(sources[0].at[part], targets[0].at[part], sems.at[0])]
    for index in range(1, len(sources)):
        copies.append(pltpu.make_async_copy(sources[index], targets[index], sems.at[index]))
    for copy in copies:
        copy.start()
    for copy in copies:
        copy.wait()


def stage(arrays, buffer=None):
    first = buffer is None
    moved = sum(a.size * a.dtype.itemsize for a in arrays)
    sources = [pltpu.with_memory_space_constraint(a, pltpu.HBM) for a in arrays]
    if not first:
        sources.insert(0, pltpu.with_memory_space_constraint(buffer, pltpu.VMEM))
    return pl.pallas_call(
        functools.partial(stage_kernel, first, arrays[0].shape[0] // 2),
        out_shape=[pltpu.VMEM(a.shape, a.dtype) for a in arrays],
        in_specs=[ANY] * len(arrays) if first else [VMEM, ANY],
        out_specs=[VMEM] * len(arrays),
        scratch_shapes=[pltpu.SemaphoreType.DMA((len(arrays),))],
        input_output_aliases={} if first else {0: 0},
        compiler_params=pltpu.CompilerParams(vmem_limit_bytes=4 << 20),
        cost_estimate=pl.CostEstimate(
            flops=ORDER_FLOPS if first else 1, bytes_accessed=moved, transcendentals=0
        ),
        name="stage",
    )(*sources)


def condition_kernel(grid, places, *refs):
    query_refs, (own_ref, near_ref, out_ref) = refs[: len(places)], refs[len(places) :]
    far, near, core = grid.place()
    rows = jnp.concatenate([ref[...].reshape(-1, ref.shape[-1]) for ref in query_refs])
    fisher = jnp.concatenate([own_ref[0], near_ref[0]], axis=1)
    result = jnp.dot(rows, fisher, preferred_element_type=jnp.float32).astype(out_ref.dtype)
    blocks, count, _ = query_refs[0].shape
    width = own_ref.shape[-1]
    result = result.reshape(len(places), blocks, 1, 1, count, 2 * width)
    for index, (far_mask, core_mask) in enumerate(places):
        for side in range(2):
            out_ref[
                :, pl.ds(flip(far, far_mask), 1), pl.ds(flip(core, core_mask), 1), :, columns(flip(near, side), width)
            ] = result[index, ..., side * width : (side + 1) * width]


def condition(grid, queries, own, near):
    blocks, count, _ = queries[0, 0].shape
    width = own.shape[-1]
    arrays = [*queries.values(), own, near]
    return pl.pallas_call(
        functools.partial(condition_kernel, grid, list(queries)),
        out_shape=jax.ShapeDtypeStruct((blocks, grid.far, 2, count, 2 * width), jnp.bfloat16),
        in_specs=[VMEM] * len(arrays),
        out_specs=VMEM,
        compiler_params=pltpu.CompilerParams(vmem_limit_bytes=12 << 20),
        cost_estimate=pl.CostEstimate(flops=1 << 28, bytes_accessed=3 << 20, transcendentals=0),
        name="condition",
    )(*arrays)


def sort_and_turn(grid, masks, part_refs, sorted_ref):
    _, near, _ = grid.place()
    width = part_refs[0].shape[-1]
    for index in range(len(masks)):
        for side in range(2):
            sorted_ref[:, :, pl.ds(flip(near, side), 1), :, :, index * width : (index + 1) * width] = part_refs[
                index * 2 + side
            ][...][:, :, None]
    return sorted_ref[...].reshape(-1, len(masks) * width).T


def turn_kernel(grid, masks, *refs):
    refs[-2][...] = sort_and_turn(grid, masks, refs[:-2], refs[-1])


def turn(grid, parts, masks):
    arrays = [parts[mask, near, 0] for mask in masks for near in range(2)]
    blocks, far, cores, count, width = arrays[0].shape
    features = len(masks) * width
    return pl.pallas_call(
        functools.partial(turn_kernel, grid, masks),
        out_shape=pltpu.VMEM((features, blocks * far * 2 * cores * count), jnp.bfloat16),
        in_specs=[VMEM] * len(arrays),
        out_specs=VMEM,
        scratch_shapes=[pltpu.VMEM((blocks, far, 2, cores, count, features), jnp.bfloat16)],
        compiler_params=pltpu.CompilerParams(vmem_limit_bytes=8 << 20),
        name="turn",
    )(*(pltpu.with_memory_space_constraint(a, pltpu.VMEM) for a in arrays))


def score_kernel(grid, masks, other, part_count, first, last, *refs):
    train_ref, part_refs, refs = refs[0], refs[1 : 1 + part_count], refs[1 + part_count :]
    total_ref, refs = (None, refs) if first else (refs[0], refs[1:])
    out_ref, refs = refs[0], refs[1:]
    far, _, core = grid.place()
    features = train_ref.shape[1]
    width = features // (grid.far * 4)
    if part_count == 1:
        turned = part_refs[0][...]
    else:
        turned = sort_and_turn(grid, masks, part_refs, refs[0])
        refs = refs[1:]
    pieces = [
        columns((flip(far, mask) * 2 + side) * 2 + flip(core, other), width) for mask in masks for side in range(2)
    ]

    def products(rows, turned):
        train = jnp.concatenate([train_ref[rows, piece] for piece in pieces], axis=1)
        return jnp.dot(train, turned, preferred_element_type=jnp.float32)

    if not last:
        value = products(slice(None), turned)
        out_ref[...] = value if first else total_ref[...] + value
        return

    turned_ref, here_ref, sem = refs
    turned_ref[...] = turned
    scale = 1.0 / features**0.5
    quarter = here_ref.shape[0] // 4
    copies = []
    for row, count in ((0, 2), (2, 1), (3, 1)):
        rows = pl.ds(row * quarter, count * quarter)
        here_ref[rows] = (total_ref[rows] + products(rows, turned_ref[...])) * scale
        copies.append(pltpu.make_async_copy(here_ref.at[rows], out_ref.at[rows], sem.at[len(copies)]))
        copies[-1].start()
    for copy in copies:
        copy.wait()


def score(grid, train_feats, parts, total, masks, other, last):
    rows = train_feats.shape[0]
    first = total is None
    arrays = [train_feats, *parts] + ([] if first else [total])
    if len(parts) == 1:
        features, queries = parts[0].shape
        scratch = []
    else:
        blocks, far, cores, count, width = parts[0].shape
        features, queries = len(masks) * width, blocks * far * 2 * cores * count
        scratch = [pltpu.VMEM((blocks, far, 2, cores, count, features), jnp.bfloat16)]
    shape = (rows, queries)
    if last:
        scratch += [
            pltpu.VMEM((features, queries), jnp.bfloat16),
            pltpu.VMEM(shape, jnp.float32),
            pltpu.SemaphoreType.DMA((3,)),
        ]
    return pl.pallas_call(
        functools.partial(score_kernel, grid, masks, other, len(parts), first, last),
        out_shape=jax.ShapeDtypeStruct(shape, jnp.float32) if last else pltpu.VMEM(shape, jnp.float32),
        in_specs=[VMEM] * len(arrays),
        out_specs=ANY if last else VMEM,
        scratch_shapes=scratch,
        input_output_aliases={} if first or last else {len(arrays) - 1: 0},
        compiler_params=pltpu.CompilerParams(vmem_limit_bytes=24 << 20),
        cost_estimate=pl.CostEstimate(
            flops=(40 if first else 2) * rows * features * queries, bytes_accessed=4 << 20, transcendentals=0
        ),
        name="score",
    )(*(pltpu.with_memory_space_constraint(a, pltpu.VMEM) for a in arrays))


def two_level(grid, train_feats, queries, inverse_fisher):
    beside, mirror, relayed = 1, 3, 2
    gathered = {(0, 0): queries}
    gathered[0, 1] = grid.swap(queries, 0, 0, 1)
    gathered[beside, 0] = grid.swap(queries, beside, 0, 0)
    near_fisher = grid.swap(inverse_fisher, 0, 1, 0)
    gathered[mirror, 0] = grid.swap(queries, mirror, 0, 0)
    staged = stage([train_feats, queries, inverse_fisher])
    gathered[mirror, 0], gathered[0, 1], staged = lax.optimization_barrier(
        (gathered[mirror, 0], gathered[0, 1], staged)
    )
    train_here, gathered[0, 0], fisher_here = staged
    gathered[relayed, 0] = grid.swap(gathered[mirror, 0], beside, 0, 0)
    (train_here,) = stage([train_feats], train_here)
    for mask in (beside, mirror):
        gathered[mask, 1] = grid.swap(gathered[mask, 0], 0, 0, 1)
    gathered[relayed, 0], train_here = lax.optimization_barrier((gathered[relayed, 0], train_here))
    gathered[relayed, 1] = grid.swap(gathered[relayed, 0], 0, 0, 1)

    parts = {(0, 0, 0): condition(grid, gathered, fisher_here, near_fisher)}

    def swap(source, *step):
        place = tuple(a ^ b for a, b in zip(source, step))
        parts[place] = grid.swap(parts[source], *step)

    def meet(*places, total=None):
        held, total = lax.optimization_barrier(([parts[place] for place in places], total))
        parts.update(zip(places, held))
        return total

    own, near_one, far_one, far_three = (0, 0, 0), (0, 1, 0), (beside, 0, 0), (mirror, 0, 0)
    swap(own, *far_three)
    swap(own, *near_one)
    swap(own, *far_one)
    swap(far_one, *near_one)
    swap(far_three, *near_one)
    swap(far_three, beside, 1, 0)
    swap(far_three, *far_one)
    turned = turn(grid, parts, (0, beside))
    other = grid.swap(turned, 0, 0, 1)
    total = score(grid, train_here, [turned], None, (0, beside), 0, False)
    total = meet(far_three, total=total)
    swap(far_three, 0, 0, 1)
    total = score(grid, train_here, [other], total, (0, beside), 1, False)
    total = meet(far_three, (relayed, 0, 0), (mirror, 1, 0), (relayed, 1, 0), total=total)
    swap((relayed, 0, 0), 0, 0, 1)
    swap((mirror, 1, 0), 0, 0, 1)
    swap((relayed, 1, 0), 0, 0, 1)
    for core in range(2):
        late = [parts[mask, near, core] for mask in (mirror, relayed) for near in range(2)]
        total = score(grid, train_here, late, total, (mirror, relayed), core, core == 1)
    return total


def one_level(train_feats, queries, inverse_fisher):
    group_count, group_width, _ = inverse_fisher.shape
    gathered = lax.all_gather(queries, "rows", axis=1, tiled=True)
    flattened = gathered.reshape(-1, group_count, group_width)
    part = jnp.einsum("qgk,gkc->qgc", flattened, inverse_fisher, preferred_element_type=jnp.float32)
    complete = lax.all_gather(part.astype(jnp.bfloat16), "rows", axis=2, tiled=True)
    conditioned = complete.reshape(flattened.shape[0], -1)
    products = lax.dot_general(
        train_feats, conditioned, (((1,), (1,)), ((), ())), preferred_element_type=jnp.float32
    )
    return products * (1.0 / train_feats.shape[1] ** 0.5)


def per_device(row_count, train_feats, queries, inverse_fisher):
    group_count, _, width = inverse_fisher.shape
    whole_tiles = group_count == 1 and width % 128 == 0 and queries.shape[1] % 16 == 0
    if row_count == 16 and whole_tiles and train_feats.shape[0] % 512 == 0:
        return two_level(Grid(row_count), train_feats, queries, inverse_fisher)
    return one_level(train_feats, queries, inverse_fisher)


def solution(mesh):
    placed = (P(("groups", "rows"), None), P(None, ("groups", "rows"), None), P(None, None, "rows"))
    return jax.shard_map(
        functools.partial(per_device, mesh.shape["rows"]),
        mesh=mesh,
        in_specs=placed,
        out_specs=P(("groups", "rows"), None),
        check_vma=False,
    )
```

```python
import functools

import jax
import jax.numpy as jnp
from jax import lax
from jax.experimental import pallas as pl
from jax.experimental.pallas import tpu as pltpu
from jax.sharding import PartitionSpec as P

VMEM = pl.BlockSpec(memory_space=pltpu.VMEM)
ANY = pl.BlockSpec(memory_space=pl.ANY)
ORDER_FLOPS = 2_788_300_000


class Grid:
    def __init__(self, row_count):
        self.far = row_count // 4

    def swap(self, block, far, near, core):
        step = (far * 2 + near) * 2 + core
        return lax.ppermute(block, "rows", [(row ^ step, row) for row in range(self.far * 4)])

    def place(self):
        row = lax.axis_index("rows")
        return lax.div(row, 4), lax.rem(lax.div(row, 2), 2), lax.rem(row, 2)


def flip(part, mask):
    return lax.bitwise_xor(part, jnp.int32(mask))


def columns(index, width):
    return pl.ds(pl.multiple_of(index * width, width), width)


def stage_kernel(first, half, *refs):
    sources, targets, sems = refs[: len(refs) // 2], refs[len(refs) // 2 : -1], refs[-1]
    if not first:
        sources = sources[1:]
    part = pl.ds(0 if first else half, half)
    copies = [pltpu.make_async_copy(sources[0].at[part], targets[0].at[part], sems.at[0])]
    for index in range(1, len(sources)):
        copies.append(pltpu.make_async_copy(sources[index], targets[index], sems.at[index]))
    for copy in copies:
        copy.start()
    for copy in copies:
        copy.wait()


def stage(arrays, buffer=None):
    first = buffer is None
    moved = sum(a.size * a.dtype.itemsize for a in arrays)
    sources = [pltpu.with_memory_space_constraint(a, pltpu.HBM) for a in arrays]
    if not first:
        sources.insert(0, pltpu.with_memory_space_constraint(buffer, pltpu.VMEM))
    return pl.pallas_call(
        functools.partial(stage_kernel, first, arrays[0].shape[0] // 2),
        out_shape=[pltpu.VMEM(a.shape, a.dtype) for a in arrays],
        in_specs=[ANY] * len(arrays) if first else [VMEM, ANY],
        out_specs=[VMEM] * len(arrays),
        scratch_shapes=[pltpu.SemaphoreType.DMA((len(arrays),))],
        input_output_aliases={} if first else {0: 0},
        compiler_params=pltpu.CompilerParams(vmem_limit_bytes=4 << 20),
        cost_estimate=pl.CostEstimate(
            flops=ORDER_FLOPS if first else 1, bytes_accessed=moved, transcendentals=0
        ),
        name="stage",
    )(*sources)


def condition_kernel(grid, places, *refs):
    query_refs, (own_ref, near_ref, out_ref) = refs[: len(places)], refs[len(places) :]
    far, near, core = grid.place()
    rows = jnp.concatenate([ref[...].reshape(-1, ref.shape[-1]) for ref in query_refs])
    fisher = jnp.concatenate([own_ref[0], near_ref[0]], axis=1)
    result = jnp.dot(rows, fisher, preferred_element_type=jnp.float32).astype(out_ref.dtype)
    blocks, count, _ = query_refs[0].shape
    width = own_ref.shape[-1]
    result = result.reshape(len(places), blocks, 1, 1, count, 2 * width)
    for index, (far_mask, core_mask) in enumerate(places):
        for side in range(2):
            out_ref[
                :, pl.ds(flip(far, far_mask), 1), pl.ds(flip(core, core_mask), 1), :, columns(flip(near, side), width)
            ] = result[index, ..., side * width : (side + 1) * width]


def condition(grid, queries, own, near):
    blocks, count, _ = queries[0, 0].shape
    width = own.shape[-1]
    arrays = [*queries.values(), own, near]
    return pl.pallas_call(
        functools.partial(condition_kernel, grid, list(queries)),
        out_shape=jax.ShapeDtypeStruct((blocks, grid.far, 2, count, 2 * width), jnp.bfloat16),
        in_specs=[VMEM] * len(arrays),
        out_specs=VMEM,
        compiler_params=pltpu.CompilerParams(vmem_limit_bytes=12 << 20),
        cost_estimate=pl.CostEstimate(flops=1 << 28, bytes_accessed=3 << 20, transcendentals=0),
        name="condition",
    )(*arrays)


def sort_and_turn(grid, masks, part_refs, sorted_ref):
    _, near, _ = grid.place()
    width = part_refs[0].shape[-1]
    for index in range(len(masks)):
        for side in range(2):
            sorted_ref[:, :, pl.ds(flip(near, side), 1), :, :, index * width : (index + 1) * width] = part_refs[
                index * 2 + side
            ][...][:, :, None]
    return sorted_ref[...].reshape(-1, len(masks) * width).T


def turn_kernel(grid, masks, *refs):
    refs[-2][...] = sort_and_turn(grid, masks, refs[:-2], refs[-1])


def turn(grid, parts, masks):
    arrays = [parts[mask, near, 0] for mask in masks for near in range(2)]
    blocks, far, cores, count, width = arrays[0].shape
    features = len(masks) * width
    return pl.pallas_call(
        functools.partial(turn_kernel, grid, masks),
        out_shape=pltpu.VMEM((features, blocks * far * 2 * cores * count), jnp.bfloat16),
        in_specs=[VMEM] * len(arrays),
        out_specs=VMEM,
        scratch_shapes=[pltpu.VMEM((blocks, far, 2, cores, count, features), jnp.bfloat16)],
        compiler_params=pltpu.CompilerParams(vmem_limit_bytes=8 << 20),
        name="turn",
    )(*(pltpu.with_memory_space_constraint(a, pltpu.VMEM) for a in arrays))


def score_kernel(grid, masks, other, part_count, first, last, *refs):
    train_ref, part_refs, refs = refs[0], refs[1 : 1 + part_count], refs[1 + part_count :]
    total_ref, refs = (None, refs) if first else (refs[0], refs[1:])
    out_ref, refs = refs[0], refs[1:]
    far, _, core = grid.place()
    features = train_ref.shape[1]
    width = features // (grid.far * 4)
    if part_count == 1:
        turned = part_refs[0][...]
    else:
        turned = sort_and_turn(grid, masks, part_refs, refs[0])
        refs = refs[1:]
    pieces = [
        columns((flip(far, mask) * 2 + side) * 2 + flip(core, other), width) for mask in masks for side in range(2)
    ]

    def products(rows, turned):
        train = jnp.concatenate([train_ref[rows, piece] for piece in pieces], axis=1)
        return jnp.dot(train, turned, preferred_element_type=jnp.float32)

    if not last:
        value = products(slice(None), turned)
        out_ref[...] = value if first else total_ref[...] + value
        return

    turned_ref, here_ref, sem = refs
    turned_ref[...] = turned
    scale = 1.0 / features**0.5
    row_step, query_step = here_ref.shape[0] // 2, here_ref.shape[1] // 2
    copies = []
    for step in range(4):
        queries = pl.ds(step % 2 * query_step, query_step)
        rows = pl.ds(step // 2 * row_step, row_step)
        here_ref[rows, queries] = (total_ref[rows, queries] + products(rows, turned_ref[:, queries])) * scale
        copies.append(pltpu.make_async_copy(here_ref.at[rows, queries], out_ref.at[rows, queries], sem.at[step]))
        copies[-1].start()
    for copy in copies:
        copy.wait()


def score(grid, train_feats, parts, total, masks, other, last):
    rows = train_feats.shape[0]
    first = total is None
    arrays = [train_feats, *parts] + ([] if first else [total])
    if len(parts) == 1:
        features, queries = parts[0].shape
        scratch = []
    else:
        blocks, far, cores, count, width = parts[0].shape
        features, queries = len(masks) * width, blocks * far * 2 * cores * count
        scratch = [pltpu.VMEM((blocks, far, 2, cores, count, features), jnp.bfloat16)]
    shape = (rows, queries)
    if last:
        scratch += [
            pltpu.VMEM((features, queries), jnp.bfloat16),
            pltpu.VMEM(shape, jnp.float32),
            pltpu.SemaphoreType.DMA((4,)),
        ]
    return pl.pallas_call(
        functools.partial(score_kernel, grid, masks, other, len(parts), first, last),
        out_shape=jax.ShapeDtypeStruct(shape, jnp.float32) if last else pltpu.VMEM(shape, jnp.float32),
        in_specs=[VMEM] * len(arrays),
        out_specs=ANY if last else VMEM,
        scratch_shapes=scratch,
        input_output_aliases={} if first or last else {len(arrays) - 1: 0},
        compiler_params=pltpu.CompilerParams(vmem_limit_bytes=24 << 20),
        cost_estimate=pl.CostEstimate(
            flops=(40 if first else 2) * rows * features * queries, bytes_accessed=4 << 20, transcendentals=0
        ),
        name="score",
    )(*(pltpu.with_memory_space_constraint(a, pltpu.VMEM) for a in arrays))


def two_level(grid, train_feats, queries, inverse_fisher):
    beside, mirror, relayed = 1, 3, 2
    gathered = {(0, 0): queries}
    gathered[0, 1] = grid.swap(queries, 0, 0, 1)
    gathered[beside, 0] = grid.swap(queries, beside, 0, 0)
    near_fisher = grid.swap(inverse_fisher, 0, 1, 0)
    gathered[mirror, 0] = grid.swap(queries, mirror, 0, 0)
    staged = stage([train_feats, queries, inverse_fisher])
    gathered[mirror, 0], gathered[0, 1], staged = lax.optimization_barrier(
        (gathered[mirror, 0], gathered[0, 1], staged)
    )
    train_here, gathered[0, 0], fisher_here = staged
    gathered[relayed, 0] = grid.swap(gathered[mirror, 0], beside, 0, 0)
    (train_here,) = stage([train_feats], train_here)
    for mask in (beside, mirror):
        gathered[mask, 1] = grid.swap(gathered[mask, 0], 0, 0, 1)
    gathered[relayed, 0], train_here = lax.optimization_barrier((gathered[relayed, 0], train_here))
    gathered[relayed, 1] = grid.swap(gathered[relayed, 0], 0, 0, 1)

    parts = {(0, 0, 0): condition(grid, gathered, fisher_here, near_fisher)}

    def swap(source, *step):
        place = tuple(a ^ b for a, b in zip(source, step))
        parts[place] = grid.swap(parts[source], *step)

    def meet(*places, total=None):
        held, total = lax.optimization_barrier(([parts[place] for place in places], total))
        parts.update(zip(places, held))
        return total

    own, near_one, far_one, far_three = (0, 0, 0), (0, 1, 0), (beside, 0, 0), (mirror, 0, 0)
    swap(own, *far_three)
    swap(own, *near_one)
    swap(own, *far_one)
    meet(far_three, far_one)
    swap(far_one, *near_one)
    swap(far_three, *near_one)
    swap(far_three, beside, 1, 0)
    swap(far_three, *far_one)
    turned = turn(grid, parts, (0, beside))
    other = grid.swap(turned, 0, 0, 1)
    total = score(grid, train_here, [turned], None, (0, beside), 0, False)
    total = meet(far_three, total=total)
    swap(far_three, 0, 0, 1)
    total = score(grid, train_here, [other], total, (0, beside), 1, False)
    total = meet(far_three, (relayed, 0, 0), (mirror, 1, 0), (relayed, 1, 0), total=total)
    swap((relayed, 0, 0), 0, 0, 1)
    swap((mirror, 1, 0), 0, 0, 1)
    swap((relayed, 1, 0), 0, 0, 1)
    for core in range(2):
        late = [parts[mask, near, core] for mask in (mirror, relayed) for near in range(2)]
        total = score(grid, train_here, late, total, (mirror, relayed), core, core == 1)
    return total


def one_level(train_feats, queries, inverse_fisher):
    group_count, group_width, _ = inverse_fisher.shape
    gathered = lax.all_gather(queries, "rows", axis=1, tiled=True)
    flattened = gathered.reshape(-1, group_count, group_width)
    part = jnp.einsum("qgk,gkc->qgc", flattened, inverse_fisher, preferred_element_type=jnp.float32)
    complete = lax.all_gather(part.astype(jnp.bfloat16), "rows", axis=2, tiled=True)
    conditioned = complete.reshape(flattened.shape[0], -1)
    products = lax.dot_general(
        train_feats, conditioned, (((1,), (1,)), ((), ())), preferred_element_type=jnp.float32
    )
    return products * (1.0 / train_feats.shape[1] ** 0.5)


def per_device(row_count, train_feats, queries, inverse_fisher):
    group_count, _, width = inverse_fisher.shape
    whole_tiles = group_count == 1 and width % 128 == 0 and queries.shape[1] % 16 == 0
    if row_count == 16 and whole_tiles and train_feats.shape[0] % 512 == 0:
        return two_level(Grid(row_count), train_feats, queries, inverse_fisher)
    return one_level(train_feats, queries, inverse_fisher)


def solution(mesh):
    placed = (P(("groups", "rows"), None), P(None, ("groups", "rows"), None), P(None, None, "rows"))
    return jax.shard_map(
        functools.partial(per_device, mesh.shape["rows"]),
        mesh=mesh,
        in_specs=placed,
        out_specs=P(("groups", "rows"), None),
        check_vma=False,
    )
```

```python
import functools

import jax
import jax.numpy as jnp
from jax import lax
from jax.experimental import pallas as pl
from jax.experimental.pallas import tpu as pltpu
from jax.sharding import PartitionSpec as P

VMEM = pl.BlockSpec(memory_space=pltpu.VMEM)
ANY = pl.BlockSpec(memory_space=pl.ANY)
ORDER_FLOPS = 2_789_900_000


class Grid:
    def __init__(self, row_count):
        self.far = row_count // 4

    def swap(self, block, far, near, core):
        step = (far * 2 + near) * 2 + core
        return lax.ppermute(block, "rows", [(row ^ step, row) for row in range(self.far * 4)])

    def place(self):
        row = lax.axis_index("rows")
        return lax.div(row, 4), lax.rem(lax.div(row, 2), 2), lax.rem(row, 2)


def flip(part, mask):
    return lax.bitwise_xor(part, jnp.int32(mask))


def columns(index, width):
    return pl.ds(pl.multiple_of(index * width, width), width)


def stage_kernel(pieces, *refs):
    sources, targets, sems = refs[: len(pieces)], refs[len(pieces) : -1], refs[-1]
    copies = []
    for source, target, count in zip(sources, targets, pieces):
        step = source.shape[0] // count
        for piece in range(count):
            part = pl.ds(piece * step, step)
            copies.append(pltpu.make_async_copy(source.at[part], target.at[part], sems.at[len(copies)]))
    for copy in copies:
        copy.start()
    for copy in copies:
        copy.wait()


def stage(pieces, *arrays):
    size = sum(a.size * a.dtype.itemsize for a in arrays)
    return pl.pallas_call(
        functools.partial(stage_kernel, pieces),
        out_shape=[pltpu.VMEM(a.shape, a.dtype) for a in arrays],
        in_specs=[ANY] * len(arrays),
        out_specs=[VMEM] * len(arrays),
        scratch_shapes=[pltpu.SemaphoreType.DMA((sum(pieces),))],
        compiler_params=pltpu.CompilerParams(vmem_limit_bytes=4 << 20),
        cost_estimate=pl.CostEstimate(flops=ORDER_FLOPS, bytes_accessed=2 * size, transcendentals=0),
        name="stage",
    )(*(pltpu.with_memory_space_constraint(a, pltpu.HBM) for a in arrays))


def condition_kernel(grid, places, *refs):
    query_refs, (own_ref, near_ref, out_ref) = refs[: len(places)], refs[len(places) :]
    far, near, core = grid.place()
    rows = jnp.concatenate([ref[...].reshape(-1, ref.shape[-1]) for ref in query_refs])
    fisher = jnp.concatenate([own_ref[0], near_ref[0]], axis=1)
    result = jnp.dot(rows, fisher, preferred_element_type=jnp.float32).astype(out_ref.dtype)
    blocks, count, _ = query_refs[0].shape
    width = own_ref.shape[-1]
    result = result.reshape(len(places), blocks, 1, 1, count, 2 * width)
    for index, (far_mask, core_mask) in enumerate(places):
        for side in range(2):
            out_ref[
                :, pl.ds(flip(far, far_mask), 1), pl.ds(flip(core, core_mask), 1), :, columns(flip(near, side), width)
            ] = result[index, ..., side * width : (side + 1) * width]


def condition(grid, queries, own, near):
    blocks, count, _ = queries[0, 0].shape
    width = own.shape[-1]
    arrays = [*queries.values(), own, near]
    return pl.pallas_call(
        functools.partial(condition_kernel, grid, list(queries)),
        out_shape=jax.ShapeDtypeStruct((blocks, grid.far, 2, count, 2 * width), jnp.bfloat16),
        in_specs=[VMEM] * len(arrays),
        out_specs=VMEM,
        compiler_params=pltpu.CompilerParams(vmem_limit_bytes=12 << 20),
        cost_estimate=pl.CostEstimate(flops=1 << 28, bytes_accessed=3 << 20, transcendentals=0),
        name="condition",
    )(*arrays)


def sort_and_turn(grid, masks, part_refs, sorted_ref):
    _, near, _ = grid.place()
    width = part_refs[0].shape[-1]
    for index in range(len(masks)):
        for side in range(2):
            sorted_ref[:, :, pl.ds(flip(near, side), 1), :, :, index * width : (index + 1) * width] = part_refs[
                index * 2 + side
            ][...][:, :, None]
    return sorted_ref[...].reshape(-1, len(masks) * width).T


def turn_kernel(grid, masks, *refs):
    refs[-2][...] = sort_and_turn(grid, masks, refs[:-2], refs[-1])


def turn(grid, parts, masks):
    arrays = [parts[mask, near, 0] for mask in masks for near in range(2)]
    blocks, far, cores, count, width = arrays[0].shape
    features = len(masks) * width
    return pl.pallas_call(
        functools.partial(turn_kernel, grid, masks),
        out_shape=pltpu.VMEM((features, blocks * far * 2 * cores * count), jnp.bfloat16),
        in_specs=[VMEM] * len(arrays),
        out_specs=VMEM,
        scratch_shapes=[pltpu.VMEM((blocks, far, 2, cores, count, features), jnp.bfloat16)],
        compiler_params=pltpu.CompilerParams(vmem_limit_bytes=8 << 20),
        name="turn",
    )(*(pltpu.with_memory_space_constraint(a, pltpu.VMEM) for a in arrays))


def score_kernel(grid, masks, other, part_count, first, last, *refs):
    train_ref, part_refs, refs = refs[0], refs[1 : 1 + part_count], refs[1 + part_count :]
    total_ref, refs = (None, refs) if first else (refs[0], refs[1:])
    out_ref, refs = refs[0], refs[1:]
    far, _, core = grid.place()
    features = train_ref.shape[1]
    width = features // (grid.far * 4)
    if part_count == 1:
        turned = part_refs[0][...]
    else:
        turned = sort_and_turn(grid, masks, part_refs, refs[0])
        refs = refs[1:]
    pieces = [
        columns((flip(far, mask) * 2 + side) * 2 + flip(core, other), width) for mask in masks for side in range(2)
    ]

    def products(rows, turned):
        train = jnp.concatenate([train_ref[rows, piece] for piece in pieces], axis=1)
        return jnp.dot(train, turned, preferred_element_type=jnp.float32)

    if not last:
        value = products(slice(None), turned)
        out_ref[...] = value if first else total_ref[...] + value
        return

    turned_ref, here_ref, sem = refs
    turned_ref[...] = turned
    scale = 1.0 / features**0.5
    row_step, query_step = here_ref.shape[0] // 2, here_ref.shape[1] // 2
    copies = []
    for step in range(4):
        queries = pl.ds(step % 2 * query_step, query_step)
        rows = pl.ds(step // 2 * row_step, row_step)
        here_ref[rows, queries] = (total_ref[rows, queries] + products(rows, turned_ref[:, queries])) * scale
        copies.append(pltpu.make_async_copy(here_ref.at[rows, queries], out_ref.at[rows, queries], sem.at[step]))
        copies[-1].start()
    for copy in copies:
        copy.wait()


def score(grid, train_feats, parts, total, masks, other, last):
    rows = train_feats.shape[0]
    first = total is None
    arrays = [train_feats, *parts] + ([] if first else [total])
    if len(parts) == 1:
        features, queries = parts[0].shape
        scratch = []
    else:
        blocks, far, cores, count, width = parts[0].shape
        features, queries = len(masks) * width, blocks * far * 2 * cores * count
        scratch = [pltpu.VMEM((blocks, far, 2, cores, count, features), jnp.bfloat16)]
    shape = (rows, queries)
    if last:
        scratch += [
            pltpu.VMEM((features, queries), jnp.bfloat16),
            pltpu.VMEM(shape, jnp.float32),
            pltpu.SemaphoreType.DMA((4,)),
        ]
    return pl.pallas_call(
        functools.partial(score_kernel, grid, masks, other, len(parts), first, last),
        out_shape=jax.ShapeDtypeStruct(shape, jnp.float32) if last else pltpu.VMEM(shape, jnp.float32),
        in_specs=[VMEM] * len(arrays),
        out_specs=ANY if last else VMEM,
        scratch_shapes=scratch,
        input_output_aliases={} if first or last else {len(arrays) - 1: 0},
        compiler_params=pltpu.CompilerParams(vmem_limit_bytes=24 << 20),
        cost_estimate=pl.CostEstimate(
            flops=(40 if first else 2) * rows * features * queries, bytes_accessed=4 << 20, transcendentals=0
        ),
        name="score",
    )(*(pltpu.with_memory_space_constraint(a, pltpu.VMEM) for a in arrays))


def two_level(grid, train_feats, queries, inverse_fisher):
    beside, mirror, relayed = 1, 3, 2
    gathered = {(0, 0): queries}
    gathered[0, 1] = grid.swap(queries, 0, 0, 1)
    gathered[beside, 0] = grid.swap(queries, beside, 0, 0)
    near_fisher = grid.swap(inverse_fisher, 0, 1, 0)
    gathered[mirror, 0] = grid.swap(queries, mirror, 0, 0)
    staged = stage((1, 1, 1), train_feats, queries, inverse_fisher)
    gathered[mirror, 0], gathered[0, 1], staged = lax.optimization_barrier(
        (gathered[mirror, 0], gathered[0, 1], staged)
    )
    train_here, gathered[0, 0], fisher_here = staged
    gathered[relayed, 0] = grid.swap(gathered[mirror, 0], beside, 0, 0)
    for mask in (beside, mirror, relayed):
        gathered[mask, 1] = grid.swap(gathered[mask, 0], 0, 0, 1)

    parts = {(0, 0, 0): condition(grid, gathered, fisher_here, near_fisher)}

    def swap(source, *step):
        place = tuple(a ^ b for a, b in zip(source, step))
        parts[place] = grid.swap(parts[source], *step)

    def meet(*places, total=None):
        held, total = lax.optimization_barrier(([parts[place] for place in places], total))
        parts.update(zip(places, held))
        return total

    own, near_one, far_one, far_three = (0, 0, 0), (0, 1, 0), (beside, 0, 0), (mirror, 0, 0)
    swap(own, *far_three)
    swap(own, *near_one)
    swap(own, *far_one)
    swap(far_one, *near_one)
    swap(far_three, *near_one)
    swap(far_three, beside, 1, 0)
    swap(far_three, *far_one)
    turned = turn(grid, parts, (0, beside))
    other = grid.swap(turned, 0, 0, 1)
    total = score(grid, train_here, [turned], None, (0, beside), 0, False)
    total = meet(far_three, total=total)
    swap(far_three, 0, 0, 1)
    total = score(grid, train_here, [other], total, (0, beside), 1, False)
    total = meet(far_three, (relayed, 0, 0), (mirror, 1, 0), (relayed, 1, 0), total=total)
    swap((relayed, 0, 0), 0, 0, 1)
    swap((mirror, 1, 0), 0, 0, 1)
    swap((relayed, 1, 0), 0, 0, 1)
    for core in range(2):
        late = [parts[mask, near, core] for mask in (mirror, relayed) for near in range(2)]
        total = score(grid, train_here, late, total, (mirror, relayed), core, core == 1)
    return total


def one_level(train_feats, queries, inverse_fisher):
    group_count, group_width, _ = inverse_fisher.shape
    gathered = lax.all_gather(queries, "rows", axis=1, tiled=True)
    flattened = gathered.reshape(-1, group_count, group_width)
    part = jnp.einsum("qgk,gkc->qgc", flattened, inverse_fisher, preferred_element_type=jnp.float32)
    complete = lax.all_gather(part.astype(jnp.bfloat16), "rows", axis=2, tiled=True)
    conditioned = complete.reshape(flattened.shape[0], -1)
    products = lax.dot_general(
        train_feats, conditioned, (((1,), (1,)), ((), ())), preferred_element_type=jnp.float32
    )
    return products * (1.0 / train_feats.shape[1] ** 0.5)


def per_device(row_count, train_feats, queries, inverse_fisher):
    group_count, _, width = inverse_fisher.shape
    whole_tiles = group_count == 1 and width % 128 == 0 and queries.shape[1] % 16 == 0
    if row_count == 16 and whole_tiles and train_feats.shape[0] % 512 == 0:
        return two_level(Grid(row_count), train_feats, queries, inverse_fisher)
    return one_level(train_feats, queries, inverse_fisher)


def solution(mesh):
    placed = (P(("groups", "rows"), None), P(None, ("groups", "rows"), None), P(None, None, "rows"))
    return jax.shard_map(
        functools.partial(per_device, mesh.shape["rows"]),
        mesh=mesh,
        in_specs=placed,
        out_specs=P(("groups", "rows"), None),
        check_vma=False,
    )
```

```python
import functools

import jax
import jax.numpy as jnp
from jax import lax
from jax.experimental import pallas as pl
from jax.experimental.pallas import tpu as pltpu
from jax.sharding import PartitionSpec as P

VMEM = pl.BlockSpec(memory_space=pltpu.VMEM)
ANY = pl.BlockSpec(memory_space=pl.ANY)
ORDER_FLOPS = 2_788_000_000


class Grid:
    def __init__(self, row_count):
        self.far = row_count // 4

    def swap(self, block, far, near, core):
        step = (far * 2 + near) * 2 + core
        return lax.ppermute(block, "rows", [(row ^ step, row) for row in range(self.far * 4)])

    def place(self):
        row = lax.axis_index("rows")
        return lax.div(row, 4), lax.rem(lax.div(row, 2), 2), lax.rem(row, 2)


def flip(part, mask):
    return lax.bitwise_xor(part, jnp.int32(mask))


def columns(index, width):
    return pl.ds(pl.multiple_of(index * width, width), width)


def stage_kernel(first, half, *refs):
    sources, targets, sems = refs[: len(refs) // 2], refs[len(refs) // 2 : -1], refs[-1]
    if not first:
        sources = sources[1:]
    part = pl.ds(0 if first else half, half)
    copies = [pltpu.make_async_copy(sources[0].at[part], targets[0].at[part], sems.at[0])]
    for index in range(1, len(sources)):
        copies.append(pltpu.make_async_copy(sources[index], targets[index], sems.at[index]))
    for copy in copies:
        copy.start()
    for copy in copies:
        copy.wait()


def stage(arrays, buffer=None):
    first = buffer is None
    moved = sum(a.size * a.dtype.itemsize for a in arrays)
    sources = [pltpu.with_memory_space_constraint(a, pltpu.HBM) for a in arrays]
    if not first:
        sources.insert(0, pltpu.with_memory_space_constraint(buffer, pltpu.VMEM))
    return pl.pallas_call(
        functools.partial(stage_kernel, first, arrays[0].shape[0] // 2),
        out_shape=[pltpu.VMEM(a.shape, a.dtype) for a in arrays],
        in_specs=[ANY] * len(arrays) if first else [VMEM, ANY],
        out_specs=[VMEM] * len(arrays),
        scratch_shapes=[pltpu.SemaphoreType.DMA((len(arrays),))],
        input_output_aliases={} if first else {0: 0},
        compiler_params=pltpu.CompilerParams(vmem_limit_bytes=4 << 20),
        cost_estimate=pl.CostEstimate(
            flops=ORDER_FLOPS if first else 1, bytes_accessed=moved, transcendentals=0
        ),
        name="stage",
    )(*sources)


def condition_kernel(grid, places, *refs):
    query_refs, (own_ref, near_ref, out_ref) = refs[: len(places)], refs[len(places) :]
    far, near, core = grid.place()
    rows = jnp.concatenate([ref[...].reshape(-1, ref.shape[-1]) for ref in query_refs])
    fisher = jnp.concatenate([own_ref[0], near_ref[0]], axis=1)
    result = jnp.dot(rows, fisher, preferred_element_type=jnp.float32).astype(out_ref.dtype)
    blocks, count, _ = query_refs[0].shape
    width = own_ref.shape[-1]
    result = result.reshape(len(places), blocks, 1, 1, count, 2 * width)
    for index, (far_mask, core_mask) in enumerate(places):
        for side in range(2):
            out_ref[
                :, pl.ds(flip(far, far_mask), 1), pl.ds(flip(core, core_mask), 1), :, columns(flip(near, side), width)
            ] = result[index, ..., side * width : (side + 1) * width]


def condition(grid, queries, own, near):
    blocks, count, _ = queries[0, 0].shape
    width = own.shape[-1]
    arrays = [*queries.values(), own, near]
    return pl.pallas_call(
        functools.partial(condition_kernel, grid, list(queries)),
        out_shape=jax.ShapeDtypeStruct((blocks, grid.far, 2, count, 2 * width), jnp.bfloat16),
        in_specs=[VMEM] * len(arrays),
        out_specs=VMEM,
        compiler_params=pltpu.CompilerParams(vmem_limit_bytes=12 << 20),
        cost_estimate=pl.CostEstimate(flops=1 << 28, bytes_accessed=3 << 20, transcendentals=0),
        name="condition",
    )(*arrays)


def sort_and_turn(grid, masks, part_refs, sorted_ref):
    _, near, _ = grid.place()
    width = part_refs[0].shape[-1]
    for index in range(len(masks)):
        for side in range(2):
            sorted_ref[:, :, pl.ds(flip(near, side), 1), :, :, index * width : (index + 1) * width] = part_refs[
                index * 2 + side
            ][...][:, :, None]
    return sorted_ref[...].reshape(-1, len(masks) * width).T


def turn_kernel(grid, masks, *refs):
    refs[-2][...] = sort_and_turn(grid, masks, refs[:-2], refs[-1])


def turn(grid, parts, masks):
    arrays = [parts[mask, near, 0] for mask in masks for near in range(2)]
    blocks, far, cores, count, width = arrays[0].shape
    features = len(masks) * width
    return pl.pallas_call(
        functools.partial(turn_kernel, grid, masks),
        out_shape=pltpu.VMEM((features, blocks * far * 2 * cores * count), jnp.bfloat16),
        in_specs=[VMEM] * len(arrays),
        out_specs=VMEM,
        scratch_shapes=[pltpu.VMEM((blocks, far, 2, cores, count, features), jnp.bfloat16)],
        compiler_params=pltpu.CompilerParams(vmem_limit_bytes=8 << 20),
        name="turn",
    )(*(pltpu.with_memory_space_constraint(a, pltpu.VMEM) for a in arrays))


def score_kernel(grid, masks, other, part_count, first, last, *refs):
    train_ref, part_refs, refs = refs[0], refs[1 : 1 + part_count], refs[1 + part_count :]
    total_ref, refs = (None, refs) if first else (refs[0], refs[1:])
    out_ref, refs = refs[0], refs[1:]
    far, _, core = grid.place()
    features = train_ref.shape[1]
    width = features // (grid.far * 4)
    if part_count == 1:
        turned = part_refs[0][...]
    else:
        turned = sort_and_turn(grid, masks, part_refs, refs[0])
        refs = refs[1:]
    pieces = [
        columns((flip(far, mask) * 2 + side) * 2 + flip(core, other), width) for mask in masks for side in range(2)
    ]

    def products(rows, turned):
        train = jnp.concatenate([train_ref[rows, piece] for piece in pieces], axis=1)
        return jnp.dot(train, turned, preferred_element_type=jnp.float32)

    if not last:
        value = products(slice(None), turned)
        out_ref[...] = value if first else total_ref[...] + value
        return

    turned_ref, here_ref, sem = refs
    turned_ref[...] = turned
    scale = 1.0 / features**0.5
    row_step, query_step = here_ref.shape[0] // 2, here_ref.shape[1] // 2
    copies = []
    for step in range(4):
        queries = pl.ds(step % 2 * query_step, query_step)
        rows = pl.ds(step // 2 * row_step, row_step)
        here_ref[rows, queries] = (total_ref[rows, queries] + products(rows, turned_ref[:, queries])) * scale
        copies.append(pltpu.make_async_copy(here_ref.at[rows, queries], out_ref.at[rows, queries], sem.at[step]))
        copies[-1].start()
    for copy in copies:
        copy.wait()


def score(grid, train_feats, parts, total, masks, other, last):
    rows = train_feats.shape[0]
    first = total is None
    arrays = [train_feats, *parts] + ([] if first else [total])
    if len(parts) == 1:
        features, queries = parts[0].shape
        scratch = []
    else:
        blocks, far, cores, count, width = parts[0].shape
        features, queries = len(masks) * width, blocks * far * 2 * cores * count
        scratch = [pltpu.VMEM((blocks, far, 2, cores, count, features), jnp.bfloat16)]
    shape = (rows, queries)
    if last:
        scratch += [
            pltpu.VMEM((features, queries), jnp.bfloat16),
            pltpu.VMEM(shape, jnp.float32),
            pltpu.SemaphoreType.DMA((4,)),
        ]
    return pl.pallas_call(
        functools.partial(score_kernel, grid, masks, other, len(parts), first, last),
        out_shape=jax.ShapeDtypeStruct(shape, jnp.float32) if last else pltpu.VMEM(shape, jnp.float32),
        in_specs=[VMEM] * len(arrays),
        out_specs=ANY if last else VMEM,
        scratch_shapes=scratch,
        input_output_aliases={} if first or last else {len(arrays) - 1: 0},
        compiler_params=pltpu.CompilerParams(vmem_limit_bytes=24 << 20),
        cost_estimate=pl.CostEstimate(
            flops=(40 if first else 2) * rows * features * queries, bytes_accessed=4 << 20, transcendentals=0
        ),
        name="score",
    )(*(pltpu.with_memory_space_constraint(a, pltpu.VMEM) for a in arrays))


def two_level(grid, train_feats, queries, inverse_fisher):
    beside, mirror, relayed = 1, 3, 2
    gathered = {(0, 0): queries}
    gathered[0, 1] = grid.swap(queries, 0, 0, 1)
    gathered[beside, 0] = grid.swap(queries, beside, 0, 0)
    near_fisher = grid.swap(inverse_fisher, 0, 1, 0)
    gathered[mirror, 0] = grid.swap(queries, mirror, 0, 0)
    staged = stage([train_feats, queries, inverse_fisher])
    gathered[mirror, 0], gathered[0, 1], staged = lax.optimization_barrier(
        (gathered[mirror, 0], gathered[0, 1], staged)
    )
    train_here, gathered[0, 0], fisher_here = staged
    gathered[relayed, 0] = grid.swap(gathered[mirror, 0], beside, 0, 0)
    (train_here,) = stage([train_feats], train_here)
    held, train_here = lax.optimization_barrier((gathered[mirror, 0], train_here))
    gathered[mirror, 1] = grid.swap(held, 0, 0, 1)
    gathered[beside, 1] = grid.swap(gathered[beside, 0], 0, 0, 1)
    gathered[relayed, 0], train_here = lax.optimization_barrier((gathered[relayed, 0], train_here))
    gathered[relayed, 1] = grid.swap(gathered[relayed, 0], 0, 0, 1)

    parts = {(0, 0, 0): condition(grid, gathered, fisher_here, near_fisher)}

    def swap(source, *step):
        place = tuple(a ^ b for a, b in zip(source, step))
        parts[place] = grid.swap(parts[source], *step)

    def meet(*places, total=None):
        held, total = lax.optimization_barrier(([parts[place] for place in places], total))
        parts.update(zip(places, held))
        return total

    own, near_one, far_one, far_three = (0, 0, 0), (0, 1, 0), (beside, 0, 0), (mirror, 0, 0)
    swap(own, *far_three)
    swap(own, *near_one)
    swap(own, *far_one)
    swap(far_one, *near_one)
    swap(far_three, *near_one)
    swap(far_three, beside, 1, 0)
    swap(far_three, *far_one)
    turned = turn(grid, parts, (0, beside))
    other = grid.swap(turned, 0, 0, 1)
    total = score(grid, train_here, [turned], None, (0, beside), 0, False)
    total = meet(far_three, total=total)
    swap(far_three, 0, 0, 1)
    total = score(grid, train_here, [other], total, (0, beside), 1, False)
    total = meet(far_three, (relayed, 0, 0), (mirror, 1, 0), (relayed, 1, 0), total=total)
    swap((relayed, 0, 0), 0, 0, 1)
    swap((mirror, 1, 0), 0, 0, 1)
    swap((relayed, 1, 0), 0, 0, 1)
    for core in range(2):
        late = [parts[mask, near, core] for mask in (mirror, relayed) for near in range(2)]
        total = score(grid, train_here, late, total, (mirror, relayed), core, core == 1)
    return total


def one_level(train_feats, queries, inverse_fisher):
    group_count, group_width, _ = inverse_fisher.shape
    gathered = lax.all_gather(queries, "rows", axis=1, tiled=True)
    flattened = gathered.reshape(-1, group_count, group_width)
    part = jnp.einsum("qgk,gkc->qgc", flattened, inverse_fisher, preferred_element_type=jnp.float32)
    complete = lax.all_gather(part.astype(jnp.bfloat16), "rows", axis=2, tiled=True)
    conditioned = complete.reshape(flattened.shape[0], -1)
    products = lax.dot_general(
        train_feats, conditioned, (((1,), (1,)), ((), ())), preferred_element_type=jnp.float32
    )
    return products * (1.0 / train_feats.shape[1] ** 0.5)


def per_device(row_count, train_feats, queries, inverse_fisher):
    group_count, _, width = inverse_fisher.shape
    whole_tiles = group_count == 1 and width % 128 == 0 and queries.shape[1] % 16 == 0
    if row_count == 16 and whole_tiles and train_feats.shape[0] % 512 == 0:
        return two_level(Grid(row_count), train_feats, queries, inverse_fisher)
    return one_level(train_feats, queries, inverse_fisher)


def solution(mesh):
    placed = (P(("groups", "rows"), None), P(None, ("groups", "rows"), None), P(None, None, "rows"))
    return jax.shard_map(
        functools.partial(per_device, mesh.shape["rows"]),
        mesh=mesh,
        in_specs=placed,
        out_specs=P(("groups", "rows"), None),
        check_vma=False,
    )
```
